32 devices in a mesh: batch: 16 (over z, x, core), tensor: 2 (over y).
Axes of the slice: x: 2, y: 2, z: 4, core: 2. Of those that a mesh axis runs over, the one named last changes fastest.
Arguments:
- tokens: float32 [4096, 768], P('batch'), may hold values from -6 to 6
- images: bfloat16 [32, 576, 768], P('batch'), may hold values from -6 to 6
- caption_image: int32 [64], P('batch'), may hold values from 0 to 31, as said below
- self_qkv: float32 [3, 768, 768], P(None, None, 'tensor'), may hold values from -0.21875 to 0.21875
- self_out: float32 [768, 768], P('tensor'), may hold values from -0.625 to 0.625
- cross_q: float32 [768, 768], P(None, 'tensor'), may hold values from -0.21875 to 0.21875
- cross_kv: float32 [2, 768, 768], P(None, None, 'tensor'), may hold values from -0.21875 to 0.21875
- cross_out: float32 [768, 768], P('tensor'), may hold values from -1.25 to 1.25
- mlp_in: float32 [768, 3072], P(None, 'tensor'), may hold values from -0.21875 to 0.21875
- mlp_out: float32 [3072, 768], P('tensor'), may hold values from -0.109375 to 0.109375
- ln_gains: float32 [3, 768], replicated, may hold values from 0.5 to 1.5
- ln_biases: float32 [3, 768], replicated, may hold values from -2 to 2
- cotangent: float32 [4096, 768], P('batch'), may hold values from -6 to 6
Outputs:
- mixed: float32 [4096, 768], P('batch')
- grad_tokens: float32 [4096, 768], P('batch')
- grad_images: float32 [32, 576, 768], P('batch')
- grad_self_qkv: float32 [3, 768, 768], P(None, 'batch', 'tensor')
- grad_self_out: float32 [768, 768], P('tensor', 'batch')
- grad_cross_q: float32 [768, 768], P('batch', 'tensor')
- grad_cross_kv: float32 [2, 768, 768], P(None, 'batch', 'tensor')
- grad_cross_out: float32 [768, 768], P('tensor', 'batch')
- grad_mlp_in: float32 [768, 3072], P('batch', 'tensor')
- grad_mlp_out: float32 [3072, 768], P('tensor', 'batch')
- grad_gains: float32 [3, 768], P(None, 'batch')
- grad_biases: float32 [3, 768], P(None, 'batch')
The draws below stay inside these ranges and needn't reach their ends.
Inputs may be any that keep to these rules, and one draw needn't show every extreme that they name: `caption_image`: aligned blocks of 4 captions: the captions of block b name the images b * 2 to (b + 1) * 2 - 1, each exactly twice.
All inputs are finite; a program needn't handle non-finite values.
Results may differ from the reference program's by a relative error of at most 0.02.
The reference program's roundings to bfloat16 on the way count: a program that leaves them out, or rounds other values in their place, can miss the bound.
Values sent between devices are 32-bit elements; how exact they have to be, the bound alone decides.
A program may use at most 128 MiB of HBM per device.

```python
import jax
import jax.numpy as jnp
from jax import lax

D = 768
HEADS = 12
HEAD_DIM = 64
FF = 3072
IMG = 576
CAP_LEN = 64
PAIRS_DEV = 2
TOK_DEV = 256
CAPTIONS = 64
IMAGES = 32
TOKENS = 4096
N_BATCH = 16


def draw_caption_image(key, part):
    key = jax.random.fold_in(key, 11)
    block_count = CAPTIONS // (2 * PAIRS_DEV)
    base = jnp.arange(2 * PAIRS_DEV, dtype=jnp.int32) // 2
    block_keys = jax.random.split(key, block_count)
    shuffled = jax.vmap(lambda single: jax.random.permutation(single, base))(block_keys)
    offsets = (jnp.arange(block_count, dtype=jnp.int32) * PAIRS_DEV)[:, None]
    return (shuffled + offsets).reshape(-1).astype(jnp.int32)


def raised(values, rng, source, target, shards_of, factor):
    def block_of(position):
        return (jnp.arange(values.shape[position]) // (values.shape[position] // shards_of)).reshape((-1,) + (1,) * (values.ndim - 1 - position))

    one_side = jax.random.permutation(rng, shards_of)[block_of(target)]
    far = (block_of(target) + shards_of // 2) % shards_of
    return jnp.where((block_of(source) == one_side) | (block_of(source) == far), factor * values, values)


def block_levels(rng, extent, pieces, smallest, high):
    level = 1.0
    for axis_at, parts in pieces:
        draws = jax.random.uniform(jax.random.fold_in(jax.random.fold_in(rng, 6), axis_at), (parts,), jnp.float32, smallest / len(pieces), high / len(pieces))
        level = level * jnp.repeat(jnp.exp(draws), extent[axis_at] // parts).reshape((-1,) + (1,) * (len(extent) - 1 - axis_at))
    return level


def normal_values(rng, extent, width, reach, cuts=(), kind=jnp.bfloat16):
    result = width * jax.random.normal(rng, extent, jnp.float32)
    if cuts:
        result = result * block_levels(rng, extent, cuts, -0.22, 0.18)
    return jnp.clip(result, -reach, reach).astype(kind)


def noise_with(stream_key, shape, deviation, bound, cuts, heavy, held_as=jnp.bfloat16):
    array = deviation * jax.random.normal(stream_key, shape, jnp.float32)
    if cuts:
        array = array * block_levels(stream_key, shape, cuts, -0.22, 0.18)
    return jnp.clip(raised(array, jax.random.fold_in(stream_key, 3), *heavy), -bound, bound).astype(held_as)


def setup_inputs(seed: int = 0) -> dict:
    arg_keys = jax.random.split(jax.random.key(seed), 14)
    tokens = noise_with(arg_keys[0], (TOKENS, D), 1.0, 6.0, ((0, 16),), (0, 1, 16, 2.0), jnp.float32)
    images = normal_values(arg_keys[1], (IMAGES, IMG, D), 1.0, 6.0, ((0, 16),))
    caption_image = draw_caption_image(jax.random.fold_in(arg_keys[13], 71), 0)
    self_qkv = normal_values(arg_keys[3], (3, D, D), D ** -0.5, 0.21875, ((2, 2),), jnp.float32)
    self_out = normal_values(arg_keys[4], (D, D), (D // 8) ** -0.5, 0.625, ((0, 2),), jnp.float32)
    cross_q = normal_values(arg_keys[5], (D, D), D ** -0.5, 0.21875, ((1, 2),), jnp.float32)
    cross_kv = normal_values(arg_keys[6], (2, D, D), D ** -0.5, 0.21875, ((2, 2),), jnp.float32)
    cross_out = normal_values(arg_keys[7], (D, D), (D // 32) ** -0.5, 1.25, ((0, 2),), jnp.float32)
    mlp_in = normal_values(arg_keys[8], (D, FF), D ** -0.5, 0.21875, ((1, 2),), jnp.float32)
    mlp_out = normal_values(arg_keys[9], (FF, D), FF ** -0.5, 0.109375, ((0, 2),), jnp.float32)
    ln_gains = jnp.clip(1.0 + 0.1 * jax.random.normal(arg_keys[10], (3, D), jnp.float32), 0.5, 1.5)
    ln_biases = normal_values(arg_keys[11], (3, D), 0.3, 2.0, (), jnp.float32)
    cotangent = noise_with(arg_keys[12], (TOKENS, D), 1.0, 6.0, ((0, 16),), (0, 1, 16, 2.0), jnp.float32)
    return dict(tokens=tokens, images=images, caption_image=caption_image, self_qkv=self_qkv, self_out=self_out, cross_q=cross_q, cross_kv=cross_kv, cross_out=cross_out, mlp_in=mlp_in, mlp_out=mlp_out, ln_gains=ln_gains, ln_biases=ln_biases, cotangent=cotangent)


EPS = 1e-05
MASKED = -1e+30
HIGH = lax.Precision.HIGHEST

@jax.custom_vjp
def low(v):
    return lax.optimization_barrier(v.astype(jnp.bfloat16)).astype(jnp.float32)

@jax.custom_vjp
def low_back(v):
    return v

def low_keep(v):
    return (low(v), None)

def low_pass(kept, grad):
    return (grad,)

def back_keep(v):
    return (v, None)

def back_low(kept, grad):
    return (low(grad),)
low.defvjp(low_keep, low_pass)
low_back.defvjp(back_keep, back_low)

def both_ways(value):
    return low(low_back(value))

def matmul(left, right):
    return jnp.dot(left, right, precision=HIGH)

def layer_norm(value, gain, bias):
    center = value - lax.optimization_barrier(jnp.mean(value, -1, keepdims=True))
    spread = lax.optimization_barrier(jnp.mean(center * center, -1, keepdims=True))
    return center * lax.rsqrt(spread + EPS) * gain + bias

def softmax_rows(scores):
    top = lax.optimization_barrier(jnp.max(scores, -1, keepdims=True))
    expo = jnp.exp(scores - top)
    return expo / lax.optimization_barrier(jnp.sum(expo, -1, keepdims=True))

def split_heads(value, count):
    return value.reshape(count, -1, HEADS, HEAD_DIM)

def attend(queries, keys, values, mask):
    scores = jnp.einsum('cqhe,ckhe->chqk', queries, keys, precision=HIGH)
    scores = low_back(scores * HEAD_DIM ** (-0.5))
    if mask is not None:
        scores = jnp.where(mask, scores, MASKED)
    weights = low(softmax_rows(scores))
    return jnp.einsum('chqk,ckhe->cqhe', weights, values, precision=HIGH)

def layer_block(masters, gains, biases, tokens, images, local_ids):
    w_qkv, w_self, w_query, w_pair, w_cross, w_inner, w_outer = masters
    captions = local_ids.shape[0]
    rows = tokens.shape[0]
    causal = lax.broadcasted_iota(jnp.int32, (CAP_LEN, CAP_LEN), 0) >= lax.broadcasted_iota(jnp.int32, (CAP_LEN, CAP_LEN), 1)
    normed_one = low(layer_norm(tokens, gains[0], biases[0]))
    projected = both_ways(jnp.einsum('td,sde->ste', normed_one, w_qkv, precision=HIGH))
    mixed_self = attend(split_heads(projected[0], captions), split_heads(projected[1], captions), split_heads(projected[2], captions), causal)
    joined_self = both_ways(mixed_self.reshape(rows, -1))
    after_self = tokens + low_back(matmul(joined_self, w_self))
    normed_two = low(layer_norm(after_self, gains[1], biases[1]))
    cross_queries = both_ways(matmul(normed_two, w_query))
    image_kv = both_ways(jnp.einsum('pnd,sde->spne', images, w_pair, precision=HIGH))
    picked = jnp.take(image_kv, local_ids, axis=1)
    mixed_cross = attend(split_heads(cross_queries, captions), split_heads(picked[0], captions), split_heads(picked[1], captions), None)
    joined_cross = both_ways(mixed_cross.reshape(rows, -1))
    after_cross = after_self + low_back(matmul(joined_cross, w_cross))
    normed_three = low(layer_norm(after_cross, gains[2], biases[2]))
    hidden_pre = low_back(matmul(normed_three, w_inner))
    hidden = low(jax.nn.gelu(hidden_pre))
    return after_cross + low_back(matmul(hidden, w_outer))

def reference(tokens, images, caption_image, self_qkv, self_out, cross_q, cross_kv, cross_out, mlp_in, mlp_out, ln_gains, ln_biases, cotangent):
    group = 1
    for count in range(1, N_BATCH + 1):
        if N_BATCH % count == 0 and count * TOK_DEV <= 4096:
            group = count
    blocks = N_BATCH // group
    block_pairs = group * PAIRS_DEV
    offsets = (jnp.arange(blocks, dtype=jnp.int32) * block_pairs)[:, None]
    local_ids = (caption_image.reshape(blocks, -1).astype(jnp.int32) - offsets).astype(jnp.int32)
    image_float = images.astype(jnp.float32)

    def forward(tokens_in, images_in, masters, gains, biases):
        rounded = tuple((low(weight) for weight in masters))

        def one_block(piece):
            return layer_block(rounded, gains, biases, piece[0], piece[1], piece[2])
        outcome = lax.map(jax.checkpoint(one_block), (tokens_in.reshape(blocks, -1, D), images_in.reshape(blocks, block_pairs, IMG, D), local_ids))
        return outcome.reshape(TOKENS, D)
    masters = (self_qkv, self_out, cross_q, cross_kv, cross_out, mlp_in, mlp_out)
    mixed, pullback = jax.vjp(forward, tokens, image_float, masters, ln_gains, ln_biases)
    grad_tokens, grad_images, grad_masters, grad_gains, grad_biases = pullback(cotangent)
    return (mixed, grad_tokens, grad_images, grad_masters[0], grad_masters[1], grad_masters[2], grad_masters[3], grad_masters[4], grad_masters[5], grad_masters[6], grad_gains, grad_biases)
```

```python
import functools

import jax
import jax.numpy as jnp
from jax import lax
from jax.experimental import pallas as pl
from jax.experimental.pallas import tpu as pltpu
from jax.sharding import PartitionSpec as P

MESH = pl.DeviceIdType.MESH

HEAD_DIM = 64
CAP_LEN = 64


EPS = 1e-05
MASKED = -1e30
NARROW = jnp.bfloat16
WIDE = jnp.float32


def scatter_kernel(chunks, n_in, *refs):
    g_refs, out_refs = refs[:n_in], refs[n_in : n_in + len(chunks)]
    keeps, from_core, from_x, from_z = refs[n_in + len(chunks) : n_in + len(chunks) + 4]
    keep_sem, send1, recv1, send2, recv2, send3, recv3 = refs[n_in + len(chunks) + 4 :]
    b, t = lax.axis_index("batch"), lax.axis_index("tensor")
    core, x, z = b % 2, (b // 2) % 2, b // 4
    core_peer = b + 1 - 2 * core
    x_peer = b + 2 - 4 * x
    z_peers = [((z + d) % 4) * 4 + b % 4 for d in (1, 2, 3)]
    barrier = pltpu.get_barrier_semaphore()
    for peer in (core_peer, x_peer, *z_peers):
        pl.semaphore_signal(barrier, 1, device_id=(peer, t), device_id_type=MESH)
    pl.semaphore_wait(barrier, 5)

    def to_core(i):
        k, col, width = chunks[i]
        return pltpu.make_async_remote_copy(
            g_refs[k].at[:, :, 1 - core, :, pl.ds(col, width)], from_core.at[i, :, :, :, pl.ds(0, width)],
            send1.at[i], recv1.at[i], device_id=(core_peer, t), device_id_type=MESH)

    def own(i):
        k, col, width = chunks[i]
        return pltpu.make_async_copy(
            g_refs[k].at[:, :, core, :, pl.ds(col, width)], keeps.at[i, :, :, :, pl.ds(0, width)], keep_sem.at[i])

    def to_x(i):
        width = chunks[i][2]
        return pltpu.make_async_remote_copy(
            from_core.at[i, :, 1 - x, :, pl.ds(0, width)], from_x.at[i, :, :, pl.ds(0, width)],
            send2.at[i], recv2.at[i], device_id=(x_peer, t), device_id_type=MESH)

    def to_z(i, d):
        width = chunks[i][2]
        return pltpu.make_async_remote_copy(
            from_core.at[i, (z + d) % 4, x, :, pl.ds(0, width)], from_z.at[i, d - 1, :, pl.ds(0, width)],
            send3.at[i, d - 1], recv3.at[i, d - 1], device_id=(z_peers[d - 1], t), device_id_type=MESH)

    n = len(chunks)
    for i in range(n):
        own(i).start()
        to_core(i).start()
    for step in range(n + 2):
        if step < n:
            i, width = step, chunks[step][2]
            own(i).wait()
            to_core(i).wait()
            cols = pl.ds(0, width)
            from_core[i, :, :, :, cols] = from_core[i, :, :, :, cols] + keeps[i, :, :, :, cols]
            to_x(i).start()
        if 0 <= step - 1 < n:
            i = step - 1
            to_x(i).wait()
            cols = pl.ds(0, chunks[i][2])
            from_core[i, :, x, :, cols] = from_core[i, :, x, :, cols] + from_x[i, :, :, cols]
            for d in (1, 2, 3):
                to_z(i, d).start()
        if 0 <= step - 2 < n:
            i = step - 2
            for d in (1, 2, 3):
                to_z(i, d).wait()
            cols = pl.ds(0, chunks[i][2])
            out_refs[i][...] = (from_core[i, z, x, :, cols] + from_z[i, 0, :, cols]) + (from_z[i, 1, :, cols] + from_z[i, 2, :, cols])


def scatter_sums(grads):
    n = 16
    rows = grads[0].shape[0] // n
    chunks = []
    for k, g in enumerate(grads):
        for col in range(0, g.shape[1], 384):
            chunks.append((k, col, min(384, g.shape[1] - col)))
    m = len(chunks)
    outs = pl.pallas_call(
        functools.partial(scatter_kernel, chunks, len(grads)),
        out_shape=[jax.ShapeDtypeStruct((rows, w), WIDE) for _, _, w in chunks],
        in_specs=[pl.BlockSpec(memory_space=pl.ANY)] * len(grads),
        out_specs=[pl.BlockSpec(memory_space=pltpu.VMEM)] * m,
        scratch_shapes=[
            pltpu.VMEM((m, 4, 2, rows, 384), WIDE),
            pltpu.VMEM((m, 4, 2, rows, 384), WIDE),
            pltpu.VMEM((m, 4, rows, 384), WIDE),
            pltpu.VMEM((m, 3, rows, 384), WIDE),
        ]
        + [pltpu.SemaphoreType.DMA((m,))] * 5
        + [pltpu.SemaphoreType.DMA((m, 3))] * 2,
        compiler_params=pltpu.CompilerParams(collective_id=0, has_side_effects=True, vmem_limit_bytes=48 * 2**20),
        name="scatter_sums",
    )(*[g.reshape(4, 2, 2, rows, g.shape[1]) for g in grads])
    sums, at = [], 0
    for g in grads:
        k = -(-g.shape[1] // 384)
        sums.append(outs[at : at + k])
        at += k
    return sums


def tensor_sum(value):
    return value + lax.ppermute(value, "tensor", [(0, 1), (1, 0)])


def layer_norm(value, gain, bias):
    center = value - jnp.mean(value, -1, keepdims=True)
    spread = jnp.mean(center * center, -1, keepdims=True)
    return center * lax.rsqrt(spread + EPS) * gain + bias


def matmul(left, right):
    return jnp.dot(left, right, preferred_element_type=WIDE)


def left_product(left, right):
    return lax.dot_general(left, right, (((0,), (0,)), ((), ())), preferred_element_type=WIDE)


def right_product(left, right):
    return lax.dot_general(left, right, (((1,), (1,)), ((), ())), preferred_element_type=WIDE)


def split_heads(value, count, heads):
    return value.reshape(count, -1, heads, HEAD_DIM)


def masked_scores(queries, keys, mask, scale):
    scores = jnp.einsum("cqhe,ckhe->chqk", queries, keys, preferred_element_type=WIDE) * scale
    if mask is not None:
        scores = jnp.where(mask, scores, MASKED)
    return scores


def attend(queries, keys, values, mask, scale):
    scores = masked_scores(queries, keys, mask, scale)
    top = jnp.max(scores, -1, keepdims=True)
    expo = jnp.exp(scores - top)
    total = jnp.sum(expo, -1, keepdims=True)
    weights = (expo / total).astype(NARROW)
    outcome = jnp.einsum("chqk,ckhe->cqhe", weights, values, preferred_element_type=WIDE)
    return (outcome, top + jnp.log(total))


def attend_back(queries, keys, values, mask, scale, logsum, grad_out):
    scores = masked_scores(queries, keys, mask, scale)
    weights = jnp.exp(scores - logsum)
    grad_weights = jnp.einsum("cqhe,ckhe->chqk", grad_out, values, preferred_element_type=WIDE)
    inner = jnp.sum(weights * grad_weights, -1, keepdims=True)
    grad_scores = (weights * (grad_weights - inner)).astype(NARROW)
    grad_queries = (
        jnp.einsum("chqk,ckhe->cqhe", grad_scores, keys, preferred_element_type=WIDE) * scale
    )
    grad_keys = (
        jnp.einsum("chqk,cqhe->ckhe", grad_scores, queries, preferred_element_type=WIDE) * scale
    )
    grad_values = jnp.einsum(
        "chqk,cqhe->ckhe", weights.astype(NARROW), grad_out, preferred_element_type=WIDE
    )
    return (grad_queries, grad_keys, grad_values)


def on_device(
    n_batch,
    tokens,
    images,
    caption_image,
    self_qkv,
    self_out,
    cross_q,
    cross_kv,
    cross_out,
    mlp_in,
    mlp_out,
    ln_gains,
    ln_biases,
    cotangent,
):
    rows = tokens.shape[0]
    captions = rows // CAP_LEN
    pairs = images.shape[0]
    local_width = self_out.shape[0]
    heads = local_width // HEAD_DIM
    scale = HEAD_DIM ** (-0.5)
    causal = lax.broadcasted_iota(jnp.int32, (CAP_LEN, CAP_LEN), 0) >= lax.broadcasted_iota(
        jnp.int32, (CAP_LEN, CAP_LEN), 1
    )
    w_qkv = self_qkv.astype(NARROW)
    w_self = self_out.astype(NARROW)
    w_query = cross_q.astype(NARROW)
    w_pair = cross_kv.astype(NARROW)
    w_cross = cross_out.astype(NARROW)
    w_inner = mlp_in.astype(NARROW)
    w_outer = mlp_out.astype(NARROW)
    normed_one = layer_norm(tokens, ln_gains[0], ln_biases[0]).astype(NARROW)
    projected = jnp.einsum("td,sde->ste", normed_one, w_qkv, preferred_element_type=WIDE).astype(
        NARROW
    )
    self_queries = split_heads(projected[0], captions, heads)
    self_keys = split_heads(projected[1], captions, heads)
    self_values = split_heads(projected[2], captions, heads)
    mixed_self, self_logsum = attend(self_queries, self_keys, self_values, causal, scale)
    joined_self = mixed_self.reshape(rows, local_width).astype(NARROW)
    after_self = tokens + tensor_sum(matmul(joined_self, w_self))
    normed_two = layer_norm(after_self, ln_gains[1], ln_biases[1]).astype(NARROW)
    cross_queries = split_heads(matmul(normed_two, w_query).astype(NARROW), captions, heads)
    image_kv = jnp.einsum("pnd,sde->spne", images, w_pair, preferred_element_type=WIDE).astype(
        NARROW
    )
    local_ids = caption_image - lax.axis_index("batch") * pairs
    picked = jnp.take(image_kv, local_ids, axis=1)
    cross_keys = split_heads(picked[0], captions, heads)
    cross_values = split_heads(picked[1], captions, heads)
    mixed_cross, cross_logsum = attend(cross_queries, cross_keys, cross_values, None, scale)
    joined_cross = mixed_cross.reshape(rows, local_width).astype(NARROW)
    after_cross = after_self + tensor_sum(matmul(joined_cross, w_cross))
    normed_three = layer_norm(after_cross, ln_gains[2], ln_biases[2]).astype(NARROW)
    hidden_pre = matmul(normed_three, w_inner)
    hidden = jax.nn.gelu(hidden_pre).astype(NARROW)
    mixed = after_cross + tensor_sum(matmul(hidden, w_outer))
    grad_branch = cotangent.astype(NARROW)
    grad_mlp_out = left_product(grad_branch, hidden)
    grad_hidden = right_product(grad_branch, w_outer)
    gelu_back = jax.vjp(jax.nn.gelu, hidden_pre)[1]
    grad_pre = gelu_back(grad_hidden)[0].astype(NARROW)
    grad_mlp_in = left_product(normed_three, grad_pre)
    grad_normed_three = tensor_sum(right_product(grad_pre, w_inner))
    norm_three_back = jax.vjp(layer_norm, after_cross, ln_gains[2], ln_biases[2])[1]
    input_three, gain_three, bias_three = norm_three_back(grad_normed_three)
    grad_after_cross = cotangent + input_three
    grad_cross_branch = grad_after_cross.astype(NARROW)
    grad_cross_out = left_product(grad_cross_branch, joined_cross)
    grad_mixed_cross = split_heads(
        right_product(grad_cross_branch, w_cross).astype(NARROW), captions, heads
    )
    grad_cq, grad_ck, grad_cv = attend_back(
        cross_queries, cross_keys, cross_values, None, scale, cross_logsum, grad_mixed_cross
    )
    grad_query_rows = grad_cq.reshape(rows, local_width).astype(NARROW)
    grad_cross_q = left_product(normed_two, grad_query_rows)
    chosen = (local_ids[:, None] == jnp.arange(pairs, dtype=jnp.int32)[None, :]).astype(WIDE)
    caption_grads = jnp.stack([grad_ck, grad_cv]).reshape(2, captions, -1, local_width)
    grad_pair = jnp.einsum(
        "cp,scne->spne", chosen, caption_grads, precision=lax.Precision.HIGHEST
    ).astype(NARROW)
    grad_cross_kv = jnp.einsum("pnd,spne->sde", images, grad_pair, preferred_element_type=WIDE)
    images_part = jnp.einsum("spne,sde->pnd", grad_pair, w_pair, preferred_element_type=WIDE)
    normed_two_part = right_product(grad_query_rows, w_query)
    grad_normed_two, grad_images = tensor_sum(normed_two_part), tensor_sum(images_part)
    norm_two_back = jax.vjp(layer_norm, after_self, ln_gains[1], ln_biases[1])[1]
    input_two, gain_two, bias_two = norm_two_back(grad_normed_two)
    grad_after_self = grad_after_cross + input_two
    grad_self_branch = grad_after_self.astype(NARROW)
    grad_self_out = left_product(grad_self_branch, joined_self)
    grad_mixed_self = split_heads(
        right_product(grad_self_branch, w_self).astype(NARROW), captions, heads
    )
    grad_sq, grad_sk, grad_sv = attend_back(
        self_queries, self_keys, self_values, causal, scale, self_logsum, grad_mixed_self
    )
    grad_projected = (
        jnp.stack([grad_sq, grad_sk, grad_sv]).reshape(3, rows, local_width).astype(NARROW)
    )
    grad_self_qkv = jnp.einsum(
        "td,ste->sde", normed_one, grad_projected, preferred_element_type=WIDE
    )
    normed_one_part = jnp.einsum("ste,sde->td", grad_projected, w_qkv, preferred_element_type=WIDE)
    grad_normed_one = tensor_sum(normed_one_part)
    norm_one_back = jax.vjp(layer_norm, tokens, ln_gains[0], ln_biases[0])[1]
    input_one, gain_one, bias_one = norm_one_back(grad_normed_one)
    grad_tokens = grad_after_self + input_one
    grad_gains = jnp.stack([gain_one, gain_two, gain_three])
    grad_biases = jnp.stack([bias_one, bias_two, bias_three])
    if n_batch == 16 and rows % 16 == 0:
        small = jnp.concatenate([grad_gains, grad_biases, jnp.zeros((122, grad_gains.shape[1]), WIDE)]).T
        s_q, s_k, s_v, s_self, s_query, s_pk, s_pv, s_cross, s_inner, s_outer, s_small = scatter_sums(
            [grad_self_qkv[0], grad_self_qkv[1], grad_self_qkv[2], grad_self_out, grad_cross_q, grad_cross_kv[0], grad_cross_kv[1],
             grad_cross_out, grad_mlp_in, grad_mlp_out, small])
        summed_qkv = jnp.stack([s_q[0], s_k[0], s_v[0]])
        summed_self = s_self[0].T
        summed_query = s_query[0]
        summed_pair = jnp.stack([s_pk[0], s_pv[0]])
        summed_cross = s_cross[0].T
        summed_inner = jnp.concatenate(s_inner, 1)
        summed_outer = jnp.concatenate([s.T for s in s_outer], 0)
        summed_gains = s_small[0][:, 0:3].T
        summed_biases = s_small[0][:, 3:6].T
    else:
        summed_qkv = lax.psum_scatter(grad_self_qkv, "batch", scatter_dimension=1, tiled=True)
        summed_self = lax.psum_scatter(grad_self_out.T, "batch", scatter_dimension=1, tiled=True)
        summed_query = lax.psum_scatter(grad_cross_q, "batch", scatter_dimension=0, tiled=True)
        summed_pair = lax.psum_scatter(grad_cross_kv, "batch", scatter_dimension=1, tiled=True)
        summed_cross = lax.psum_scatter(grad_cross_out.T, "batch", scatter_dimension=1, tiled=True)
        summed_inner = lax.psum_scatter(grad_mlp_in, "batch", scatter_dimension=0, tiled=True)
        summed_outer = lax.psum_scatter(grad_mlp_out.T, "batch", scatter_dimension=1, tiled=True)
        summed_gains = lax.psum_scatter(grad_gains, "batch", scatter_dimension=1, tiled=True)
        summed_biases = lax.psum_scatter(grad_biases, "batch", scatter_dimension=1, tiled=True)
    return (
        mixed,
        grad_tokens,
        grad_images,
        summed_qkv,
        summed_self,
        summed_query,
        summed_pair,
        summed_cross,
        summed_inner,
        summed_outer,
        summed_gains,
        summed_biases,
    )


def solution(mesh):
    in_specs = (
        P("batch", None),
        P("batch", None, None),
        P("batch"),
        P(None, None, "tensor"),
        P("tensor", None),
        P(None, "tensor"),
        P(None, None, "tensor"),
        P("tensor", None),
        P(None, "tensor"),
        P("tensor", None),
        P(),
        P(),
        P("batch", None),
    )
    out_specs = (
        P("batch", None),
        P("batch", None),
        P("batch", None, None),
        P(None, "batch", "tensor"),
        P("tensor", "batch"),
        P("batch", "tensor"),
        P(None, "batch", "tensor"),
        P("tensor", "batch"),
        P("batch", "tensor"),
        P("tensor", "batch"),
        P(None, "batch"),
        P(None, "batch"),
    )
    return jax.shard_map(
        functools.partial(on_device, mesh.shape["batch"]), mesh=mesh, in_specs=in_specs, out_specs=out_specs, check_vma=False
    )
```

```python
import functools

import jax
import jax.numpy as jnp
from jax import lax
from jax.experimental import pallas as pl
from jax.experimental.pallas import tpu as pltpu
from jax.sharding import PartitionSpec as P

HEAD_DIM = 64
CAP_LEN = 64


EPS = 1e-05
MASKED = -1e30
NARROW = jnp.bfloat16
WIDE = jnp.float32


MESH = pl.DeviceIdType.MESH
SIDE = 384
ROWS_OUT = 48
SCALE = HEAD_DIM ** (-0.5)
GELU_A = 0.7978845608028654
GELU_B = 0.044715
N_BLOCKS = 16
VMEM_BYTES = 64 * 2**20


def dot_nn(a, b):
    return lax.dot_general(a, b, (((1,), (0,)), ((), ())), preferred_element_type=WIDE)


def dot_nt(a, b):
    return lax.dot_general(a, b, (((1,), (1,)), ((), ())), preferred_element_type=WIDE)


def dot_tn(a, b):
    return lax.dot_general(a, b, (((0,), (0,)), ((), ())), preferred_element_type=WIDE)


def ln_parts(v):
    center = v - jnp.mean(v, -1, keepdims=True)
    spread = jnp.mean(center * center, -1, keepdims=True)
    r = lax.rsqrt(spread + EPS)
    return center * r, r


def ln_back(v, gain, grad):
    hat, r = ln_parts(v)
    e = grad * gain
    inner = jnp.mean(e * hat, -1, keepdims=True)
    dx = r * (e - jnp.mean(e, -1, keepdims=True) - hat * inner)
    return dx, jnp.sum(grad * hat, 0, keepdims=True), jnp.sum(grad, 0, keepdims=True)


def two_heads(v):
    lane = lax.broadcasted_iota(jnp.int32, v.shape, 1)
    zero = jnp.zeros_like(v)
    return jnp.concatenate([jnp.where(lane < HEAD_DIM, v, zero), jnp.where(lane >= HEAD_DIM, v, zero)], 0)


def one_pair(v):
    n = v.shape[0] // 2
    lane = lax.broadcasted_iota(jnp.int32, (n, v.shape[1]), 1)
    return jnp.where(lane < HEAD_DIM, v[:n], v[n:])


def weights_of(k, q2, mask):
    s = dot_nt(k, q2) * SCALE
    if mask is not None:
        s = jnp.where(mask, s, MASKED)
    e = jnp.exp(s - jnp.max(s, 0, keepdims=True))
    return e * (1.0 / jnp.sum(e, 0, keepdims=True))


def pair_forward(q, k, v, mask):
    p = weights_of(k, two_heads(q), mask)
    return one_pair(dot_tn(p.astype(NARROW), v)).astype(NARROW)


def pair_backward(q, k, v, do, mask):
    q2, do2 = two_heads(q), two_heads(do)
    p = weights_of(k, q2, mask)
    dp = dot_nt(v, do2)
    ds = (p * (dp - jnp.sum(p * dp, 0, keepdims=True))).astype(NARROW)
    dq = one_pair(dot_tn(ds, k)) * SCALE
    dk = dot_nn(ds, q2) * SCALE
    dv = dot_nn(p.astype(NARROW), do2)
    return dq.astype(NARROW), dk.astype(NARROW), dv.astype(NARROW)


def layer_kernel(
    tokens, images, caption_image, self_qkv, self_out, cross_q, cross_kv, cross_out, mlp_in, mlp_out, gains, biases, cotangent,
    o_mixed, o_tokens, o_images, o_qkv, o_self, o_query, o_pair, o_cross, o_inner, o_outer, o_small,
    stage, from_core, from_x, from_z, small, small_core, small_x, small_z,
    w_qkv, w_self, w_query, w_pair, w_cross, w_inner, w_outer, land_r, land_c,
    f_a, f_b, tok, cot, aft_self, aft_cross,
    rows, normed_two, t_one, t_two, t_a, t_b,
    qkv, o_s, q_c, o_c, d_oc, kv, img,
    send_o, land_os, land_oc, hidden, g_pre, g_m,
    send_n, land_n3, send_m, land_m, land_n1, sums,
    in_sem, stage_sem, out_sem, ws, wr, ex_s, ex_r, s1, r1, s2, r2, s3, r3,
):
    b, t = lax.axis_index("batch"), lax.axis_index("tensor")
    core, x, z = b % 2, (b // 2) % 2, b // 4
    zl = z % 2
    core_peer = b + 1 - 2 * core
    x_peer = b + 2 - 4 * x
    zn_peer = b + 4 - 8 * zl
    z_peers = [((z + d) % 4) * 4 + b % 4 for d in (1, 2, 3)]
    other = 1 - t

    def remote(src, dst, send, recv, peer, side=None):
        return pltpu.make_async_remote_copy(
            src, dst, send, recv, device_id=(peer, t if side is None else side), device_id_type=MESH)

    loads = [
        pltpu.make_async_copy(tokens, f_a, in_sem.at[0]),
        pltpu.make_async_copy(images, img, in_sem.at[1]),
        pltpu.make_async_copy(cotangent, f_b, in_sem.at[2]),
    ]
    jobs = []
    for j in range(3):
        for r in range(2):
            jobs.append((self_qkv.at[j, pl.ds(r * SIDE, SIDE)], w_qkv, (j, pl.ds(r * SIDE, SIDE))))
    for c in range(2):
        jobs.append((self_out.at[:, pl.ds(c * SIDE, SIDE)], w_self, (t, slice(None), pl.ds(c * SIDE, SIDE))))
    for j in range(2):
        for r in range(2):
            jobs.append((cross_kv.at[j, pl.ds(r * SIDE, SIDE)], w_pair, (j, t, pl.ds(r * SIDE, SIDE))))
    for r in range(2):
        jobs.append((cross_q.at[pl.ds(r * SIDE, SIDE)], w_query, (t, pl.ds(r * SIDE, SIDE))))
    for c in range(2):
        jobs.append((cross_out.at[:, pl.ds(c * SIDE, SIDE)], w_cross, (t, slice(None), pl.ds(c * SIDE, SIDE))))
    for c in range(4):
        for r in range(2):
            jobs.append((mlp_in.at[pl.ds(r * SIDE, SIDE), pl.ds(c * SIDE, SIDE)], w_inner, (pl.ds(r * SIDE, SIDE), pl.ds(c * SIDE, SIDE))))
    for r in range(4):
        for c in range(2):
            jobs.append((mlp_out.at[pl.ds(r * SIDE, SIDE), pl.ds(c * SIDE, SIDE)], w_outer, (pl.ds(r * SIDE, SIDE), pl.ds(c * SIDE, SIDE))))
    slots = stage.shape[0]
    staged = [0]

    def stage_copy(n):
        return pltpu.make_async_copy(jobs[n][0], stage.at[n % slots], stage_sem.at[n % slots])

    def stage_until(n):
        while staged[0] < n:
            k = staged[0]
            stage_copy(k).wait()
            jobs[k][1][jobs[k][2]] = stage[k % slots].astype(NARROW)
            if k + slots < len(jobs):
                stage_copy(k + slots).start()
            staged[0] += 1

    loads[0].start()
    for n in range(slots):
        stage_copy(n).start()
    loads[1].start()
    loads[2].start()

    barrier = pltpu.get_barrier_semaphore()
    for peer in (core_peer, x_peer, *z_peers):
        pl.semaphore_signal(barrier, 1, device_id=(peer, t), device_id_type=MESH)
    pl.semaphore_signal(barrier, 1, device_id=(b, other), device_id_type=MESH)
    pl.semaphore_wait(barrier, 6)

    piece = zl * 4 + x * 2 + core
    at_x, at_z, at_xz = piece + 2 - 4 * x, piece + 4 - 8 * zl, piece + 6 - 4 * x - 8 * zl
    exchange_from = [self_out, cross_out, cross_q, cross_kv.at[0], cross_kv.at[1]]

    def part(k, p, half=None):
        size = ROWS_OUT if k < 2 else 2 * ROWS_OUT
        start = p * size
        if half is not None:
            size = size // 2
            start = start + half * size
        start = pl.multiple_of(start, 8)
        return land_r.at[k, pl.ds(start, size)] if k < 2 else land_c.at[k - 2, pl.ds(start, size)]

    def over_y(k):
        size = ROWS_OUT if k < 2 else 2 * ROWS_OUT
        src = exchange_from[k].at[pl.ds(pl.multiple_of(piece * size, 8), size)]
        return remote(src, part(k, piece), ws.at[k, 0], wr.at[k, 0], b, other)

    def over_x(k, p):
        return remote(part(k, p), part(k, p), ws.at[k, 1], wr.at[k, 1], x_peer)

    def over_z(k, p):
        return remote(part(k, p), part(k, p), ws.at[k, 2], wr.at[k, 2], zn_peer)

    def half_z(k, p):
        return remote(part(k, p, 0), part(k, p, 0), ws.at[k, 3], wr.at[k, 3], zn_peer)

    def half_x(k, p):
        return remote(part(k, p, 1), part(k, p, 1), ws.at[k, 4], wr.at[k, 4], x_peer)

    def to_core(k, p, n):
        return remote(part(k, p), part(k, p), ws.at[k, 5 + n], wr.at[k, 5 + n], core_peer)

    def w_first(k):
        over_y(k).start()

    def w_second(k):
        over_y(k).wait_recv()
        over_x(k, piece).start()
        over_z(k, piece).start()
        to_core(k, piece, 0).start()

    def w_third(k):
        over_x(k, at_x).wait_recv()
        half_z(k, at_x).start()
        to_core(k, at_x, 1).start()
        over_z(k, at_z).wait_recv()
        half_x(k, at_z).start()
        to_core(k, at_z, 2).start()

    def w_fourth(k):
        half_z(k, at_xz).wait_recv()
        half_x(k, at_xz).wait_recv()
        to_core(k, at_xz, 3).start()

    def w_last(k):
        flip = 1 - 2 * core
        for n, p in enumerate((piece, at_x, at_z, at_xz)):
            to_core(k, p + flip, n).wait_recv()
        if k == 0:
            w_self[other] = land_r[0].astype(NARROW)
        elif k == 1:
            w_cross[other] = land_r[1].astype(NARROW)
        elif k == 2:
            w_query[other] = land_c[0].astype(NARROW)
        else:
            w_pair[k - 3, other] = land_c[k - 2].astype(NARROW)

    def w_drain(k):
        over_y(k).wait_send()
        over_x(k, piece).wait_send()
        over_z(k, piece).wait_send()
        half_z(k, at_x).wait_send()
        half_x(k, at_z).wait_send()
        for n, p in enumerate((piece, at_x, at_z, at_xz)):
            to_core(k, p, n).wait_send()

    def swap(n, src, dst):
        return remote(src, dst, ex_s.at[n], ex_r.at[n], b, other)

    out_of = (
        [o_outer.at[:, pl.ds(i * SIDE, SIDE)] for i in range(4)]
        + [o_inner.at[:, pl.ds(i * SIDE, SIDE)] for i in range(4)]
        + [o_cross, o_query, o_pair.at[0], o_pair.at[1], o_self, o_qkv.at[0], o_qkv.at[1], o_qkv.at[2]]
    )

    def core_rows(side):
        return pl.ds(pl.multiple_of(side * SIDE, SIDE), SIDE)

    def x_rows(side):
        return pl.ds(pl.multiple_of(side * (SIDE // 2), SIDE // 2), SIDE // 2)

    def z_rows(at):
        return pl.ds(pl.multiple_of(at * ROWS_OUT, ROWS_OUT), ROWS_OUT)

    def block_of(i):
        return (stage.at[i % slots], from_core.at[i], from_x.at[i], from_z.at[i]) if i < N_BLOCKS else (
            small.at[core_rows(1 - core)], small_core, small_x, small_z)

    def sc_core(i):
        src, dst, _, _ = block_of(i)
        return remote(src, dst, s1.at[i], r1.at[i], core_peer)

    def sc_x(i):
        _, src, dst, _ = block_of(i)
        return remote(src.at[x_rows(1 - x)], dst, s2.at[i], r2.at[i], x_peer)

    def sc_z(i, d):
        _, _, src, dst = block_of(i)
        return remote(src.at[z_rows((z + d) % 4)], dst.at[d - 1], s3.at[i, d - 1], r3.at[i, d - 1], z_peers[d - 1])

    def sc_out(i):
        return pltpu.make_async_copy(block_of(i)[3].at[0], out_of[i] if i < N_BLOCKS else o_small, out_sem.at[i])

    def sc_send(i, left, right):
        if i >= slots:
            sc_core(i - slots).wait_send()
        stage[i % slots] = dot_nn(left(1 - core), right())
        sc_core(i).start()

    def sc_keep(i, left, right):
        mine = dot_nn(left(core), right())
        sc_core(i).wait_recv()
        from_core[i] = from_core[i] + mine
        sc_x(i).start()

    def sc_x_sum(i):
        sc_x(i).wait_recv()
        _, got, mine, _ = block_of(i)
        mine[...] = mine[...] + got[x_rows(x)]
        for d in (1, 2, 3):
            sc_z(i, d).start()

    def sc_z_sum(i):
        for d in (1, 2, 3):
            sc_z(i, d).wait_recv()
        _, _, mine, got = block_of(i)
        got[0] = (mine[z_rows(z)] + got[0]) + (got[1] + got[2])
        sc_out(i).start()

    ticked = [0]

    def tick(n=1):
        for _ in range(n):
            i = ticked[0]
            if i <= N_BLOCKS:
                sc_x_sum(i)
            if i - 2 >= 0:
                sc_z_sum(i - 2)
            ticked[0] += 1

    def put_transposed(value, ref):
        vt = value.T
        for zz in range(4):
            for xx in range(2):
                for cc in range(2):
                    block = (zz * 2 + xx) * 2 + cc
                    ref[pl.ds(cc * SIDE + xx * (SIDE // 2) + zz * ROWS_OUT, ROWS_OUT)] = vt[block * ROWS_OUT : (block + 1) * ROWS_OUT]

    def left_of(ref):
        return lambda side: ref[core_rows(side)]

    ids = [caption_image[c] - 2 * b for c in range(4)]
    def pick(options, at):
        value = options[3]
        for e in (2, 1, 0):
            value = jnp.where(at == e, options[e], value)
        return value

    slot_of = [ids[c] * 2 + sum([(ids[e] == ids[c]).astype(jnp.int32) for e in range(c)], jnp.int32(0)) for c in range(4)]
    caption_at = [sum([jnp.where(slot_of[c] == s, c, 0) for c in range(4)], jnp.int32(0)) for s in range(4)]

    def text(s):
        return pl.ds(s * CAP_LEN, CAP_LEN)

    for k in (0, 1):
        w_first(k)
    loads[0].wait()
    for s in range(4):
        v = pick([f_a[e] for e in range(4)], caption_at[s])
        tok[text(s)] = v
        hat, _ = ln_parts(v)
        rows[text(s)] = (hat * gains[0:1] + biases[0:1]).astype(NARROW)
    for j in range(3):
        stage_until(2 * j + 2)
        qkv[j] = dot_nn(rows[...], w_qkv[j]).astype(NARROW)

    key_at = lax.broadcasted_iota(jnp.int32, (256, 512), 0)
    query_at = lax.broadcasted_iota(jnp.int32, (256, 512), 1) % 256
    causal = (key_at <= query_at) & (key_at // CAP_LEN == query_at // CAP_LEN)

    def pair_cols(p):
        return pl.ds(p * 2 * HEAD_DIM, 2 * HEAD_DIM)

    for p in range(3):
        c = pair_cols(p)
        o = pair_forward(qkv[0, :, c], qkv[1, :, c], qkv[2, :, c], causal)
        o_s[t, :, c] = o
        send_o[:, c] = o.astype(WIDE)
    swap(0, send_o, land_os).start()

    stage_until(12)
    w_second(0)
    w_second(1)
    loads[1].wait()

    def kv_half(side):
        for j in range(2):
            for r in range(3):
                at = pl.ds(r * SIDE, SIDE)
                kv[j, side, at] = dot_nn(img[at], w_pair[j, side]).astype(NARROW)

    kv_half(t)
    w_third(0)
    put_transposed(rows[...], t_one)
    w_third(1)
    stage_until(16)
    loads[2].wait()
    for s in range(4):
        v = pick([f_b[e] for e in range(4)], caption_at[s])
        cot[text(s)] = v
        g_m[text(s)] = v.astype(NARROW)
    put_transposed(g_m[...], t_b)
    w_fourth(0)
    w_last(0)
    swap(0, send_o, land_os).wait()
    o_s[other] = land_os[...].astype(NARROW)
    for k in (2, 3, 4):
        w_first(k)
    after = dot_nn(o_s[0], w_self[0]) + dot_nn(o_s[1], w_self[1])
    aft_self[...] = tok[...] + after
    for s in range(4):
        hat, _ = ln_parts(aft_self[text(s)])
        normed_two[text(s)] = (hat * gains[1:2] + biases[1:2]).astype(NARROW)
    q_c[t] = dot_nn(normed_two[...], w_query[t]).astype(NARROW)

    def caps(i):
        return pl.ds(i * 2 * CAP_LEN, 2 * CAP_LEN)

    def keys(i):
        return pl.ds(i * 576, 576)

    for p in range(3):
        for i in range(2):
            c = pair_cols(p)
            o = pair_forward(q_c[t, caps(i), c], kv[0, t, keys(i), c], kv[1, t, keys(i), c], None)
            o_c[t, caps(i), c] = o
            send_o[caps(i), c] = o.astype(WIDE)
    swap(1, send_o, land_oc).start()
    w_fourth(1)
    w_last(1)
    put_transposed(normed_two[...], t_two)
    stage_until(32)
    for k in (2, 3, 4):
        w_second(k)
    for k in (2, 3, 4):
        w_third(k)
    swap(1, send_o, land_oc).wait()
    o_c[other] = land_oc[...].astype(NARROW)
    after = dot_nn(o_c[0], w_cross[0]) + dot_nn(o_c[1], w_cross[1])
    aft_cross[...] = aft_self[...] + after
    for s in range(4):
        hat, _ = ln_parts(aft_cross[text(s)])
        rows[text(s)] = (hat * gains[2:3] + biases[2:3]).astype(NARROW)

    def cols(i):
        return pl.ds(i * SIDE, SIDE)

    for i in range(4):
        v = dot_nn(rows[...], w_inner[:, cols(i)])
        th = jnp.tanh(GELU_A * (v + GELU_B * (v * v * v)))
        hidden[:, cols(i)] = (0.5 * v * (1.0 + th)).astype(NARROW)
        slope = 0.5 * (1.0 + th) + 0.5 * v * (1.0 - th * th) * (GELU_A * (1.0 + 3.0 * GELU_B * (v * v)))
        g_pre[:, cols(i)] = (slope * dot_nt(g_m[...], w_outer[cols(i)])).astype(NARROW)
        sc_send(i, left_of(t_b), lambda: hidden[:, cols(i)])
        if i:
            sc_keep(i - 1, left_of(t_b), lambda: hidden[:, cols(i - 1)])
    send_n[...] = dot_nt(g_pre[...], w_inner[...])
    swap(2, send_n, land_n3).start()
    sc_keep(3, left_of(t_b), lambda: hidden[:, cols(3)])
    put_transposed(rows[...], t_a)
    for i in range(4):
        sc_send(4 + i, left_of(t_a), lambda: g_pre[:, cols(i)])
        if i:
            sc_keep(3 + i, left_of(t_a), lambda: g_pre[:, cols(i - 1)])
    sc_keep(7, left_of(t_a), lambda: g_pre[:, cols(3)])
    send_m[...] = dot_nn(hidden[...], w_outer[...])
    swap(3, send_m, land_m).start()

    for k in (2, 3, 4):
        w_fourth(k)
    tick()
    for k in (2, 3, 4):
        w_last(k)
    q_c[other] = dot_nn(normed_two[...], w_query[other]).astype(NARROW)
    kv_half(other)
    for r in range(3):
        vt = img[pl.ds(r * SIDE, SIDE)].T
        for zz in range(4):
            for xx in range(2):
                for cc in range(2):
                    block = (zz * 2 + xx) * 2 + cc
                    w_inner[pl.ds(cc * SIDE + xx * (SIDE // 2) + zz * ROWS_OUT, ROWS_OUT), cols(r)] = vt[block * ROWS_OUT : (block + 1) * ROWS_OUT]
    tick()
    swap(2, send_n, land_n3).wait()

    def norm_back(n, value, grad_of, into_rows):
        gain_sum, bias_sum = jnp.zeros((1, 768), WIDE), jnp.zeros((1, 768), WIDE)
        for s in range(4):
            dx, gs, bs = ln_back(value[text(s)], gains[n : n + 1], grad_of(s))
            res = cot[text(s)] + dx
            cot[text(s)] = res
            if into_rows is not None:
                into_rows[text(s)] = res.astype(NARROW)
            gain_sum, bias_sum = gain_sum + gs, bias_sum + bs
        sums[n : n + 1] = gain_sum
        sums[3 + n : 4 + n] = bias_sum

    sums[...] = jnp.zeros_like(sums)
    norm_back(2, aft_cross, lambda s: send_n[text(s)] + land_n3[text(s)], rows)
    put_transposed(rows[...], t_a)
    sc_send(8, left_of(t_a), lambda: o_c[t])
    for h in range(2):
        d_oc[h] = dot_nt(rows[...], w_cross[h]).astype(NARROW)
    sc_keep(8, left_of(t_a), lambda: o_c[t])
    tick()

    for h in range(2):
        for p in range(3):
            for i in range(2):
                c = pair_cols(p)
                dq, dk, dv = pair_backward(q_c[h, caps(i), c], kv[0, h, keys(i), c], kv[1, h, keys(i), c], d_oc[h, caps(i), c], None)
                q_c[h, caps(i), c] = dq
                kv[0, h, keys(i), c] = dk
                kv[1, h, keys(i), c] = dv
        tick()
    f_a[...] = (dot_nt(q_c[0], w_query[0]) + dot_nt(q_c[1], w_query[1])).reshape(f_a.shape)
    sc_send(9, left_of(t_two), lambda: q_c[t])
    norm_back(1, aft_self, lambda s: f_a[s], rows)
    sc_keep(9, left_of(t_two), lambda: q_c[t])
    for j in range(2):
        sc_send(10 + j, lambda side: w_inner[core_rows(side), pl.ds(0, 1152)], lambda: kv[j, t])
    for j in range(2):
        sc_keep(10 + j, lambda side: w_inner[core_rows(side), pl.ds(0, 1152)], lambda: kv[j, t])
    tick()
    put_transposed(rows[...], t_a)
    sc_send(12, left_of(t_a), lambda: o_s[t])
    d_oc[0] = dot_nt(rows[...], w_self[t]).astype(NARROW)
    sc_keep(12, left_of(t_a), lambda: o_s[t])
    for p in range(3):
        c = pair_cols(p)
        dq, dk, dv = pair_backward(qkv[0, :, c], qkv[1, :, c], qkv[2, :, c], d_oc[0, :, c], causal)
        qkv[0, :, c] = dq
        qkv[1, :, c] = dk
        qkv[2, :, c] = dv
    send_n[...] = (dot_nt(qkv[0], w_qkv[0]) + dot_nt(qkv[1], w_qkv[1])) + dot_nt(qkv[2], w_qkv[2])
    swap(4, send_n, land_n1).start()
    tick()
    for j in range(3):
        sc_send(13 + j, left_of(t_one), lambda: qkv[j])
    for j in range(3):
        sc_keep(13 + j, left_of(t_one), lambda: qkv[j])
    tick()

    for k in range(5):
        w_drain(k)

    def image_out(n):
        r, c = n // 2, n % 2
        return pltpu.make_async_copy(
            land_c.at[r, pl.ds(c * SIDE, SIDE)], o_images.at[pl.ds(r * SIDE, SIDE), cols(c)], out_sem.at[N_BLOCKS + 1 + n])

    for r in range(3):
        for c in range(2):
            at = pl.ds(r * SIDE, SIDE)
            total = None
            for j in range(2):
                for h in range(2):
                    term = dot_nt(kv[j, h, at], w_pair[j, h, cols(c)])
                    total = term if total is None else total + term
            land_c[r, pl.ds(c * SIDE, SIDE)] = total
            image_out(2 * r + c).start()
        tick()
    swap(3, send_m, land_m).wait()

    for s in range(4):
        send_m[text(s)] = aft_cross[text(s)] + (send_m[text(s)] + land_m[text(s)])
    for c in range(4):
        f_b[c] = pick([send_m[text(e)] for e in range(4)], slot_of[c])
    mixed_out = pltpu.make_async_copy(f_b, o_mixed, in_sem.at[0])
    mixed_out.start()
    tick()
    swap(4, send_n, land_n1).wait()
    norm_back(0, tok, lambda s: send_n[text(s)] + land_n1[text(s)], None)
    put_transposed(jnp.concatenate([sums[...], jnp.zeros((120, 768), WIDE)], 0), small)
    sc_core(N_BLOCKS).start()
    for c in range(4):
        f_a[c] = pick([cot[text(e)] for e in range(4)], slot_of[c])
    tokens_out = pltpu.make_async_copy(f_a, o_tokens, in_sem.at[1])
    tokens_out.start()
    sc_core(N_BLOCKS).wait_recv()
    small_core[...] = small_core[...] + small[core_rows(core)]
    sc_x(N_BLOCKS).start()
    while ticked[0] < N_BLOCKS + 3:
        tick()

    for i in range(N_BLOCKS + 1):
        if i >= N_BLOCKS - slots:
            sc_core(i).wait_send()
        sc_x(i).wait_send()
        for d in (1, 2, 3):
            sc_z(i, d).wait_send()
        sc_out(i).wait()
    for n in range(6):
        image_out(n).wait()
    mixed_out.wait()
    tokens_out.wait()


def fast_layer(
    tokens, images, caption_image, self_qkv, self_out, cross_q, cross_kv, cross_out, mlp_in, mlp_out, ln_gains, ln_biases, cotangent
):
    f32, bf16, dma = WIDE, NARROW, pltpu.SemaphoreType.DMA
    out = lambda *shape: jax.ShapeDtypeStruct(shape, f32)
    vmem = lambda kind, *shape: pltpu.VMEM(shape, kind)
    n = N_BLOCKS
    anywhere, local = pl.BlockSpec(memory_space=pl.ANY), pl.BlockSpec(memory_space=pltpu.VMEM)
    results = pl.pallas_call(
        layer_kernel,
        out_shape=[
            out(4, 64, 768), out(4, 64, 768), out(1152, 768), out(3, 48, 384), out(48, 384), out(48, 384), out(2, 48, 384),
            out(48, 384), out(48, 1536), out(48, 1536), out(48, 128),
        ],
        in_specs=[anywhere, anywhere, pl.BlockSpec(memory_space=pltpu.SMEM)] + [anywhere] * 7 + [local, local, anywhere],
        out_specs=[anywhere] * 11,
        scratch_shapes=[
            vmem(f32, 4, 384, 384), vmem(f32, n, 384, 384), vmem(f32, n, 192, 384), vmem(f32, n, 3, 48, 384),
            vmem(f32, 768, 128), vmem(f32, 384, 128), vmem(f32, 192, 128), vmem(f32, 3, 48, 128),
            vmem(bf16, 3, 768, 384), vmem(bf16, 2, 384, 768), vmem(bf16, 2, 768, 384), vmem(bf16, 2, 2, 768, 384),
            vmem(bf16, 2, 384, 768), vmem(bf16, 768, 1536), vmem(bf16, 1536, 768), vmem(f32, 2, 384, 768), vmem(f32, 3, 768, 384),
            vmem(f32, 4, 64, 768), vmem(f32, 4, 64, 768), vmem(f32, 256, 768), vmem(f32, 256, 768), vmem(f32, 256, 768), vmem(f32, 256, 768),
            vmem(bf16, 256, 768), vmem(bf16, 256, 768), vmem(bf16, 768, 256), vmem(bf16, 768, 256), vmem(bf16, 768, 256), vmem(bf16, 768, 256),
            vmem(bf16, 3, 256, 384), vmem(bf16, 2, 256, 384), vmem(bf16, 2, 256, 384), vmem(bf16, 2, 256, 384), vmem(bf16, 2, 256, 384),
            vmem(bf16, 2, 2, 1152, 384), vmem(bf16, 1152, 768),
            vmem(f32, 256, 384), vmem(f32, 256, 384), vmem(f32, 256, 384), vmem(bf16, 256, 1536), vmem(bf16, 256, 1536), vmem(bf16, 256, 768),
            vmem(f32, 256, 768), vmem(f32, 256, 768), vmem(f32, 256, 768), vmem(f32, 256, 768), vmem(f32, 256, 768), vmem(f32, 8, 768),
            dma((3,)), dma((4,)), dma((n + 7,)), dma((5, 9)), dma((5, 9)), dma((5,)), dma((5,)),
            dma((n + 1,)), dma((n + 1,)), dma((n + 1,)), dma((n + 1,)), dma((n + 1, 3)), dma((n + 1, 3)),
        ],
        compiler_params=pltpu.CompilerParams(collective_id=0, has_side_effects=True, vmem_limit_bytes=VMEM_BYTES),
        cost_estimate=pl.CostEstimate(flops=15_000_000_000, bytes_accessed=32_000_000, transcendentals=8_000_000),
        name="layer",
    )(
        tokens.reshape(4, 64, 768), images.reshape(1152, 768), caption_image, self_qkv, self_out, cross_q, cross_kv, cross_out,
        mlp_in, mlp_out, ln_gains, ln_biases, cotangent.reshape(4, 64, 768),
    )
    mixed, grad_tokens, grad_images, qkv, own_out, query, pair, cross, inner, outer, small = results
    return (
        mixed.reshape(256, 768), grad_tokens.reshape(256, 768), grad_images.reshape(2, 576, 768),
        qkv, own_out.T, query, pair, cross.T, inner, outer.T, small[:, 0:3].T, small[:, 3:6].T,
    )


def layer_norm(value, gain, bias):
    center = value - jnp.mean(value, -1, keepdims=True)
    spread = jnp.mean(center * center, -1, keepdims=True)
    return center * lax.rsqrt(spread + EPS) * gain + bias


def matmul(left, right):
    return jnp.dot(left, right, preferred_element_type=WIDE)


def left_product(left, right):
    return lax.dot_general(left, right, (((0,), (0,)), ((), ())), preferred_element_type=WIDE)


def right_product(left, right):
    return lax.dot_general(left, right, (((1,), (1,)), ((), ())), preferred_element_type=WIDE)


def split_heads(value, count, heads):
    return value.reshape(count, -1, heads, HEAD_DIM)


def masked_scores(queries, keys, mask, scale):
    scores = jnp.einsum("cqhe,ckhe->chqk", queries, keys, preferred_element_type=WIDE) * scale
    if mask is not None:
        scores = jnp.where(mask, scores, MASKED)
    return scores


def attend(queries, keys, values, mask, scale):
    scores = masked_scores(queries, keys, mask, scale)
    top = jnp.max(scores, -1, keepdims=True)
    expo = jnp.exp(scores - top)
    total = jnp.sum(expo, -1, keepdims=True)
    weights = (expo / total).astype(NARROW)
    outcome = jnp.einsum("chqk,ckhe->cqhe", weights, values, preferred_element_type=WIDE)
    return (outcome, top + jnp.log(total))


def attend_back(queries, keys, values, mask, scale, logsum, grad_out):
    scores = masked_scores(queries, keys, mask, scale)
    weights = jnp.exp(scores - logsum)
    grad_weights = jnp.einsum("cqhe,ckhe->chqk", grad_out, values, preferred_element_type=WIDE)
    inner = jnp.sum(weights * grad_weights, -1, keepdims=True)
    grad_scores = (weights * (grad_weights - inner)).astype(NARROW)
    grad_queries = (
        jnp.einsum("chqk,ckhe->cqhe", grad_scores, keys, preferred_element_type=WIDE) * scale
    )
    grad_keys = (
        jnp.einsum("chqk,cqhe->ckhe", grad_scores, queries, preferred_element_type=WIDE) * scale
    )
    grad_values = jnp.einsum(
        "chqk,cqhe->ckhe", weights.astype(NARROW), grad_out, preferred_element_type=WIDE
    )
    return (grad_queries, grad_keys, grad_values)


def on_device(
    tokens,
    images,
    caption_image,
    self_qkv,
    self_out,
    cross_q,
    cross_kv,
    cross_out,
    mlp_in,
    mlp_out,
    ln_gains,
    ln_biases,
    cotangent,
):
    rows = tokens.shape[0]
    captions = rows // CAP_LEN
    pairs = images.shape[0]
    local_width = self_out.shape[0]
    heads = local_width // HEAD_DIM
    scale = HEAD_DIM ** (-0.5)
    causal = lax.broadcasted_iota(jnp.int32, (CAP_LEN, CAP_LEN), 0) >= lax.broadcasted_iota(
        jnp.int32, (CAP_LEN, CAP_LEN), 1
    )
    w_qkv = self_qkv.astype(NARROW)
    w_self = self_out.astype(NARROW)
    w_query = cross_q.astype(NARROW)
    w_pair = cross_kv.astype(NARROW)
    w_cross = cross_out.astype(NARROW)
    w_inner = mlp_in.astype(NARROW)
    w_outer = mlp_out.astype(NARROW)
    normed_one = layer_norm(tokens, ln_gains[0], ln_biases[0]).astype(NARROW)
    projected = jnp.einsum("td,sde->ste", normed_one, w_qkv, preferred_element_type=WIDE).astype(
        NARROW
    )
    self_queries = split_heads(projected[0], captions, heads)
    self_keys = split_heads(projected[1], captions, heads)
    self_values = split_heads(projected[2], captions, heads)
    mixed_self, self_logsum = attend(self_queries, self_keys, self_values, causal, scale)
    joined_self = mixed_self.reshape(rows, local_width).astype(NARROW)
    after_self = tokens + lax.psum(matmul(joined_self, w_self), "tensor")
    normed_two = layer_norm(after_self, ln_gains[1], ln_biases[1]).astype(NARROW)
    cross_queries = split_heads(matmul(normed_two, w_query).astype(NARROW), captions, heads)
    image_kv = jnp.einsum("pnd,sde->spne", images, w_pair, preferred_element_type=WIDE).astype(
        NARROW
    )
    local_ids = caption_image - lax.axis_index("batch") * pairs
    picked = jnp.take(image_kv, local_ids, axis=1)
    cross_keys = split_heads(picked[0], captions, heads)
    cross_values = split_heads(picked[1], captions, heads)
    mixed_cross, cross_logsum = attend(cross_queries, cross_keys, cross_values, None, scale)
    joined_cross = mixed_cross.reshape(rows, local_width).astype(NARROW)
    after_cross = after_self + lax.psum(matmul(joined_cross, w_cross), "tensor")
    normed_three = layer_norm(after_cross, ln_gains[2], ln_biases[2]).astype(NARROW)
    hidden_pre = matmul(normed_three, w_inner)
    hidden = jax.nn.gelu(hidden_pre).astype(NARROW)
    mixed = after_cross + lax.psum(matmul(hidden, w_outer), "tensor")
    grad_branch = cotangent.astype(NARROW)
    grad_mlp_out = left_product(hidden, grad_branch)
    grad_hidden = right_product(grad_branch, w_outer)
    gelu_back = jax.vjp(jax.nn.gelu, hidden_pre)[1]
    grad_pre = gelu_back(grad_hidden)[0].astype(NARROW)
    grad_mlp_in = left_product(normed_three, grad_pre)
    grad_normed_three = lax.psum(right_product(grad_pre, w_inner), "tensor")
    norm_three_back = jax.vjp(layer_norm, after_cross, ln_gains[2], ln_biases[2])[1]
    input_three, gain_three, bias_three = norm_three_back(grad_normed_three)
    grad_after_cross = cotangent + input_three
    grad_cross_branch = grad_after_cross.astype(NARROW)
    grad_cross_out = left_product(joined_cross, grad_cross_branch)
    grad_mixed_cross = split_heads(
        right_product(grad_cross_branch, w_cross).astype(NARROW), captions, heads
    )
    grad_cq, grad_ck, grad_cv = attend_back(
        cross_queries, cross_keys, cross_values, None, scale, cross_logsum, grad_mixed_cross
    )
    grad_query_rows = grad_cq.reshape(rows, local_width).astype(NARROW)
    grad_cross_q = left_product(normed_two, grad_query_rows)
    chosen = (local_ids[:, None] == jnp.arange(pairs, dtype=jnp.int32)[None, :]).astype(WIDE)
    caption_grads = jnp.stack([grad_ck, grad_cv]).reshape(2, captions, -1, local_width)
    grad_pair = jnp.einsum(
        "cp,scne->spne", chosen, caption_grads, precision=lax.Precision.HIGHEST
    ).astype(NARROW)
    grad_cross_kv = jnp.einsum("pnd,spne->sde", images, grad_pair, preferred_element_type=WIDE)
    images_part = jnp.einsum("spne,sde->pnd", grad_pair, w_pair, preferred_element_type=WIDE)
    normed_two_part = right_product(grad_query_rows, w_query)
    grad_normed_two, grad_images = lax.psum((normed_two_part, images_part), "tensor")
    norm_two_back = jax.vjp(layer_norm, after_self, ln_gains[1], ln_biases[1])[1]
    input_two, gain_two, bias_two = norm_two_back(grad_normed_two)
    grad_after_self = grad_after_cross + input_two
    grad_self_branch = grad_after_self.astype(NARROW)
    grad_self_out = left_product(joined_self, grad_self_branch)
    grad_mixed_self = split_heads(
        right_product(grad_self_branch, w_self).astype(NARROW), captions, heads
    )
    grad_sq, grad_sk, grad_sv = attend_back(
        self_queries, self_keys, self_values, causal, scale, self_logsum, grad_mixed_self
    )
    grad_projected = (
        jnp.stack([grad_sq, grad_sk, grad_sv]).reshape(3, rows, local_width).astype(NARROW)
    )
    grad_self_qkv = jnp.einsum(
        "td,ste->sde", normed_one, grad_projected, preferred_element_type=WIDE
    )
    normed_one_part = jnp.einsum("ste,sde->td", grad_projected, w_qkv, preferred_element_type=WIDE)
    grad_normed_one = lax.psum(normed_one_part, "tensor")
    norm_one_back = jax.vjp(layer_norm, tokens, ln_gains[0], ln_biases[0])[1]
    input_one, gain_one, bias_one = norm_one_back(grad_normed_one)
    grad_tokens = grad_after_self + input_one
    grad_gains = jnp.stack([gain_one, gain_two, gain_three])
    grad_biases = jnp.stack([bias_one, bias_two, bias_three])
    every_sum = (
        lax.psum_scatter(grad_self_qkv, "batch", scatter_dimension=1, tiled=True),
        lax.psum_scatter(grad_self_out, "batch", scatter_dimension=1, tiled=True),
        lax.psum_scatter(grad_cross_q, "batch", scatter_dimension=0, tiled=True),
        lax.psum_scatter(grad_cross_kv, "batch", scatter_dimension=1, tiled=True),
        lax.psum_scatter(grad_cross_out, "batch", scatter_dimension=1, tiled=True),
        lax.psum_scatter(grad_mlp_in, "batch", scatter_dimension=0, tiled=True),
        lax.psum_scatter(grad_mlp_out, "batch", scatter_dimension=1, tiled=True),
        lax.psum_scatter(grad_gains, "batch", scatter_dimension=1, tiled=True),
        lax.psum_scatter(grad_biases, "batch", scatter_dimension=1, tiled=True),
    )
    (
        summed_qkv,
        summed_self,
        summed_query,
        summed_pair,
        summed_cross,
        summed_inner,
        summed_outer,
        summed_gains,
        summed_biases,
    ) = every_sum
    return (
        mixed,
        grad_tokens,
        grad_images,
        summed_qkv,
        summed_self,
        summed_query,
        summed_pair,
        summed_cross,
        summed_inner,
        summed_outer,
        summed_gains,
        summed_biases,
    )


def solution(mesh):
    in_specs = (
        P("batch", None),
        P("batch", None, None),
        P("batch"),
        P(None, None, "tensor"),
        P("tensor", None),
        P(None, "tensor"),
        P(None, None, "tensor"),
        P("tensor", None),
        P(None, "tensor"),
        P("tensor", None),
        P(),
        P(),
        P("batch", None),
    )
    out_specs = (
        P("batch", None),
        P("batch", None),
        P("batch", None, None),
        P(None, "batch", "tensor"),
        P("tensor", "batch"),
        P("batch", "tensor"),
        P(None, "batch", "tensor"),
        P("tensor", "batch"),
        P("batch", "tensor"),
        P("tensor", "batch"),
        P(None, "batch"),
        P(None, "batch"),
    )
    fast = mesh.shape["batch"] == 16 and mesh.shape["tensor"] == 2
    return jax.shard_map(
        fast_layer if fast else on_device, mesh=mesh, in_specs=in_specs, out_specs=out_specs, check_vma=False
    )
```

```python
import functools

import jax
import jax.numpy as jnp
from jax import lax
from jax.experimental import pallas as pl
from jax.experimental.pallas import tpu as pltpu
from jax.sharding import PartitionSpec as P

HEAD_DIM = 64
CAP_LEN = 64


EPS = 1e-05
MASKED = -1e30
NARROW = jnp.bfloat16
WIDE = jnp.float32


MESH = pl.DeviceIdType.MESH
SIDE = 384
ROWS_OUT = 48
SCALE = HEAD_DIM ** (-0.5)
GELU_A = 0.7978845608028654
GELU_B = 0.044715
N_BLOCKS = 16
VMEM_BYTES = 64 * 2**20
Z_FIRST = (1, 6, 11)
X_DEPTH = 3
LAGS = (0, 3, 6)
W_AFTER_SELF, W_AFTER_CROSS = [2], [3]


def dot_nn(a, b):
    return lax.dot_general(a, b, (((1,), (0,)), ((), ())), preferred_element_type=WIDE)


def dot_nt(a, b):
    return lax.dot_general(a, b, (((1,), (1,)), ((), ())), preferred_element_type=WIDE)


def dot_tn(a, b):
    return lax.dot_general(a, b, (((0,), (0,)), ((), ())), preferred_element_type=WIDE)


def ln_parts(v):
    center = v - jnp.mean(v, -1, keepdims=True)
    spread = jnp.mean(center * center, -1, keepdims=True)
    r = lax.rsqrt(spread + EPS)
    return center * r, r


def ln_back(v, gain, grad):
    hat, r = ln_parts(v)
    e = grad * gain
    inner = jnp.mean(e * hat, -1, keepdims=True)
    dx = r * (e - jnp.mean(e, -1, keepdims=True) - hat * inner)
    return dx, jnp.sum(grad * hat, 0, keepdims=True), jnp.sum(grad, 0, keepdims=True)


def two_heads(v):
    lane = lax.broadcasted_iota(jnp.int32, v.shape, 1)
    zero = jnp.zeros_like(v)
    return jnp.concatenate([jnp.where(lane < HEAD_DIM, v, zero), jnp.where(lane >= HEAD_DIM, v, zero)], 0)


def one_pair(v):
    n = v.shape[0] // 2
    lane = lax.broadcasted_iota(jnp.int32, (n, v.shape[1]), 1)
    return jnp.where(lane < HEAD_DIM, v[:n], v[n:])


def weights_of(k, q2, mask):
    s = dot_nt(k, q2) * SCALE
    if mask is not None:
        s = jnp.where(mask, s, MASKED)
    e = jnp.exp(s - jnp.max(s, 0, keepdims=True))
    return e * (1.0 / jnp.sum(e, 0, keepdims=True))


def pair_forward(q, k, v, mask):
    p = weights_of(k, two_heads(q), mask)
    return one_pair(dot_tn(p.astype(NARROW), v)).astype(NARROW)


def pair_backward(q, k, v, do, mask):
    q2, do2 = two_heads(q), two_heads(do)
    p = weights_of(k, q2, mask)
    dp = dot_nt(v, do2)
    ds = (p * (dp - jnp.sum(p * dp, 0, keepdims=True))).astype(NARROW)
    dq = one_pair(dot_tn(ds, k)) * SCALE
    dk = dot_nn(ds, q2) * SCALE
    dv = dot_nn(p.astype(NARROW), do2)
    return dq.astype(NARROW), dk.astype(NARROW), dv.astype(NARROW)


def layer_kernel(
    tokens, images, caption_image, self_qkv, self_out, cross_q, cross_kv, cross_out, mlp_in, mlp_out, gains, biases, cotangent,
    o_mixed, o_tokens, o_images, o_qkv, o_self, o_query, o_pair, o_cross, o_inner, o_outer, o_small,
    stage, from_core, from_x, from_z, late_z, late_x, small, small_core, small_x, small_z,
    w_qkv, w_self, w_query, w_pair, w_cross, w_inner, w_outer, land_r, land_c,
    f_a, f_b, tok, cot, aft_self, aft_cross,
    rows, normed_two, t_one, t_two, t_a, t_b,
    qkv, o_s, q_c, o_c, d_oc, kv, img,
    send_os, send_oc, land_os, land_oc, hidden, g_pre, g_m,
    send_n, land_n3, send_m, land_m, land_n1, sums,
    in_sem, stage_sem, out_sem, ws, wr, ex_s, ex_r, s1, r1, s2, r2, s3, r3,
):
    b, t = lax.axis_index("batch"), lax.axis_index("tensor")
    core, x, z = b % 2, (b // 2) % 2, b // 4
    zl = z % 2
    core_peer = b + 1 - 2 * core
    x_peer = b + 2 - 4 * x
    zn_peer = b + 4 - 8 * zl
    z_near, z_far, z_across = z + 1 - 2 * zl, (z + 2) % 4, 3 - z
    z_of = (z_near, z_far, z_across)
    z_peers = [at * 4 + b % 4 for at in z_of]
    at_end = (z == 0) | (z == 3)
    inside = (z == 1) | (z == 2)
    other = 1 - t

    def remote(src, dst, send, recv, peer, side=None):
        return pltpu.make_async_remote_copy(
            src, dst, send, recv, device_id=(peer, t if side is None else side), device_id_type=MESH)

    loads = [
        pltpu.make_async_copy(tokens, f_a, in_sem.at[0]),
        pltpu.make_async_copy(images, img, in_sem.at[1]),
        pltpu.make_async_copy(cotangent, f_b, in_sem.at[2]),
    ]
    jobs = []
    for j in range(3):
        for r in range(2):
            jobs.append((self_qkv.at[j, pl.ds(r * SIDE, SIDE)], w_qkv, (j, pl.ds(r * SIDE, SIDE))))
    for c in range(2):
        jobs.append((self_out.at[:, pl.ds(c * SIDE, SIDE)], w_self, (t, slice(None), pl.ds(c * SIDE, SIDE))))
    for j in range(2):
        for r in range(2):
            jobs.append((cross_kv.at[j, pl.ds(r * SIDE, SIDE)], w_pair, (j, t, pl.ds(r * SIDE, SIDE))))
    for r in range(2):
        jobs.append((cross_q.at[pl.ds(r * SIDE, SIDE)], w_query, (t, pl.ds(r * SIDE, SIDE))))
    for c in range(2):
        jobs.append((cross_out.at[:, pl.ds(c * SIDE, SIDE)], w_cross, (t, slice(None), pl.ds(c * SIDE, SIDE))))
    for c in range(4):
        for r in range(2):
            jobs.append((mlp_in.at[pl.ds(r * SIDE, SIDE), pl.ds(c * SIDE, SIDE)], w_inner, (pl.ds(r * SIDE, SIDE), pl.ds(c * SIDE, SIDE))))
    for r in range(4):
        for c in range(2):
            jobs.append((mlp_out.at[pl.ds(r * SIDE, SIDE), pl.ds(c * SIDE, SIDE)], w_outer, (pl.ds(r * SIDE, SIDE), pl.ds(c * SIDE, SIDE))))
    slots = stage.shape[0]
    staged = [0]

    def stage_copy(n):
        return pltpu.make_async_copy(jobs[n][0], stage.at[n % slots], stage_sem.at[n % slots])

    def stage_until(n):
        while staged[0] < n:
            k = staged[0]
            stage_copy(k).wait()
            jobs[k][1][jobs[k][2]] = stage[k % slots].astype(NARROW)
            if k + slots < len(jobs):
                stage_copy(k + slots).start()
            staged[0] += 1

    loads[0].start()
    for n in range(slots):
        stage_copy(n).start()
    loads[1].start()
    loads[2].start()

    barrier = pltpu.get_barrier_semaphore()
    for peer in (core_peer, x_peer, *z_peers):
        pl.semaphore_signal(barrier, 1, device_id=(peer, t), device_id_type=MESH)
    pl.semaphore_signal(barrier, 1, device_id=(b, other), device_id_type=MESH)

    piece = zl * 4 + x * 2 + core
    at_x, at_z, at_xz = piece + 2 - 4 * x, piece + 4 - 8 * zl, piece + 6 - 4 * x - 8 * zl
    exchange_from = [self_out, cross_out, cross_q]

    def part(k, p, half=None):
        size = ROWS_OUT if k < 2 else 2 * ROWS_OUT
        start = p * size
        if half is not None:
            size = size // 2
            start = start + half * size
        at = pl.ds(pl.multiple_of(start, 8), size)
        return land_r.at[k, at] if k < 2 else land_c.at[0, at] if k == 2 else land_c.at[pl.ds(1, 2), at]

    def over_y(k):
        size = ROWS_OUT if k < 2 else 2 * ROWS_OUT
        at = pl.ds(pl.multiple_of(piece * size, 8), size)
        src = exchange_from[k].at[at] if k < 3 else cross_kv.at[:, at]
        return remote(src, part(k, piece), ws.at[k, 0], wr.at[k, 0], b, other)

    def over_x(k, p):
        return remote(part(k, p), part(k, p), ws.at[k, 1], wr.at[k, 1], x_peer)

    def over_z(k, p):
        return remote(part(k, p), part(k, p), ws.at[k, 2], wr.at[k, 2], zn_peer)

    def half_z(k, p):
        return remote(part(k, p, 0), part(k, p, 0), ws.at[k, 3], wr.at[k, 3], zn_peer)

    def half_x(k, p):
        return remote(part(k, p, 1), part(k, p, 1), ws.at[k, 4], wr.at[k, 4], x_peer)

    def to_core(k, p, n):
        return remote(part(k, p), part(k, p), ws.at[k, 5 + n], wr.at[k, 5 + n], core_peer)

    def w_first(k):
        over_y(k).start()

    def w_second(k):
        over_y(k).wait_recv()
        over_x(k, piece).start()
        over_z(k, piece).start()
        to_core(k, piece, 0).start()

    def w_third(k):
        over_x(k, at_x).wait_recv()
        half_z(k, at_x).start()
        to_core(k, at_x, 1).start()
        over_z(k, at_z).wait_recv()
        half_x(k, at_z).start()
        to_core(k, at_z, 2).start()

    def w_fourth(k):
        half_z(k, at_xz).wait_recv()
        half_x(k, at_xz).wait_recv()
        to_core(k, at_xz, 3).start()

    def w_last(k):
        flip = 1 - 2 * core
        for n, p in enumerate((piece, at_x, at_z, at_xz)):
            to_core(k, p + flip, n).wait_recv()
        if k == 0:
            w_self[other] = land_r[0].astype(NARROW)
        elif k == 1:
            w_cross[other] = land_r[1].astype(NARROW)
        elif k == 2:
            w_query[other] = land_c[0].astype(NARROW)
        else:
            for j in range(2):
                w_pair[j, other] = land_c[1 + j].astype(NARROW)

    def w_drain(k):
        over_y(k).wait_send()
        over_x(k, piece).wait_send()
        over_z(k, piece).wait_send()
        half_z(k, at_x).wait_send()
        half_x(k, at_z).wait_send()
        for n, p in enumerate((piece, at_x, at_z, at_xz)):
            to_core(k, p, n).wait_send()

    def swap(n, src, dst):
        return remote(src, dst, ex_s.at[n], ex_r.at[n], b, other)

    out_of = (
        [o_outer.at[:, pl.ds(i * SIDE, SIDE)] for i in range(4)]
        + [o_inner.at[:, pl.ds(i * SIDE, SIDE)] for i in range(4)]
        + [o_cross, o_query, o_pair.at[0], o_pair.at[1], o_self, o_qkv.at[0], o_qkv.at[1], o_qkv.at[2], o_small]
    )
    x_first = [i for i in range(N_BLOCKS) if i not in Z_FIRST]

    def span(start, size):
        return pl.ds(pl.multiple_of(start, ROWS_OUT), size)

    def core_rows(side):
        return span(side * SIDE, SIDE)

    def x_rows(side):
        return span(side * (SIDE // 2), SIDE // 2)

    def z_rows(at):
        return span(at * ROWS_OUT, ROWS_OUT)

    def xz_rows(side, at):
        return span(side * (SIDE // 2) + at * ROWS_OUT, ROWS_OUT)

    def core_of(i):
        return (stage.at[i % slots], from_core.at[i]) if i < N_BLOCKS else (small.at[core_rows(1 - core)], small_core)

    def x_of(i):
        return from_x.at[x_first.index(i)] if i < N_BLOCKS else small_x

    def parts_of(i):
        if i in Z_FIRST:
            n = Z_FIRST.index(i)
            return [
                (lambda at, count=1, side=side: from_core.at[i, span(side * (SIDE // 2) + at * ROWS_OUT, ROWS_OUT * count)],
                 lambda slot, count=1, side=side: late_z.at[n, side, span(slot * ROWS_OUT, ROWS_OUT * count)])
                for side in range(2)
            ]
        land = from_z.at[x_first.index(i)] if i < N_BLOCKS else small_z
        return [
            (lambda at, count=1: x_of(i).at[span(at * ROWS_OUT, ROWS_OUT * count)],
             lambda slot, count=1: land.at[span(slot * ROWS_OUT, ROWS_OUT * count)])
        ]

    def sc_core(i):
        src, dst = core_of(i)
        return remote(src, dst, s1.at[i], r1.at[i], core_peer)

    def sc_x(i):
        if i in Z_FIRST:
            return remote(from_core.at[i, xz_rows(1 - x, z)], late_x.at[Z_FIRST.index(i)], s2.at[i], r2.at[i], x_peer)
        return remote(core_of(i)[1].at[x_rows(1 - x)], x_of(i), s2.at[i], r2.at[i], x_peer)

    def z_long(i, part):
        rows_of, land = parts_of(i)[part]
        return remote(rows_of(1 - z // 2, 3), land(0, 3), s3.at[i, 0, part], r3.at[i, 0, part], z_peers[0])

    def z_short(i, part, n):
        rows_of, land = parts_of(i)[part]
        at, slot = ((z_near, 0), (z_far, 1), (z_across, 3))[n]
        return remote(rows_of(at), land(slot), s3.at[i, n, part], r3.at[i, n, part], z_peers[n])

    def sc_out(i):
        src = from_core.at[i, xz_rows(x, z)] if i in Z_FIRST else x_of(i).at[z_rows(z)]
        return pltpu.make_async_copy(src, out_of[i], out_sem.at[i])

    waiting, flying = [], [0]

    def x_push():
        while waiting and flying[0] < X_DEPTH:
            sc_x(waiting.pop(0)).start()
            flying[0] += 1

    def sc_send(i, left, right):
        if i >= slots:
            sc_core(i - slots).wait_send()
        stage[i % slots] = dot_nn(left(1 - core), right())
        sc_core(i).start()

    def sc_kept(i):
        if i in Z_FIRST:
            z_begin(i)
        else:
            waiting.append(i)
            x_push()

    def sc_keep(i, left, right):
        mine = dot_nn(left(core), right())
        sc_core(i).wait_recv()
        from_core[i] = from_core[i] + mine
        sc_kept(i)

    def x_sum(i):
        sc_x(i).wait_recv()
        mine = x_of(i)
        mine[...] = mine[...] + core_of(i)[1][x_rows(x)]
        flying[0] -= 1
        x_push()

    def z_begin(i):
        for part in range(len(parts_of(i))):

            @pl.when(at_end)
            def _():
                z_long(i, part).start()

            @pl.when(inside)
            def _():
                z_short(i, part, 0).start()

    def z_middle(i):
        for part, (rows_of, land) in enumerate(parts_of(i)):

            @pl.when(inside)
            def _():
                z_long(i, part).wait_recv()
                for at, slot in ((z_across, 1), (z_far, 2 - 2 * (z // 2)), (z, 2 * (z // 2))):
                    ref = rows_of(at)
                    ref[...] = ref[...] + land(slot)[...]
                z_short(i, part, 2).start()
                z_short(i, part, 1).start()

    def z_end(i):
        for part, (rows_of, land) in enumerate(parts_of(i)):
            ref = rows_of(z)

            @pl.when(at_end)
            def _():
                z_short(i, part, 0).wait_recv()
                z_short(i, part, 1).wait_recv()
                ref[...] = ref[...] + (land(0)[...] + land(1)[...])

            @pl.when(inside)
            def _():
                z_short(i, part, 2).wait_recv()
                ref[...] = ref[...] + land(3)[...]

    def z_drain(i):
        for part in range(len(parts_of(i))):

            @pl.when(at_end)
            def _():
                z_long(i, part).wait_send()

            @pl.when(inside)
            def _():
                for n in range(3):
                    z_short(i, part, n).wait_send()

    def step(i, n):
        if i in Z_FIRST:
            if n == 0:
                z_middle(i)
            elif n == 1:
                z_end(i)
                sc_x(i).start()
            else:
                sc_x(i).wait_recv()
                ref = from_core.at[i, xz_rows(x, z)]
                ref[...] = ref[...] + late_x[Z_FIRST.index(i)]
                sc_out(i).start()
        elif n == 0:
            x_sum(i)
            z_begin(i)
        elif n == 1:
            z_middle(i)
        else:
            z_end(i)
            sc_out(i).start()

    ticked = [0]

    def tick(n=1):
        for _ in range(n):
            for n in (2, 1, 0):
                if 0 <= ticked[0] - LAGS[n] <= N_BLOCKS:
                    step(ticked[0] - LAGS[n], n)
            ticked[0] += 1

    def put_transposed(value, ref):
        vt = value.T
        for zz in range(4):
            for xx in range(2):
                for cc in range(2):
                    block = (zz * 2 + xx) * 2 + cc
                    ref[pl.ds(cc * SIDE + xx * (SIDE // 2) + zz * ROWS_OUT, ROWS_OUT)] = vt[block * ROWS_OUT : (block + 1) * ROWS_OUT]

    def left_of(ref):
        return lambda side: ref[core_rows(side)]

    ids = [caption_image[c] - 2 * b for c in range(4)]
    def pick(options, at):
        value = options[3]
        for e in (2, 1, 0):
            value = jnp.where(at == e, options[e], value)
        return value

    slot_of = [ids[c] * 2 + sum([(ids[e] == ids[c]).astype(jnp.int32) for e in range(c)], jnp.int32(0)) for c in range(4)]
    caption_at = [sum([jnp.where(slot_of[c] == s, c, 0) for c in range(4)], jnp.int32(0)) for s in range(4)]

    def text(s):
        return pl.ds(s * CAP_LEN, CAP_LEN)

    loads[0].wait()
    for s in range(4):
        v = pick([f_a[e] for e in range(4)], caption_at[s])
        tok[text(s)] = v
        hat, _ = ln_parts(v)
        rows[text(s)] = (hat * gains[0:1] + biases[0:1]).astype(NARROW)
    pl.semaphore_wait(barrier, 6)
    w_first(0)
    for j in range(3):
        stage_until(2 * j + 2)
        qkv[j] = dot_nn(rows[...], w_qkv[j]).astype(NARROW)

    w_first(1)
    key_at = lax.broadcasted_iota(jnp.int32, (128, 256), 0)
    query_at = lax.broadcasted_iota(jnp.int32, (128, 256), 1) % 128
    causal = (key_at <= query_at) & (key_at // CAP_LEN == query_at // CAP_LEN)

    def pair_cols(p):
        return pl.ds(p * 2 * HEAD_DIM, 2 * HEAD_DIM)

    def caps(i):
        return pl.ds(i * 2 * CAP_LEN, 2 * CAP_LEN)

    def keys(i):
        return pl.ds(i * 576, 576)

    def os_swap(i):
        return swap(i, send_os.at[caps(i)], land_os.at[caps(i)])

    def oc_swap(i):
        return swap(2 + i, send_oc.at[caps(i)], land_oc.at[caps(i)])

    for i in range(2):
        for p in range(3):
            c = pair_cols(p)
            o = pair_forward(qkv[0, caps(i), c], qkv[1, caps(i), c], qkv[2, caps(i), c], causal)
            o_s[t, caps(i), c] = o
            send_os[caps(i), c] = o.astype(WIDE)
        os_swap(i).start()

    def kv_half(side):
        for j in range(2):
            for r in range(3):
                at = pl.ds(r * SIDE, SIDE)
                kv[j, side, at] = dot_nn(img[at], w_pair[j, side]).astype(NARROW)

    for k in W_AFTER_SELF:
        w_first(k)
    w_second(0)
    stage_until(12)
    loads[1].wait()
    kv_half(t)
    w_third(0)
    w_second(1)
    put_transposed(rows[...], t_one)
    stage_until(16)
    loads[2].wait()
    for s in range(4):
        v = pick([f_b[e] for e in range(4)], caption_at[s])
        cot[text(s)] = v
        g_m[text(s)] = v.astype(NARROW)
    w_fourth(0)
    put_transposed(g_m[...], t_b)
    w_last(0)
    for i in range(2):
        os_swap(i).wait_recv()
        at = caps(i)
        o_s[other, at] = land_os[at].astype(NARROW)
        aft_self[at] = tok[at] + (dot_nn(o_s[0, at], w_self[0]) + dot_nn(o_s[1, at], w_self[1]))
        hat, _ = ln_parts(aft_self[at])
        normed_two[at] = (hat * gains[1:2] + biases[1:2]).astype(NARROW)
        q_c[t, at] = dot_nn(normed_two[at], w_query[t]).astype(NARROW)
        for p in range(3):
            c = pair_cols(p)
            o = pair_forward(q_c[t, at, c], kv[0, t, keys(i), c], kv[1, t, keys(i), c], None)
            o_c[t, at, c] = o
            send_oc[at, c] = o.astype(WIDE)
        oc_swap(i).start()
        if i == 0:
            w_third(1)
    for k in W_AFTER_CROSS:
        w_first(k)
    w_fourth(1)
    stage_until(24)
    w_last(1)
    for k in W_AFTER_SELF:
        w_second(k)
    put_transposed(normed_two[...], t_two)
    stage_until(32)
    for k in W_AFTER_SELF:
        w_third(k)

    def cols(i):
        return pl.ds(i * SIDE, SIDE)

    for i in range(2):
        oc_swap(i).wait_recv()
        at = caps(i)
        o_c[other, at] = land_oc[at].astype(NARROW)
        aft_cross[at] = aft_self[at] + (dot_nn(o_c[0, at], w_cross[0]) + dot_nn(o_c[1, at], w_cross[1]))
        hat, _ = ln_parts(aft_cross[at])
        rows[at] = (hat * gains[2:3] + biases[2:3]).astype(NARROW)
        for n in range(4):
            v = dot_nn(rows[at], w_inner[:, cols(n)])
            th = jnp.tanh(GELU_A * (v + GELU_B * (v * v * v)))
            hidden[at, cols(n)] = (0.5 * v * (1.0 + th)).astype(NARROW)
            slope = 0.5 * (1.0 + th) + 0.5 * v * (1.0 - th * th) * (GELU_A * (1.0 + 3.0 * GELU_B * (v * v)))
            if i == 1:
                sc_send(n, left_of(t_b), lambda: hidden[:, cols(n)])
            g_pre[at, cols(n)] = (slope * dot_nt(g_m[at], w_outer[cols(n)])).astype(NARROW)
            if i == 1 and n:
                sc_keep(n - 1, left_of(t_b), lambda: hidden[:, cols(n - 1)])

    send_n[...] = dot_nt(g_pre[...], w_inner[...])
    swap(4, send_n, land_n3).start()
    sc_keep(3, left_of(t_b), lambda: hidden[:, cols(3)])
    put_transposed(rows[...], t_a)
    for i in range(4):
        sc_send(4 + i, left_of(t_a), lambda: g_pre[:, cols(i)])
        if i:
            sc_keep(3 + i, left_of(t_a), lambda: g_pre[:, cols(i - 1)])
    sc_keep(7, left_of(t_a), lambda: g_pre[:, cols(3)])
    send_m[...] = dot_nn(hidden[...], w_outer[...])
    for k in W_AFTER_CROSS:
        w_second(k)
    for k in W_AFTER_CROSS:
        w_third(k)
    tick()
    for k in (2, 3):
        w_fourth(k)
    tick()
    for k in (2, 3):
        w_last(k)
    q_c[other] = dot_nn(normed_two[...], w_query[other]).astype(NARROW)
    kv_half(other)
    for r in range(3):
        vt = img[pl.ds(r * SIDE, SIDE)].T
        for zz in range(4):
            for xx in range(2):
                for cc in range(2):
                    block = (zz * 2 + xx) * 2 + cc
                    w_inner[pl.ds(cc * SIDE + xx * (SIDE // 2) + zz * ROWS_OUT, ROWS_OUT), cols(r)] = vt[block * ROWS_OUT : (block + 1) * ROWS_OUT]
    tick()
    swap(4, send_n, land_n3).wait()
    swap(5, send_m, land_m).start()

    def norm_back(n, value, grad_of, into_rows):
        gain_sum, bias_sum = jnp.zeros((1, 768), WIDE), jnp.zeros((1, 768), WIDE)
        for s in range(4):
            dx, gs, bs = ln_back(value[text(s)], gains[n : n + 1], grad_of(s))
            res = cot[text(s)] + dx
            cot[text(s)] = res
            if into_rows is not None:
                into_rows[text(s)] = res.astype(NARROW)
            gain_sum, bias_sum = gain_sum + gs, bias_sum + bs
        sums[n : n + 1] = gain_sum
        sums[3 + n : 4 + n] = bias_sum

    sums[...] = jnp.zeros_like(sums)
    norm_back(2, aft_cross, lambda s: send_n[text(s)] + land_n3[text(s)], rows)
    put_transposed(rows[...], t_a)
    sc_send(8, left_of(t_a), lambda: o_c[t])
    for h in range(2):
        d_oc[h] = dot_nt(rows[...], w_cross[h]).astype(NARROW)
    sc_keep(8, left_of(t_a), lambda: o_c[t])
    tick()

    for h in range(2):
        for p in range(3):
            for i in range(2):
                c = pair_cols(p)
                dq, dk, dv = pair_backward(q_c[h, caps(i), c], kv[0, h, keys(i), c], kv[1, h, keys(i), c], d_oc[h, caps(i), c], None)
                q_c[h, caps(i), c] = dq
                kv[0, h, keys(i), c] = dk
                kv[1, h, keys(i), c] = dv
        tick()
    f_a[...] = (dot_nt(q_c[0], w_query[0]) + dot_nt(q_c[1], w_query[1])).reshape(f_a.shape)
    sc_send(9, left_of(t_two), lambda: q_c[t])
    norm_back(1, aft_self, lambda s: f_a[s], rows)
    sc_keep(9, left_of(t_two), lambda: q_c[t])
    for j in range(2):
        sc_send(10 + j, lambda side: w_inner[core_rows(side), pl.ds(0, 1152)], lambda: kv[j, t])
    for j in range(2):
        sc_keep(10 + j, lambda side: w_inner[core_rows(side), pl.ds(0, 1152)], lambda: kv[j, t])
    tick()
    put_transposed(rows[...], t_a)
    sc_send(12, left_of(t_a), lambda: o_s[t])
    d_oc[0] = dot_nt(rows[...], w_self[t]).astype(NARROW)
    sc_keep(12, left_of(t_a), lambda: o_s[t])
    for i in range(2):
        for p in range(3):
            c = pair_cols(p)
            at = caps(i)
            dq, dk, dv = pair_backward(qkv[0, at, c], qkv[1, at, c], qkv[2, at, c], d_oc[0, at, c], causal)
            qkv[0, at, c] = dq
            qkv[1, at, c] = dk
            qkv[2, at, c] = dv
    send_n[...] = (dot_nt(qkv[0], w_qkv[0]) + dot_nt(qkv[1], w_qkv[1])) + dot_nt(qkv[2], w_qkv[2])
    swap(6, send_n, land_n1).start()
    tick()
    for j in range(3):
        sc_send(13 + j, left_of(t_one), lambda: qkv[j])
    for j in range(3):
        sc_keep(13 + j, left_of(t_one), lambda: qkv[j])
    tick()

    for k in range(4):
        w_drain(k)

    def image_out(n):
        r, c = n // 2, n % 2
        return pltpu.make_async_copy(
            land_c.at[r, pl.ds(c * SIDE, SIDE)], o_images.at[pl.ds(r * SIDE, SIDE), cols(c)], out_sem.at[N_BLOCKS + 1 + n])

    for r in range(3):
        for c in range(2):
            at = pl.ds(r * SIDE, SIDE)
            total = None
            for j in range(2):
                for h in range(2):
                    term = dot_nt(kv[j, h, at], w_pair[j, h, cols(c)])
                    total = term if total is None else total + term
            land_c[r, pl.ds(c * SIDE, SIDE)] = total
            image_out(2 * r + c).start()
        tick()
    swap(5, send_m, land_m).wait()

    for s in range(4):
        send_m[text(s)] = aft_cross[text(s)] + (send_m[text(s)] + land_m[text(s)])
    for c in range(4):
        f_b[c] = pick([send_m[text(e)] for e in range(4)], slot_of[c])
    mixed_out = pltpu.make_async_copy(f_b, o_mixed, in_sem.at[0])
    mixed_out.start()
    tick()
    swap(6, send_n, land_n1).wait()
    norm_back(0, tok, lambda s: send_n[text(s)] + land_n1[text(s)], None)
    put_transposed(jnp.concatenate([sums[...], jnp.zeros((120, 768), WIDE)], 0), small)
    sc_core(N_BLOCKS).start()
    for c in range(4):
        f_a[c] = pick([cot[text(e)] for e in range(4)], slot_of[c])
    tokens_out = pltpu.make_async_copy(f_a, o_tokens, in_sem.at[1])
    tokens_out.start()
    sc_core(N_BLOCKS).wait_recv()
    small_core[...] = small_core[...] + small[core_rows(core)]
    sc_kept(N_BLOCKS)
    tick(N_BLOCKS + 1 + LAGS[2] - ticked[0])

    for i in range(2):
        os_swap(i).wait_send()
        oc_swap(i).wait_send()
    for i in range(N_BLOCKS + 1):
        if i >= N_BLOCKS - slots:
            sc_core(i).wait_send()
        sc_x(i).wait_send()
        z_drain(i)
        sc_out(i).wait()
    for n in range(6):
        image_out(n).wait()
    mixed_out.wait()
    tokens_out.wait()


def finish_kernel(*refs):
    ins, outs, held, turned, (get, put) = refs[:11], refs[11:23], refs[23:34], refs[34:36], refs[36:38]
    pieces = [(0, slice(0, 2)), (0, slice(2, 4)), (1, slice(0, 2)), (1, slice(2, 4))]
    pieces += [(2, pl.ds(r * 192, 192)) for r in range(6)] + [(k, slice(None)) for k in range(3, 11)]
    loads = [pltpu.make_async_copy(ins[k].at[at], held[k].at[at], get.at[n]) for n, (k, at) in enumerate(pieces)]
    puts = [pltpu.make_async_copy(held[k].at[at], outs[k].at[at], put.at[n]) for n, (k, at) in enumerate(pieces[:-1])]
    for c in loads:
        c.start()
    loads[-1].wait()
    small = held[10][...].T
    for h in range(2):
        turned[h][...] = small[3 * h : 3 * h + 3]
        puts.append(pltpu.make_async_copy(turned[h], outs[10 + h], put.at[len(pieces) - 1 + h]))
        puts[-1].start()
    for n in range(len(pieces) - 1):
        loads[n].wait()
        puts[n].start()
    for c in puts:
        c.wait()


def fast_layer(
    tokens, images, caption_image, self_qkv, self_out, cross_q, cross_kv, cross_out, mlp_in, mlp_out, ln_gains, ln_biases, cotangent
):
    f32, bf16, dma = WIDE, NARROW, pltpu.SemaphoreType.DMA
    out = lambda *shape: jax.ShapeDtypeStruct(shape, f32)
    vmem = lambda kind, *shape: pltpu.VMEM(shape, kind)
    n, late = N_BLOCKS, len(Z_FIRST)
    anywhere, local = pl.BlockSpec(memory_space=pl.ANY), pl.BlockSpec(memory_space=pltpu.VMEM)
    results = pl.pallas_call(
        layer_kernel,
        out_shape=[
            out(4, 64, 768), out(4, 64, 768), out(1152, 768), out(3, 48, 384), out(48, 384), out(48, 384), out(2, 48, 384),
            out(48, 384), out(48, 1536), out(48, 1536), out(48, 128),
        ],
        in_specs=[anywhere, anywhere, pl.BlockSpec(memory_space=pltpu.SMEM)] + [anywhere] * 7 + [local, local, anywhere],
        out_specs=[anywhere] * 11,
        scratch_shapes=[
            vmem(f32, 4, 384, 384), vmem(f32, n, 384, 384), vmem(f32, n - late, 192, 384), vmem(f32, n - late, 192, 384),
            vmem(f32, late, 2, 192, 384), vmem(f32, late, 48, 384),
            vmem(f32, 768, 128), vmem(f32, 384, 128), vmem(f32, 192, 128), vmem(f32, 192, 128),
            vmem(bf16, 3, 768, 384), vmem(bf16, 2, 384, 768), vmem(bf16, 2, 768, 384), vmem(bf16, 2, 2, 768, 384),
            vmem(bf16, 2, 384, 768), vmem(bf16, 768, 1536), vmem(bf16, 1536, 768), vmem(f32, 2, 384, 768), vmem(f32, 3, 768, 384),
            vmem(f32, 4, 64, 768), vmem(f32, 4, 64, 768), vmem(f32, 256, 768), vmem(f32, 256, 768), vmem(f32, 256, 768), vmem(f32, 256, 768),
            vmem(bf16, 256, 768), vmem(bf16, 256, 768), vmem(bf16, 768, 256), vmem(bf16, 768, 256), vmem(bf16, 768, 256), vmem(bf16, 768, 256),
            vmem(bf16, 3, 256, 384), vmem(bf16, 2, 256, 384), vmem(bf16, 2, 256, 384), vmem(bf16, 2, 256, 384), vmem(bf16, 2, 256, 384),
            vmem(bf16, 2, 2, 1152, 384), vmem(bf16, 1152, 768),
            vmem(f32, 256, 384), vmem(f32, 256, 384), vmem(f32, 256, 384), vmem(f32, 256, 384), vmem(bf16, 256, 1536), vmem(bf16, 256, 1536), vmem(bf16, 256, 768),
            vmem(f32, 256, 768), vmem(f32, 256, 768), vmem(f32, 256, 768), vmem(f32, 256, 768), vmem(f32, 256, 768), vmem(f32, 8, 768),
            dma((3,)), dma((4,)), dma((n + 7,)), dma((4, 9)), dma((4, 9)), dma((7,)), dma((7,)),
            dma((n + 1,)), dma((n + 1,)), dma((n + 1,)), dma((n + 1,)), dma((n + 1, 3, 2)), dma((n + 1, 3, 2)),
        ],
        compiler_params=pltpu.CompilerParams(collective_id=0, has_side_effects=True, vmem_limit_bytes=VMEM_BYTES),
        cost_estimate=pl.CostEstimate(flops=15_000_000_000, bytes_accessed=32_000_000, transcendentals=8_000_000),
        name="layer",
    )(
        tokens.reshape(4, 64, 768), images.reshape(1152, 768), caption_image, self_qkv, self_out, cross_q, cross_kv, cross_out,
        mlp_in, mlp_out, ln_gains, ln_biases, cotangent.reshape(4, 64, 768),
    )
    shapes = [tuple(r.shape) for r in results]
    mixed, grad_tokens, grad_images, qkv, own_out, query, pair, cross, inner, outer, by_gain, by_bias = pl.pallas_call(
        finish_kernel,
        out_shape=[out(*s) for s in shapes[:-1]] + [out(3, 48), out(3, 48)],
        in_specs=[anywhere] * 11,
        out_specs=[anywhere] * 12,
        scratch_shapes=[vmem(f32, *s) for s in shapes] + [vmem(f32, 3, 48), vmem(f32, 3, 48), dma((18,)), dma((19,))],
        compiler_params=pltpu.CompilerParams(vmem_limit_bytes=VMEM_BYTES),
        name="finish",
    )(*results)
    return (
        mixed.reshape(256, 768), grad_tokens.reshape(256, 768), grad_images.reshape(2, 576, 768),
        qkv, own_out.T, query, pair, cross.T, inner, outer.T, by_gain, by_bias,
    )


def layer_norm(value, gain, bias):
    center = value - jnp.mean(value, -1, keepdims=True)
    spread = jnp.mean(center * center, -1, keepdims=True)
    return center * lax.rsqrt(spread + EPS) * gain + bias


def matmul(left, right):
    return jnp.dot(left, right, preferred_element_type=WIDE)


def left_product(left, right):
    return lax.dot_general(left, right, (((0,), (0,)), ((), ())), preferred_element_type=WIDE)


def right_product(left, right):
    return lax.dot_general(left, right, (((1,), (1,)), ((), ())), preferred_element_type=WIDE)


def split_heads(value, count, heads):
    return value.reshape(count, -1, heads, HEAD_DIM)


def masked_scores(queries, keys, mask, scale):
    scores = jnp.einsum("cqhe,ckhe->chqk", queries, keys, preferred_element_type=WIDE) * scale
    if mask is not None:
        scores = jnp.where(mask, scores, MASKED)
    return scores


def attend(queries, keys, values, mask, scale):
    scores = masked_scores(queries, keys, mask, scale)
    top = jnp.max(scores, -1, keepdims=True)
    expo = jnp.exp(scores - top)
    total = jnp.sum(expo, -1, keepdims=True)
    weights = (expo / total).astype(NARROW)
    outcome = jnp.einsum("chqk,ckhe->cqhe", weights, values, preferred_element_type=WIDE)
    return (outcome, top + jnp.log(total))


def attend_back(queries, keys, values, mask, scale, logsum, grad_out):
    scores = masked_scores(queries, keys, mask, scale)
    weights = jnp.exp(scores - logsum)
    grad_weights = jnp.einsum("cqhe,ckhe->chqk", grad_out, values, preferred_element_type=WIDE)
    inner = jnp.sum(weights * grad_weights, -1, keepdims=True)
    grad_scores = (weights * (grad_weights - inner)).astype(NARROW)
    grad_queries = (
        jnp.einsum("chqk,ckhe->cqhe", grad_scores, keys, preferred_element_type=WIDE) * scale
    )
    grad_keys = (
        jnp.einsum("chqk,cqhe->ckhe", grad_scores, queries, preferred_element_type=WIDE) * scale
    )
    grad_values = jnp.einsum(
        "chqk,cqhe->ckhe", weights.astype(NARROW), grad_out, preferred_element_type=WIDE
    )
    return (grad_queries, grad_keys, grad_values)


def on_device(
    tokens,
    images,
    caption_image,
    self_qkv,
    self_out,
    cross_q,
    cross_kv,
    cross_out,
    mlp_in,
    mlp_out,
    ln_gains,
    ln_biases,
    cotangent,
):
    rows = tokens.shape[0]
    captions = rows // CAP_LEN
    pairs = images.shape[0]
    local_width = self_out.shape[0]
    heads = local_width // HEAD_DIM
    scale = HEAD_DIM ** (-0.5)
    causal = lax.broadcasted_iota(jnp.int32, (CAP_LEN, CAP_LEN), 0) >= lax.broadcasted_iota(
        jnp.int32, (CAP_LEN, CAP_LEN), 1
    )
    w_qkv = self_qkv.astype(NARROW)
    w_self = self_out.astype(NARROW)
    w_query = cross_q.astype(NARROW)
    w_pair = cross_kv.astype(NARROW)
    w_cross = cross_out.astype(NARROW)
    w_inner = mlp_in.astype(NARROW)
    w_outer = mlp_out.astype(NARROW)
    normed_one = layer_norm(tokens, ln_gains[0], ln_biases[0]).astype(NARROW)
    projected = jnp.einsum("td,sde->ste", normed_one, w_qkv, preferred_element_type=WIDE).astype(
        NARROW
    )
    self_queries = split_heads(projected[0], captions, heads)
    self_keys = split_heads(projected[1], captions, heads)
    self_values = split_heads(projected[2], captions, heads)
    mixed_self, self_logsum = attend(self_queries, self_keys, self_values, causal, scale)
    joined_self = mixed_self.reshape(rows, local_width).astype(NARROW)
    after_self = tokens + lax.psum(matmul(joined_self, w_self), "tensor")
    normed_two = layer_norm(after_self, ln_gains[1], ln_biases[1]).astype(NARROW)
    cross_queries = split_heads(matmul(normed_two, w_query).astype(NARROW), captions, heads)
    image_kv = jnp.einsum("pnd,sde->spne", images, w_pair, preferred_element_type=WIDE).astype(
        NARROW
    )
    local_ids = caption_image - lax.axis_index("batch") * pairs
    picked = jnp.take(image_kv, local_ids, axis=1)
    cross_keys = split_heads(picked[0], captions, heads)
    cross_values = split_heads(picked[1], captions, heads)
    mixed_cross, cross_logsum = attend(cross_queries, cross_keys, cross_values, None, scale)
    joined_cross = mixed_cross.reshape(rows, local_width).astype(NARROW)
    after_cross = after_self + lax.psum(matmul(joined_cross, w_cross), "tensor")
    normed_three = layer_norm(after_cross, ln_gains[2], ln_biases[2]).astype(NARROW)
    hidden_pre = matmul(normed_three, w_inner)
    hidden = jax.nn.gelu(hidden_pre).astype(NARROW)
    mixed = after_cross + lax.psum(matmul(hidden, w_outer), "tensor")
    grad_branch = cotangent.astype(NARROW)
    grad_mlp_out = left_product(hidden, grad_branch)
    grad_hidden = right_product(grad_branch, w_outer)
    gelu_back = jax.vjp(jax.nn.gelu, hidden_pre)[1]
    grad_pre = gelu_back(grad_hidden)[0].astype(NARROW)
    grad_mlp_in = left_product(normed_three, grad_pre)
    grad_normed_three = lax.psum(right_product(grad_pre, w_inner), "tensor")
    norm_three_back = jax.vjp(layer_norm, after_cross, ln_gains[2], ln_biases[2])[1]
    input_three, gain_three, bias_three = norm_three_back(grad_normed_three)
    grad_after_cross = cotangent + input_three
    grad_cross_branch = grad_after_cross.astype(NARROW)
    grad_cross_out = left_product(joined_cross, grad_cross_branch)
    grad_mixed_cross = split_heads(
        right_product(grad_cross_branch, w_cross).astype(NARROW), captions, heads
    )
    grad_cq, grad_ck, grad_cv = attend_back(
        cross_queries, cross_keys, cross_values, None, scale, cross_logsum, grad_mixed_cross
    )
    grad_query_rows = grad_cq.reshape(rows, local_width).astype(NARROW)
    grad_cross_q = left_product(normed_two, grad_query_rows)
    chosen = (local_ids[:, None] == jnp.arange(pairs, dtype=jnp.int32)[None, :]).astype(WIDE)
    caption_grads = jnp.stack([grad_ck, grad_cv]).reshape(2, captions, -1, local_width)
    grad_pair = jnp.einsum(
        "cp,scne->spne", chosen, caption_grads, precision=lax.Precision.HIGHEST
    ).astype(NARROW)
    grad_cross_kv = jnp.einsum("pnd,spne->sde", images, grad_pair, preferred_element_type=WIDE)
    images_part = jnp.einsum("spne,sde->pnd", grad_pair, w_pair, preferred_element_type=WIDE)
    normed_two_part = right_product(grad_query_rows, w_query)
    grad_normed_two, grad_images = lax.psum((normed_two_part, images_part), "tensor")
    norm_two_back = jax.vjp(layer_norm, after_self, ln_gains[1], ln_biases[1])[1]
    input_two, gain_two, bias_two = norm_two_back(grad_normed_two)
    grad_after_self = grad_after_cross + input_two
    grad_self_branch = grad_after_self.astype(NARROW)
    grad_self_out = left_product(joined_self, grad_self_branch)
    grad_mixed_self = split_heads(
        right_product(grad_self_branch, w_self).astype(NARROW), captions, heads
    )
    grad_sq, grad_sk, grad_sv = attend_back(
        self_queries, self_keys, self_values, causal, scale, self_logsum, grad_mixed_self
    )
    grad_projected = (
        jnp.stack([grad_sq, grad_sk, grad_sv]).reshape(3, rows, local_width).astype(NARROW)
    )
    grad_self_qkv = jnp.einsum(
        "td,ste->sde", normed_one, grad_projected, preferred_element_type=WIDE
    )
    normed_one_part = jnp.einsum("ste,sde->td", grad_projected, w_qkv, preferred_element_type=WIDE)
    grad_normed_one = lax.psum(normed_one_part, "tensor")
    norm_one_back = jax.vjp(layer_norm, tokens, ln_gains[0], ln_biases[0])[1]
    input_one, gain_one, bias_one = norm_one_back(grad_normed_one)
    grad_tokens = grad_after_self + input_one
    grad_gains = jnp.stack([gain_one, gain_two, gain_three])
    grad_biases = jnp.stack([bias_one, bias_two, bias_three])
    every_sum = (
        lax.psum_scatter(grad_self_qkv, "batch", scatter_dimension=1, tiled=True),
        lax.psum_scatter(grad_self_out, "batch", scatter_dimension=1, tiled=True),
        lax.psum_scatter(grad_cross_q, "batch", scatter_dimension=0, tiled=True),
        lax.psum_scatter(grad_cross_kv, "batch", scatter_dimension=1, tiled=True),
        lax.psum_scatter(grad_cross_out, "batch", scatter_dimension=1, tiled=True),
        lax.psum_scatter(grad_mlp_in, "batch", scatter_dimension=0, tiled=True),
        lax.psum_scatter(grad_mlp_out, "batch", scatter_dimension=1, tiled=True),
        lax.psum_scatter(grad_gains, "batch", scatter_dimension=1, tiled=True),
        lax.psum_scatter(grad_biases, "batch", scatter_dimension=1, tiled=True),
    )
    (
        summed_qkv,
        summed_self,
        summed_query,
        summed_pair,
        summed_cross,
        summed_inner,
        summed_outer,
        summed_gains,
        summed_biases,
    ) = every_sum
    return (
        mixed,
        grad_tokens,
        grad_images,
        summed_qkv,
        summed_self,
        summed_query,
        summed_pair,
        summed_cross,
        summed_inner,
        summed_outer,
        summed_gains,
        summed_biases,
    )


def solution(mesh):
    in_specs = (
        P("batch", None),
        P("batch", None, None),
        P("batch"),
        P(None, None, "tensor"),
        P("tensor", None),
        P(None, "tensor"),
        P(None, None, "tensor"),
        P("tensor", None),
        P(None, "tensor"),
        P("tensor", None),
        P(),
        P(),
        P("batch", None),
    )
    out_specs = (
        P("batch", None),
        P("batch", None),
        P("batch", None, None),
        P(None, "batch", "tensor"),
        P("tensor", "batch"),
        P("batch", "tensor"),
        P(None, "batch", "tensor"),
        P("tensor", "batch"),
        P("batch", "tensor"),
        P("tensor", "batch"),
        P(None, "batch"),
        P(None, "batch"),
    )
    fast = mesh.shape["batch"] == 16 and mesh.shape["tensor"] == 2
    return jax.shard_map(
        fast_layer if fast else on_device, mesh=mesh, in_specs=in_specs, out_specs=out_specs, check_vma=False
    )
```

```python
import functools

import jax
import jax.numpy as jnp
from jax import lax
from jax.experimental import pallas as pl
from jax.experimental.pallas import tpu as pltpu
from jax.sharding import PartitionSpec as P

HEAD_DIM = 64
CAP_LEN = 64


EPS = 1e-05
MASKED = -1e30
NARROW = jnp.bfloat16
WIDE = jnp.float32


MESH = pl.DeviceIdType.MESH
SIDE = 384
ROWS_OUT = 48
SCALE = HEAD_DIM ** (-0.5)
GELU_A = 0.7978845608028654
GELU_B = 0.044715
N_BLOCKS = 16
VMEM_BYTES = 64 * 2**20
Z_FIRST = (1, 7, 13)
X_DEPTH = 3
LAGS = (0, 3, 6)
W_AFTER_SELF, W_AFTER_CROSS = [2, 3], []


def dot_nn(a, b):
    return lax.dot_general(a, b, (((1,), (0,)), ((), ())), preferred_element_type=WIDE)


def dot_nt(a, b):
    return lax.dot_general(a, b, (((1,), (1,)), ((), ())), preferred_element_type=WIDE)


def dot_tn(a, b):
    return lax.dot_general(a, b, (((0,), (0,)), ((), ())), preferred_element_type=WIDE)


def ln_parts(v):
    center = v - jnp.mean(v, -1, keepdims=True)
    spread = jnp.mean(center * center, -1, keepdims=True)
    r = lax.rsqrt(spread + EPS)
    return center * r, r


def ln_back(v, gain, grad):
    hat, r = ln_parts(v)
    e = grad * gain
    inner = jnp.mean(e * hat, -1, keepdims=True)
    dx = r * (e - jnp.mean(e, -1, keepdims=True) - hat * inner)
    return dx, jnp.sum(grad * hat, 0, keepdims=True), jnp.sum(grad, 0, keepdims=True)


def two_heads(v):
    lane = lax.broadcasted_iota(jnp.int32, v.shape, 1)
    zero = jnp.zeros_like(v)
    return jnp.concatenate([jnp.where(lane < HEAD_DIM, v, zero), jnp.where(lane >= HEAD_DIM, v, zero)], 0)


def one_pair(v):
    n = v.shape[0] // 2
    lane = lax.broadcasted_iota(jnp.int32, (n, v.shape[1]), 1)
    return jnp.where(lane < HEAD_DIM, v[:n], v[n:])


def weights_of(k, q2, mask):
    s = dot_nt(k, q2) * SCALE
    if mask is not None:
        s = jnp.where(mask, s, MASKED)
    e = jnp.exp(s - jnp.max(s, 0, keepdims=True))
    return e * (1.0 / jnp.sum(e, 0, keepdims=True))


def pair_forward(q, k, v, mask):
    p = weights_of(k, two_heads(q), mask)
    return one_pair(dot_tn(p.astype(NARROW), v)).astype(NARROW)


def pair_backward(q, k, v, do, mask):
    q2, do2 = two_heads(q), two_heads(do)
    p = weights_of(k, q2, mask)
    dp = dot_nt(v, do2)
    ds = (p * (dp - jnp.sum(p * dp, 0, keepdims=True))).astype(NARROW)
    dq = one_pair(dot_tn(ds, k)) * SCALE
    dk = dot_nn(ds, q2) * SCALE
    dv = dot_nn(p.astype(NARROW), do2)
    return dq.astype(NARROW), dk.astype(NARROW), dv.astype(NARROW)


def layer_kernel(
    tokens, images, caption_image, self_qkv, self_out, cross_q, cross_kv, cross_out, mlp_in, mlp_out, gains, biases, cotangent,
    o_mixed, o_tokens, o_images, o_qkv, o_self, o_query, o_pair, o_cross, o_inner, o_outer, o_small,
    stage, from_core, from_x, from_z, late_z, late_x, small, small_core, small_x, small_z,
    w_qkv, w_self, w_query, w_pair, w_cross, w_inner, w_outer, land_r, land_c,
    f_a, f_b, tok, cot, aft_self, aft_cross,
    rows, normed_two, t_one, t_two, t_a, t_b,
    qkv, o_s, q_c, o_c, d_oc, kv, img,
    send_os, send_oc, land_os, land_oc, hidden, g_pre, g_m,
    send_n, land_n3, send_m, land_m, land_n1, sums,
    in_sem, stage_sem, out_sem, ws, wr, ex_s, ex_r, s1, r1, s2, r2, s3, r3,
):
    b, t = lax.axis_index("batch"), lax.axis_index("tensor")
    core, x, z = b % 2, (b // 2) % 2, b // 4
    zl = z % 2
    core_peer = b + 1 - 2 * core
    x_peer = b + 2 - 4 * x
    zn_peer = b + 4 - 8 * zl
    z_near, z_far, z_across = z + 1 - 2 * zl, (z + 2) % 4, 3 - z
    z_of = (z_near, z_far, z_across)
    z_peers = [at * 4 + b % 4 for at in z_of]
    at_end = (z == 0) | (z == 3)
    inside = (z == 1) | (z == 2)
    other = 1 - t

    def remote(src, dst, send, recv, peer, side=None):
        return pltpu.make_async_remote_copy(
            src, dst, send, recv, device_id=(peer, t if side is None else side), device_id_type=MESH)

    loads = [
        pltpu.make_async_copy(tokens, f_a, in_sem.at[0]),
        pltpu.make_async_copy(images, img, in_sem.at[1]),
        pltpu.make_async_copy(cotangent, f_b, in_sem.at[2]),
    ]
    jobs = []
    for j in range(3):
        for r in range(2):
            jobs.append((self_qkv.at[j, pl.ds(r * SIDE, SIDE)], w_qkv, (j, pl.ds(r * SIDE, SIDE))))
    for c in range(2):
        jobs.append((self_out.at[:, pl.ds(c * SIDE, SIDE)], w_self, (t, slice(None), pl.ds(c * SIDE, SIDE))))
    for j in range(2):
        for r in range(2):
            jobs.append((cross_kv.at[j, pl.ds(r * SIDE, SIDE)], w_pair, (j, t, pl.ds(r * SIDE, SIDE))))
    for r in range(2):
        jobs.append((cross_q.at[pl.ds(r * SIDE, SIDE)], w_query, (t, pl.ds(r * SIDE, SIDE))))
    for c in range(2):
        jobs.append((cross_out.at[:, pl.ds(c * SIDE, SIDE)], w_cross, (t, slice(None), pl.ds(c * SIDE, SIDE))))
    for c in range(4):
        for r in range(2):
            jobs.append((mlp_in.at[pl.ds(r * SIDE, SIDE), pl.ds(c * SIDE, SIDE)], w_inner, (pl.ds(r * SIDE, SIDE), pl.ds(c * SIDE, SIDE))))
    for r in range(4):
        for c in range(2):
            jobs.append((mlp_out.at[pl.ds(r * SIDE, SIDE), pl.ds(c * SIDE, SIDE)], w_outer, (pl.ds(r * SIDE, SIDE), pl.ds(c * SIDE, SIDE))))
    slots = stage.shape[0]
    staged = [0]

    def stage_copy(n):
        return pltpu.make_async_copy(jobs[n][0], stage.at[n % slots], stage_sem.at[n % slots])

    def stage_until(n):
        while staged[0] < n:
            k = staged[0]
            stage_copy(k).wait()
            jobs[k][1][jobs[k][2]] = stage[k % slots].astype(NARROW)
            if k + slots < len(jobs):
                stage_copy(k + slots).start()
            staged[0] += 1

    loads[0].start()
    for n in range(slots):
        stage_copy(n).start()
    loads[1].start()
    loads[2].start()

    barrier = pltpu.get_barrier_semaphore()
    for peer in (core_peer, x_peer, *z_peers):
        pl.semaphore_signal(barrier, 1, device_id=(peer, t), device_id_type=MESH)
    pl.semaphore_signal(barrier, 1, device_id=(b, other), device_id_type=MESH)

    piece = zl * 4 + x * 2 + core
    at_x, at_z, at_xz = piece + 2 - 4 * x, piece + 4 - 8 * zl, piece + 6 - 4 * x - 8 * zl
    exchange_from = [self_out, cross_out, cross_q]

    def part(k, p, half=None):
        size = ROWS_OUT if k < 2 else 2 * ROWS_OUT
        start = p * size
        if half is not None:
            size = size // 2
            start = start + half * size
        at = pl.ds(pl.multiple_of(start, 8), size)
        return land_r.at[k, at] if k < 2 else land_c.at[0, at] if k == 2 else land_c.at[pl.ds(1, 2), at]

    def over_y(k):
        size = ROWS_OUT if k < 2 else 2 * ROWS_OUT
        at = pl.ds(pl.multiple_of(piece * size, 8), size)
        src = exchange_from[k].at[at] if k < 3 else cross_kv.at[:, at]
        return remote(src, part(k, piece), ws.at[k, 0], wr.at[k, 0], b, other)

    def over_x(k, p):
        return remote(part(k, p), part(k, p), ws.at[k, 1], wr.at[k, 1], x_peer)

    def over_z(k, p):
        return remote(part(k, p), part(k, p), ws.at[k, 2], wr.at[k, 2], zn_peer)

    def half_z(k, p):
        return remote(part(k, p, 0), part(k, p, 0), ws.at[k, 3], wr.at[k, 3], zn_peer)

    def half_x(k, p):
        return remote(part(k, p, 1), part(k, p, 1), ws.at[k, 4], wr.at[k, 4], x_peer)

    def to_core(k, p, n):
        return remote(part(k, p), part(k, p), ws.at[k, 5 + n], wr.at[k, 5 + n], core_peer)

    def w_first(k):
        over_y(k).start()

    def w_second(k):
        over_y(k).wait_recv()
        over_x(k, piece).start()
        over_z(k, piece).start()
        to_core(k, piece, 0).start()

    def w_third(k):
        over_x(k, at_x).wait_recv()
        half_z(k, at_x).start()
        to_core(k, at_x, 1).start()
        over_z(k, at_z).wait_recv()
        half_x(k, at_z).start()
        to_core(k, at_z, 2).start()

    def w_fourth(k):
        half_z(k, at_xz).wait_recv()
        half_x(k, at_xz).wait_recv()
        to_core(k, at_xz, 3).start()

    def w_last(k):
        flip = 1 - 2 * core
        for n, p in enumerate((piece, at_x, at_z, at_xz)):
            to_core(k, p + flip, n).wait_recv()
        if k == 0:
            w_self[other] = land_r[0].astype(NARROW)
        elif k == 1:
            w_cross[other] = land_r[1].astype(NARROW)
        elif k == 2:
            w_query[other] = land_c[0].astype(NARROW)
        else:
            for j in range(2):
                w_pair[j, other] = land_c[1 + j].astype(NARROW)

    def w_drain(k):
        over_y(k).wait_send()
        over_x(k, piece).wait_send()
        over_z(k, piece).wait_send()
        half_z(k, at_x).wait_send()
        half_x(k, at_z).wait_send()
        for n, p in enumerate((piece, at_x, at_z, at_xz)):
            to_core(k, p, n).wait_send()

    def swap(n, src, dst):
        return remote(src, dst, ex_s.at[n], ex_r.at[n], b, other)

    out_of = (
        [o_outer.at[:, pl.ds(i * SIDE, SIDE)] for i in range(4)]
        + [o_inner.at[:, pl.ds(i * SIDE, SIDE)] for i in range(4)]
        + [o_cross, o_query, o_pair.at[0], o_pair.at[1], o_self, o_qkv.at[0], o_qkv.at[1], o_qkv.at[2], o_small]
    )
    x_first = [i for i in range(N_BLOCKS) if i not in Z_FIRST]

    def span(start, size):
        return pl.ds(pl.multiple_of(start, ROWS_OUT), size)

    def core_rows(side):
        return span(side * SIDE, SIDE)

    def x_rows(side):
        return span(side * (SIDE // 2), SIDE // 2)

    def z_rows(at):
        return span(at * ROWS_OUT, ROWS_OUT)

    def xz_rows(side, at):
        return span(side * (SIDE // 2) + at * ROWS_OUT, ROWS_OUT)

    def core_of(i):
        return (stage.at[i % slots], from_core.at[i]) if i < N_BLOCKS else (small.at[core_rows(1 - core)], small_core)

    def x_of(i):
        return from_x.at[x_first.index(i)] if i < N_BLOCKS else small_x

    def parts_of(i):
        if i in Z_FIRST:
            n = Z_FIRST.index(i)
            return [
                (lambda at, count=1, side=side: from_core.at[i, span(side * (SIDE // 2) + at * ROWS_OUT, ROWS_OUT * count)],
                 lambda slot, count=1, side=side: late_z.at[n, side, span(slot * ROWS_OUT, ROWS_OUT * count)])
                for side in range(2)
            ]
        land = from_z.at[x_first.index(i)] if i < N_BLOCKS else small_z
        return [
            (lambda at, count=1: x_of(i).at[span(at * ROWS_OUT, ROWS_OUT * count)],
             lambda slot, count=1: land.at[span(slot * ROWS_OUT, ROWS_OUT * count)])
        ]

    def sc_core(i):
        src, dst = core_of(i)
        return remote(src, dst, s1.at[i], r1.at[i], core_peer)

    def sc_x(i):
        if i in Z_FIRST:
            return remote(from_core.at[i, xz_rows(1 - x, z)], late_x.at[Z_FIRST.index(i)], s2.at[i], r2.at[i], x_peer)
        return remote(core_of(i)[1].at[x_rows(1 - x)], x_of(i), s2.at[i], r2.at[i], x_peer)

    def z_long(i, part):
        rows_of, land = parts_of(i)[part]
        return remote(rows_of(1 - z // 2, 3), land(0, 3), s3.at[i, 0, part], r3.at[i, 0, part], z_peers[0])

    def z_short(i, part, n):
        rows_of, land = parts_of(i)[part]
        at, slot = ((z_near, 0), (z_far, 1), (z_across, 3))[n]
        return remote(rows_of(at), land(slot), s3.at[i, n, part], r3.at[i, n, part], z_peers[n])

    def sc_out(i):
        src = from_core.at[i, xz_rows(x, z)] if i in Z_FIRST else x_of(i).at[z_rows(z)]
        return pltpu.make_async_copy(src, out_of[i], out_sem.at[i])

    waiting, flying = [], [0]

    def x_push():
        while waiting and flying[0] < X_DEPTH:
            sc_x(waiting.pop(0)).start()
            flying[0] += 1

    def sc_send(i, left, right):
        if i >= slots:
            sc_core(i - slots).wait_send()
        stage[i % slots] = dot_nn(left(1 - core), right())
        sc_core(i).start()

    def sc_kept(i):
        if i in Z_FIRST:
            z_begin(i)
        else:
            waiting.append(i)
            x_push()

    def sc_keep(i, left, right):
        mine = dot_nn(left(core), right())
        sc_core(i).wait_recv()
        from_core[i] = from_core[i] + mine
        sc_kept(i)

    def x_sum(i):
        sc_x(i).wait_recv()
        mine = x_of(i)
        mine[...] = mine[...] + core_of(i)[1][x_rows(x)]
        flying[0] -= 1
        x_push()

    def z_begin(i):
        for part in range(len(parts_of(i))):

            @pl.when(at_end)
            def _():
                z_long(i, part).start()

            @pl.when(inside)
            def _():
                z_short(i, part, 0).start()

    def z_middle(i):
        for part, (rows_of, land) in enumerate(parts_of(i)):

            @pl.when(inside)
            def _():
                z_long(i, part).wait_recv()
                for at, slot in ((z_across, 1), (z_far, 2 - 2 * (z // 2)), (z, 2 * (z // 2))):
                    ref = rows_of(at)
                    ref[...] = ref[...] + land(slot)[...]
                z_short(i, part, 2).start()
                z_short(i, part, 1).start()

    def z_end(i):
        for part, (rows_of, land) in enumerate(parts_of(i)):
            ref = rows_of(z)

            @pl.when(at_end)
            def _():
                z_short(i, part, 0).wait_recv()
                z_short(i, part, 1).wait_recv()
                ref[...] = ref[...] + (land(0)[...] + land(1)[...])

            @pl.when(inside)
            def _():
                z_short(i, part, 2).wait_recv()
                ref[...] = ref[...] + land(3)[...]

    def z_drain(i):
        for part in range(len(parts_of(i))):

            @pl.when(at_end)
            def _():
                z_long(i, part).wait_send()

            @pl.when(inside)
            def _():
                for n in range(3):
                    z_short(i, part, n).wait_send()

    def step(i, n):
        if i in Z_FIRST:
            if n == 0:
                z_middle(i)
            elif n == 1:
                z_end(i)
                sc_x(i).start()
            else:
                sc_x(i).wait_recv()
                ref = from_core.at[i, xz_rows(x, z)]
                ref[...] = ref[...] + late_x[Z_FIRST.index(i)]
                sc_out(i).start()
        elif n == 0:
            x_sum(i)
            z_begin(i)
        elif n == 1:
            z_middle(i)
        else:
            z_end(i)
            sc_out(i).start()

    ticked = [0]

    def tick(n=1):
        for _ in range(n):
            for n in (2, 1, 0):
                if 0 <= ticked[0] - LAGS[n] <= N_BLOCKS:
                    step(ticked[0] - LAGS[n], n)
            ticked[0] += 1

    def put_transposed(value, ref):
        vt = value.T
        for zz in range(4):
            for xx in range(2):
                for cc in range(2):
                    block = (zz * 2 + xx) * 2 + cc
                    ref[pl.ds(cc * SIDE + xx * (SIDE // 2) + zz * ROWS_OUT, ROWS_OUT)] = vt[block * ROWS_OUT : (block + 1) * ROWS_OUT]

    def left_of(ref):
        return lambda side: ref[core_rows(side)]

    ids = [caption_image[c] - 2 * b for c in range(4)]
    def pick(options, at):
        value = options[3]
        for e in (2, 1, 0):
            value = jnp.where(at == e, options[e], value)
        return value

    slot_of = [ids[c] * 2 + sum([(ids[e] == ids[c]).astype(jnp.int32) for e in range(c)], jnp.int32(0)) for c in range(4)]
    caption_at = [sum([jnp.where(slot_of[c] == s, c, 0) for c in range(4)], jnp.int32(0)) for s in range(4)]

    def text(s):
        return pl.ds(s * CAP_LEN, CAP_LEN)

    loads[0].wait()
    for s in range(4):
        v = pick([f_a[e] for e in range(4)], caption_at[s])
        tok[text(s)] = v
        hat, _ = ln_parts(v)
        rows[text(s)] = (hat * gains[0:1] + biases[0:1]).astype(NARROW)
    pl.semaphore_wait(barrier, 6)
    w_first(0)
    for j in range(3):
        stage_until(2 * j + 2)
        qkv[j] = dot_nn(rows[...], w_qkv[j]).astype(NARROW)

    w_first(1)
    key_at = lax.broadcasted_iota(jnp.int32, (128, 256), 0)
    query_at = lax.broadcasted_iota(jnp.int32, (128, 256), 1) % 128
    causal = (key_at <= query_at) & (key_at // CAP_LEN == query_at // CAP_LEN)

    def pair_cols(p):
        return pl.ds(p * 2 * HEAD_DIM, 2 * HEAD_DIM)

    def caps(i):
        return pl.ds(i * 2 * CAP_LEN, 2 * CAP_LEN)

    def keys(i):
        return pl.ds(i * 576, 576)

    def os_swap(i):
        return swap(i, send_os.at[caps(i)], land_os.at[caps(i)])

    def oc_swap(i):
        return swap(2 + i, send_oc.at[caps(i)], land_oc.at[caps(i)])

    for i in range(2):
        for p in range(3):
            c = pair_cols(p)
            o = pair_forward(qkv[0, caps(i), c], qkv[1, caps(i), c], qkv[2, caps(i), c], causal)
            o_s[t, caps(i), c] = o
            send_os[caps(i), c] = o.astype(WIDE)
        os_swap(i).start()

    def kv_half(side):
        for j in range(2):
            for r in range(3):
                at = pl.ds(r * SIDE, SIDE)
                kv[j, side, at] = dot_nn(img[at], w_pair[j, side]).astype(NARROW)

    for k in W_AFTER_SELF:
        w_first(k)
    w_second(0)
    stage_until(12)
    loads[1].wait()
    kv_half(t)
    w_third(0)
    w_second(1)
    put_transposed(rows[...], t_one)
    stage_until(16)
    loads[2].wait()
    for s in range(4):
        v = pick([f_b[e] for e in range(4)], caption_at[s])
        cot[text(s)] = v
        g_m[text(s)] = v.astype(NARROW)
    w_fourth(0)
    put_transposed(g_m[...], t_b)
    w_last(0)
    for i in range(2):
        os_swap(i).wait_recv()
        at = caps(i)
        o_s[other, at] = land_os[at].astype(NARROW)
        aft_self[at] = tok[at] + (dot_nn(o_s[0, at], w_self[0]) + dot_nn(o_s[1, at], w_self[1]))
        hat, _ = ln_parts(aft_self[at])
        normed_two[at] = (hat * gains[1:2] + biases[1:2]).astype(NARROW)
        q_c[t, at] = dot_nn(normed_two[at], w_query[t]).astype(NARROW)
        for p in range(3):
            c = pair_cols(p)
            o = pair_forward(q_c[t, at, c], kv[0, t, keys(i), c], kv[1, t, keys(i), c], None)
            o_c[t, at, c] = o
            send_oc[at, c] = o.astype(WIDE)
        oc_swap(i).start()
        if i == 0:
            w_third(1)
    for k in W_AFTER_CROSS:
        w_first(k)
    w_fourth(1)
    stage_until(24)
    w_last(1)
    for k in W_AFTER_SELF:
        w_second(k)
    put_transposed(normed_two[...], t_two)
    stage_until(32)
    for k in W_AFTER_SELF:
        w_third(k)

    def cols(i):
        return pl.ds(i * SIDE, SIDE)

    for i in range(2):
        oc_swap(i).wait_recv()
        at = caps(i)
        o_c[other, at] = land_oc[at].astype(NARROW)
        aft_cross[at] = aft_self[at] + (dot_nn(o_c[0, at], w_cross[0]) + dot_nn(o_c[1, at], w_cross[1]))
        hat, _ = ln_parts(aft_cross[at])
        rows[at] = (hat * gains[2:3] + biases[2:3]).astype(NARROW)
        for n in range(4):
            v = dot_nn(rows[at], w_inner[:, cols(n)])
            th = jnp.tanh(GELU_A * (v + GELU_B * (v * v * v)))
            hidden[at, cols(n)] = (0.5 * v * (1.0 + th)).astype(NARROW)
            slope = 0.5 * (1.0 + th) + 0.5 * v * (1.0 - th * th) * (GELU_A * (1.0 + 3.0 * GELU_B * (v * v)))
            if i == 1:
                sc_send(n, left_of(t_b), lambda: hidden[:, cols(n)])
            g_pre[at, cols(n)] = (slope * dot_nt(g_m[at], w_outer[cols(n)])).astype(NARROW)
            if i == 1 and n:
                sc_keep(n - 1, left_of(t_b), lambda: hidden[:, cols(n - 1)])

    send_n[...] = dot_nt(g_pre[...], w_inner[...])
    swap(4, send_n, land_n3).start()
    sc_keep(3, left_of(t_b), lambda: hidden[:, cols(3)])
    put_transposed(rows[...], t_a)
    for i in range(4):
        sc_send(4 + i, left_of(t_a), lambda: g_pre[:, cols(i)])
        if i:
            sc_keep(3 + i, left_of(t_a), lambda: g_pre[:, cols(i - 1)])
    sc_keep(7, left_of(t_a), lambda: g_pre[:, cols(3)])
    send_m[...] = dot_nn(hidden[...], w_outer[...])
    for k in W_AFTER_CROSS:
        w_second(k)
    for k in W_AFTER_CROSS:
        w_third(k)
    tick()
    for k in (2, 3):
        w_fourth(k)
    tick()
    for k in (2, 3):
        w_last(k)
    q_c[other] = dot_nn(normed_two[...], w_query[other]).astype(NARROW)
    kv_half(other)
    for r in range(3):
        vt = img[pl.ds(r * SIDE, SIDE)].T
        for zz in range(4):
            for xx in range(2):
                for cc in range(2):
                    block = (zz * 2 + xx) * 2 + cc
                    w_inner[pl.ds(cc * SIDE + xx * (SIDE // 2) + zz * ROWS_OUT, ROWS_OUT), cols(r)] = vt[block * ROWS_OUT : (block + 1) * ROWS_OUT]
    tick()
    swap(4, send_n, land_n3).wait()
    swap(5, send_m, land_m).start()

    def norm_back(n, value, grad_of, into_rows):
        gain_sum, bias_sum = jnp.zeros((1, 768), WIDE), jnp.zeros((1, 768), WIDE)
        for s in range(4):
            dx, gs, bs = ln_back(value[text(s)], gains[n : n + 1], grad_of(s))
            res = cot[text(s)] + dx
            cot[text(s)] = res
            if into_rows is not None:
                into_rows[text(s)] = res.astype(NARROW)
            gain_sum, bias_sum = gain_sum + gs, bias_sum + bs
        sums[n : n + 1] = gain_sum
        sums[3 + n : 4 + n] = bias_sum

    sums[...] = jnp.zeros_like(sums)
    norm_back(2, aft_cross, lambda s: send_n[text(s)] + land_n3[text(s)], rows)
    put_transposed(rows[...], t_a)
    sc_send(8, left_of(t_a), lambda: o_c[t])
    for h in range(2):
        d_oc[h] = dot_nt(rows[...], w_cross[h]).astype(NARROW)
    sc_keep(8, left_of(t_a), lambda: o_c[t])
    tick()

    for h in range(2):
        for p in range(3):
            for i in range(2):
                c = pair_cols(p)
                dq, dk, dv = pair_backward(q_c[h, caps(i), c], kv[0, h, keys(i), c], kv[1, h, keys(i), c], d_oc[h, caps(i), c], None)
                q_c[h, caps(i), c] = dq
                kv[0, h, keys(i), c] = dk
                kv[1, h, keys(i), c] = dv
        tick()
    f_a[...] = (dot_nt(q_c[0], w_query[0]) + dot_nt(q_c[1], w_query[1])).reshape(f_a.shape)
    sc_send(9, left_of(t_two), lambda: q_c[t])
    norm_back(1, aft_self, lambda s: f_a[s], rows)
    sc_keep(9, left_of(t_two), lambda: q_c[t])
    for j in range(2):
        sc_send(10 + j, lambda side: w_inner[core_rows(side), pl.ds(0, 1152)], lambda: kv[j, t])
    for j in range(2):
        sc_keep(10 + j, lambda side: w_inner[core_rows(side), pl.ds(0, 1152)], lambda: kv[j, t])
    tick()
    put_transposed(rows[...], t_a)
    sc_send(12, left_of(t_a), lambda: o_s[t])
    d_oc[0] = dot_nt(rows[...], w_self[t]).astype(NARROW)
    sc_keep(12, left_of(t_a), lambda: o_s[t])
    for i in range(2):
        for p in range(3):
            c = pair_cols(p)
            at = caps(i)
            dq, dk, dv = pair_backward(qkv[0, at, c], qkv[1, at, c], qkv[2, at, c], d_oc[0, at, c], causal)
            qkv[0, at, c] = dq
            qkv[1, at, c] = dk
            qkv[2, at, c] = dv
    send_n[...] = (dot_nt(qkv[0], w_qkv[0]) + dot_nt(qkv[1], w_qkv[1])) + dot_nt(qkv[2], w_qkv[2])
    swap(6, send_n, land_n1).start()
    tick()
    for j in range(3):
        sc_send(13 + j, left_of(t_one), lambda: qkv[j])
    for j in range(3):
        sc_keep(13 + j, left_of(t_one), lambda: qkv[j])
    tick()

    for k in range(4):
        w_drain(k)

    def image_out(n):
        r, c = n // 2, n % 2
        return pltpu.make_async_copy(
            land_c.at[r, pl.ds(c * SIDE, SIDE)], o_images.at[pl.ds(r * SIDE, SIDE), cols(c)], out_sem.at[N_BLOCKS + 1 + n])

    for r in range(3):
        for c in range(2):
            at = pl.ds(r * SIDE, SIDE)
            total = None
            for j in range(2):
                for h in range(2):
                    term = dot_nt(kv[j, h, at], w_pair[j, h, cols(c)])
                    total = term if total is None else total + term
            land_c[r, pl.ds(c * SIDE, SIDE)] = total
            image_out(2 * r + c).start()
        tick()
    swap(5, send_m, land_m).wait()

    for s in range(4):
        send_m[text(s)] = aft_cross[text(s)] + (send_m[text(s)] + land_m[text(s)])
    for c in range(4):
        f_b[c] = pick([send_m[text(e)] for e in range(4)], slot_of[c])
    mixed_out = pltpu.make_async_copy(f_b, o_mixed, in_sem.at[0])
    mixed_out.start()
    tick()
    swap(6, send_n, land_n1).wait()
    norm_back(0, tok, lambda s: send_n[text(s)] + land_n1[text(s)], None)
    put_transposed(jnp.concatenate([sums[...], jnp.zeros((120, 768), WIDE)], 0), small)
    sc_core(N_BLOCKS).start()
    for c in range(4):
        f_a[c] = pick([cot[text(e)] for e in range(4)], slot_of[c])
    tokens_out = pltpu.make_async_copy(f_a, o_tokens, in_sem.at[1])
    tokens_out.start()
    sc_core(N_BLOCKS).wait_recv()
    small_core[...] = small_core[...] + small[core_rows(core)]
    sc_kept(N_BLOCKS)
    tick(N_BLOCKS + 1 + LAGS[2] - ticked[0])

    for i in range(2):
        os_swap(i).wait_send()
        oc_swap(i).wait_send()
    for i in range(N_BLOCKS + 1):
        if i >= N_BLOCKS - slots:
            sc_core(i).wait_send()
        sc_x(i).wait_send()
        z_drain(i)
        sc_out(i).wait()
    for n in range(6):
        image_out(n).wait()
    mixed_out.wait()
    tokens_out.wait()


def finish_kernel(*refs):
    ins, outs, held, turned, (get, put) = refs[:11], refs[11:23], refs[23:34], refs[34:36], refs[36:38]
    pieces = [(0, slice(0, 2)), (0, slice(2, 4)), (1, slice(0, 2)), (1, slice(2, 4))]
    pieces += [(2, pl.ds(r * 192, 192)) for r in range(6)] + [(k, slice(None)) for k in range(3, 11)]
    loads = [pltpu.make_async_copy(ins[k].at[at], held[k].at[at], get.at[n]) for n, (k, at) in enumerate(pieces)]
    puts = [pltpu.make_async_copy(held[k].at[at], outs[k].at[at], put.at[n]) for n, (k, at) in enumerate(pieces[:-1])]
    for c in loads:
        c.start()
    loads[-1].wait()
    small = held[10][...].T
    for h in range(2):
        turned[h][...] = small[3 * h : 3 * h + 3]
        puts.append(pltpu.make_async_copy(turned[h], outs[10 + h], put.at[len(pieces) - 1 + h]))
        puts[-1].start()
    for n in range(len(pieces) - 1):
        loads[n].wait()
        puts[n].start()
    for c in puts:
        c.wait()


def fast_layer(
    tokens, images, caption_image, self_qkv, self_out, cross_q, cross_kv, cross_out, mlp_in, mlp_out, ln_gains, ln_biases, cotangent
):
    f32, bf16, dma = WIDE, NARROW, pltpu.SemaphoreType.DMA
    out = lambda *shape: jax.ShapeDtypeStruct(shape, f32)
    vmem = lambda kind, *shape: pltpu.VMEM(shape, kind)
    n, late = N_BLOCKS, len(Z_FIRST)
    anywhere, local = pl.BlockSpec(memory_space=pl.ANY), pl.BlockSpec(memory_space=pltpu.VMEM)
    results = pl.pallas_call(
        layer_kernel,
        out_shape=[
            out(4, 64, 768), out(4, 64, 768), out(1152, 768), out(3, 48, 384), out(48, 384), out(48, 384), out(2, 48, 384),
            out(48, 384), out(48, 1536), out(48, 1536), out(48, 128),
        ],
        in_specs=[anywhere, anywhere, pl.BlockSpec(memory_space=pltpu.SMEM)] + [anywhere] * 7 + [local, local, anywhere],
        out_specs=[anywhere] * 11,
        scratch_shapes=[
            vmem(f32, 4, 384, 384), vmem(f32, n, 384, 384), vmem(f32, n - late, 192, 384), vmem(f32, n - late, 192, 384),
            vmem(f32, late, 2, 192, 384), vmem(f32, late, 48, 384),
            vmem(f32, 768, 128), vmem(f32, 384, 128), vmem(f32, 192, 128), vmem(f32, 192, 128),
            vmem(bf16, 3, 768, 384), vmem(bf16, 2, 384, 768), vmem(bf16, 2, 768, 384), vmem(bf16, 2, 2, 768, 384),
            vmem(bf16, 2, 384, 768), vmem(bf16, 768, 1536), vmem(bf16, 1536, 768), vmem(f32, 2, 384, 768), vmem(f32, 3, 768, 384),
            vmem(f32, 4, 64, 768), vmem(f32, 4, 64, 768), vmem(f32, 256, 768), vmem(f32, 256, 768), vmem(f32, 256, 768), vmem(f32, 256, 768),
            vmem(bf16, 256, 768), vmem(bf16, 256, 768), vmem(bf16, 768, 256), vmem(bf16, 768, 256), vmem(bf16, 768, 256), vmem(bf16, 768, 256),
            vmem(bf16, 3, 256, 384), vmem(bf16, 2, 256, 384), vmem(bf16, 2, 256, 384), vmem(bf16, 2, 256, 384), vmem(bf16, 2, 256, 384),
            vmem(bf16, 2, 2, 1152, 384), vmem(bf16, 1152, 768),
            vmem(f32, 256, 384), vmem(f32, 256, 384), vmem(f32, 256, 384), vmem(f32, 256, 384), vmem(bf16, 256, 1536), vmem(bf16, 256, 1536), vmem(bf16, 256, 768),
            vmem(f32, 256, 768), vmem(f32, 256, 768), vmem(f32, 256, 768), vmem(f32, 256, 768), vmem(f32, 256, 768), vmem(f32, 8, 768),
            dma((3,)), dma((4,)), dma((n + 7,)), dma((4, 9)), dma((4, 9)), dma((7,)), dma((7,)),
            dma((n + 1,)), dma((n + 1,)), dma((n + 1,)), dma((n + 1,)), dma((n + 1, 3, 2)), dma((n + 1, 3, 2)),
        ],
        compiler_params=pltpu.CompilerParams(collective_id=0, has_side_effects=True, vmem_limit_bytes=VMEM_BYTES),
        cost_estimate=pl.CostEstimate(flops=15_000_000_000, bytes_accessed=32_000_000, transcendentals=8_000_000),
        name="layer",
    )(
        tokens.reshape(4, 64, 768), images.reshape(1152, 768), caption_image, self_qkv, self_out, cross_q, cross_kv, cross_out,
        mlp_in, mlp_out, ln_gains, ln_biases, cotangent.reshape(4, 64, 768),
    )
    shapes = [tuple(r.shape) for r in results]
    mixed, grad_tokens, grad_images, qkv, own_out, query, pair, cross, inner, outer, by_gain, by_bias = pl.pallas_call(
        finish_kernel,
        out_shape=[out(*s) for s in shapes[:-1]] + [out(3, 48), out(3, 48)],
        in_specs=[anywhere] * 11,
        out_specs=[anywhere] * 12,
        scratch_shapes=[vmem(f32, *s) for s in shapes] + [vmem(f32, 3, 48), vmem(f32, 3, 48), dma((18,)), dma((19,))],
        compiler_params=pltpu.CompilerParams(vmem_limit_bytes=VMEM_BYTES),
        name="finish",
    )(*results)
    return (
        mixed.reshape(256, 768), grad_tokens.reshape(256, 768), grad_images.reshape(2, 576, 768),
        qkv, own_out.T, query, pair, cross.T, inner, outer.T, by_gain, by_bias,
    )


def layer_norm(value, gain, bias):
    center = value - jnp.mean(value, -1, keepdims=True)
    spread = jnp.mean(center * center, -1, keepdims=True)
    return center * lax.rsqrt(spread + EPS) * gain + bias


def matmul(left, right):
    return jnp.dot(left, right, preferred_element_type=WIDE)


def left_product(left, right):
    return lax.dot_general(left, right, (((0,), (0,)), ((), ())), preferred_element_type=WIDE)


def right_product(left, right):
    return lax.dot_general(left, right, (((1,), (1,)), ((), ())), preferred_element_type=WIDE)


def split_heads(value, count, heads):
    return value.reshape(count, -1, heads, HEAD_DIM)


def masked_scores(queries, keys, mask, scale):
    scores = jnp.einsum("cqhe,ckhe->chqk", queries, keys, preferred_element_type=WIDE) * scale
    if mask is not None:
        scores = jnp.where(mask, scores, MASKED)
    return scores


def attend(queries, keys, values, mask, scale):
    scores = masked_scores(queries, keys, mask, scale)
    top = jnp.max(scores, -1, keepdims=True)
    expo = jnp.exp(scores - top)
    total = jnp.sum(expo, -1, keepdims=True)
    weights = (expo / total).astype(NARROW)
    outcome = jnp.einsum("chqk,ckhe->cqhe", weights, values, preferred_element_type=WIDE)
    return (outcome, top + jnp.log(total))


def attend_back(queries, keys, values, mask, scale, logsum, grad_out):
    scores = masked_scores(queries, keys, mask, scale)
    weights = jnp.exp(scores - logsum)
    grad_weights = jnp.einsum("cqhe,ckhe->chqk", grad_out, values, preferred_element_type=WIDE)
    inner = jnp.sum(weights * grad_weights, -1, keepdims=True)
    grad_scores = (weights * (grad_weights - inner)).astype(NARROW)
    grad_queries = (
        jnp.einsum("chqk,ckhe->cqhe", grad_scores, keys, preferred_element_type=WIDE) * scale
    )
    grad_keys = (
        jnp.einsum("chqk,cqhe->ckhe", grad_scores, queries, preferred_element_type=WIDE) * scale
    )
    grad_values = jnp.einsum(
        "chqk,cqhe->ckhe", weights.astype(NARROW), grad_out, preferred_element_type=WIDE
    )
    return (grad_queries, grad_keys, grad_values)


def on_device(
    tokens,
    images,
    caption_image,
    self_qkv,
    self_out,
    cross_q,
    cross_kv,
    cross_out,
    mlp_in,
    mlp_out,
    ln_gains,
    ln_biases,
    cotangent,
):
    rows = tokens.shape[0]
    captions = rows // CAP_LEN
    pairs = images.shape[0]
    local_width = self_out.shape[0]
    heads = local_width // HEAD_DIM
    scale = HEAD_DIM ** (-0.5)
    causal = lax.broadcasted_iota(jnp.int32, (CAP_LEN, CAP_LEN), 0) >= lax.broadcasted_iota(
        jnp.int32, (CAP_LEN, CAP_LEN), 1
    )
    w_qkv = self_qkv.astype(NARROW)
    w_self = self_out.astype(NARROW)
    w_query = cross_q.astype(NARROW)
    w_pair = cross_kv.astype(NARROW)
    w_cross = cross_out.astype(NARROW)
    w_inner = mlp_in.astype(NARROW)
    w_outer = mlp_out.astype(NARROW)
    normed_one = layer_norm(tokens, ln_gains[0], ln_biases[0]).astype(NARROW)
    projected = jnp.einsum("td,sde->ste", normed_one, w_qkv, preferred_element_type=WIDE).astype(
        NARROW
    )
    self_queries = split_heads(projected[0], captions, heads)
    self_keys = split_heads(projected[1], captions, heads)
    self_values = split_heads(projected[2], captions, heads)
    mixed_self, self_logsum = attend(self_queries, self_keys, self_values, causal, scale)
    joined_self = mixed_self.reshape(rows, local_width).astype(NARROW)
    after_self = tokens + lax.psum(matmul(joined_self, w_self), "tensor")
    normed_two = layer_norm(after_self, ln_gains[1], ln_biases[1]).astype(NARROW)
    cross_queries = split_heads(matmul(normed_two, w_query).astype(NARROW), captions, heads)
    image_kv = jnp.einsum("pnd,sde->spne", images, w_pair, preferred_element_type=WIDE).astype(
        NARROW
    )
    local_ids = caption_image - lax.axis_index("batch") * pairs
    picked = jnp.take(image_kv, local_ids, axis=1)
    cross_keys = split_heads(picked[0], captions, heads)
    cross_values = split_heads(picked[1], captions, heads)
    mixed_cross, cross_logsum = attend(cross_queries, cross_keys, cross_values, None, scale)
    joined_cross = mixed_cross.reshape(rows, local_width).astype(NARROW)
    after_cross = after_self + lax.psum(matmul(joined_cross, w_cross), "tensor")
    normed_three = layer_norm(after_cross, ln_gains[2], ln_biases[2]).astype(NARROW)
    hidden_pre = matmul(normed_three, w_inner)
    hidden = jax.nn.gelu(hidden_pre).astype(NARROW)
    mixed = after_cross + lax.psum(matmul(hidden, w_outer), "tensor")
    grad_branch = cotangent.astype(NARROW)
    grad_mlp_out = left_product(hidden, grad_branch)
    grad_hidden = right_product(grad_branch, w_outer)
    gelu_back = jax.vjp(jax.nn.gelu, hidden_pre)[1]
    grad_pre = gelu_back(grad_hidden)[0].astype(NARROW)
    grad_mlp_in = left_product(normed_three, grad_pre)
    grad_normed_three = lax.psum(right_product(grad_pre, w_inner), "tensor")
    norm_three_back = jax.vjp(layer_norm, after_cross, ln_gains[2], ln_biases[2])[1]
    input_three, gain_three, bias_three = norm_three_back(grad_normed_three)
    grad_after_cross = cotangent + input_three
    grad_cross_branch = grad_after_cross.astype(NARROW)
    grad_cross_out = left_product(joined_cross, grad_cross_branch)
    grad_mixed_cross = split_heads(
        right_product(grad_cross_branch, w_cross).astype(NARROW), captions, heads
    )
    grad_cq, grad_ck, grad_cv = attend_back(
        cross_queries, cross_keys, cross_values, None, scale, cross_logsum, grad_mixed_cross
    )
    grad_query_rows = grad_cq.reshape(rows, local_width).astype(NARROW)
    grad_cross_q = left_product(normed_two, grad_query_rows)
    chosen = (local_ids[:, None] == jnp.arange(pairs, dtype=jnp.int32)[None, :]).astype(WIDE)
    caption_grads = jnp.stack([grad_ck, grad_cv]).reshape(2, captions, -1, local_width)
    grad_pair = jnp.einsum(
        "cp,scne->spne", chosen, caption_grads, precision=lax.Precision.HIGHEST
    ).astype(NARROW)
    grad_cross_kv = jnp.einsum("pnd,spne->sde", images, grad_pair, preferred_element_type=WIDE)
    images_part = jnp.einsum("spne,sde->pnd", grad_pair, w_pair, preferred_element_type=WIDE)
    normed_two_part = right_product(grad_query_rows, w_query)
    grad_normed_two, grad_images = lax.psum((normed_two_part, images_part), "tensor")
    norm_two_back = jax.vjp(layer_norm, after_self, ln_gains[1], ln_biases[1])[1]
    input_two, gain_two, bias_two = norm_two_back(grad_normed_two)
    grad_after_self = grad_after_cross + input_two
    grad_self_branch = grad_after_self.astype(NARROW)
    grad_self_out = left_product(joined_self, grad_self_branch)
    grad_mixed_self = split_heads(
        right_product(grad_self_branch, w_self).astype(NARROW), captions, heads
    )
    grad_sq, grad_sk, grad_sv = attend_back(
        self_queries, self_keys, self_values, causal, scale, self_logsum, grad_mixed_self
    )
    grad_projected = (
        jnp.stack([grad_sq, grad_sk, grad_sv]).reshape(3, rows, local_width).astype(NARROW)
    )
    grad_self_qkv = jnp.einsum(
        "td,ste->sde", normed_one, grad_projected, preferred_element_type=WIDE
    )
    normed_one_part = jnp.einsum("ste,sde->td", grad_projected, w_qkv, preferred_element_type=WIDE)
    grad_normed_one = lax.psum(normed_one_part, "tensor")
    norm_one_back = jax.vjp(layer_norm, tokens, ln_gains[0], ln_biases[0])[1]
    input_one, gain_one, bias_one = norm_one_back(grad_normed_one)
    grad_tokens = grad_after_self + input_one
    grad_gains = jnp.stack([gain_one, gain_two, gain_three])
    grad_biases = jnp.stack([bias_one, bias_two, bias_three])
    every_sum = (
        lax.psum_scatter(grad_self_qkv, "batch", scatter_dimension=1, tiled=True),
        lax.psum_scatter(grad_self_out, "batch", scatter_dimension=1, tiled=True),
        lax.psum_scatter(grad_cross_q, "batch", scatter_dimension=0, tiled=True),
        lax.psum_scatter(grad_cross_kv, "batch", scatter_dimension=1, tiled=True),
        lax.psum_scatter(grad_cross_out, "batch", scatter_dimension=1, tiled=True),
        lax.psum_scatter(grad_mlp_in, "batch", scatter_dimension=0, tiled=True),
        lax.psum_scatter(grad_mlp_out, "batch", scatter_dimension=1, tiled=True),
        lax.psum_scatter(grad_gains, "batch", scatter_dimension=1, tiled=True),
        lax.psum_scatter(grad_biases, "batch", scatter_dimension=1, tiled=True),
    )
    (
        summed_qkv,
        summed_self,
        summed_query,
        summed_pair,
        summed_cross,
        summed_inner,
        summed_outer,
        summed_gains,
        summed_biases,
    ) = every_sum
    return (
        mixed,
        grad_tokens,
        grad_images,
        summed_qkv,
        summed_self,
        summed_query,
        summed_pair,
        summed_cross,
        summed_inner,
        summed_outer,
        summed_gains,
        summed_biases,
    )


def solution(mesh):
    in_specs = (
        P("batch", None),
        P("batch", None, None),
        P("batch"),
        P(None, None, "tensor"),
        P("tensor", None),
        P(None, "tensor"),
        P(None, None, "tensor"),
        P("tensor", None),
        P(None, "tensor"),
        P("tensor", None),
        P(),
        P(),
        P("batch", None),
    )
    out_specs = (
        P("batch", None),
        P("batch", None),
        P("batch", None, None),
        P(None, "batch", "tensor"),
        P("tensor", "batch"),
        P("batch", "tensor"),
        P(None, "batch", "tensor"),
        P("tensor", "batch"),
        P("batch", "tensor"),
        P("tensor", "batch"),
        P(None, "batch"),
        P(None, "batch"),
    )
    fast = mesh.shape["batch"] == 16 and mesh.shape["tensor"] == 2
    return jax.shard_map(
        fast_layer if fast else on_device, mesh=mesh, in_specs=in_specs, out_specs=out_specs, check_vma=False
    )
```

```python
import functools

import jax
import jax.numpy as jnp
from jax import lax
from jax.experimental import pallas as pl
from jax.experimental.pallas import tpu as pltpu
from jax.sharding import PartitionSpec as P

HEAD_DIM = 64
CAP_LEN = 64


EPS = 1e-05
MASKED = -1e30
NARROW = jnp.bfloat16
WIDE = jnp.float32


MESH = pl.DeviceIdType.MESH
SIDE = 384
ROWS_OUT = 48
SCALE = HEAD_DIM ** (-0.5)
GELU_A = 0.7978845608028654
GELU_B = 0.044715
N_BLOCKS = 16
VMEM_BYTES = 64 * 2**20
Z_FIRST = (1, 7, 13)
X_DEPTH = 3
LAGS = (0, 3, 6)
W_AFTER_SELF, W_AFTER_CROSS = [3, 2], []


def dot_nn(a, b):
    return lax.dot_general(a, b, (((1,), (0,)), ((), ())), preferred_element_type=WIDE)


def dot_nt(a, b):
    return lax.dot_general(a, b, (((1,), (1,)), ((), ())), preferred_element_type=WIDE)


def dot_tn(a, b):
    return lax.dot_general(a, b, (((0,), (0,)), ((), ())), preferred_element_type=WIDE)


def ln_parts(v):
    center = v - jnp.mean(v, -1, keepdims=True)
    spread = jnp.mean(center * center, -1, keepdims=True)
    r = lax.rsqrt(spread + EPS)
    return center * r, r


def ln_back(v, gain, grad):
    hat, r = ln_parts(v)
    e = grad * gain
    inner = jnp.mean(e * hat, -1, keepdims=True)
    dx = r * (e - jnp.mean(e, -1, keepdims=True) - hat * inner)
    return dx, jnp.sum(grad * hat, 0, keepdims=True), jnp.sum(grad, 0, keepdims=True)


def two_heads(v):
    lane = lax.broadcasted_iota(jnp.int32, v.shape, 1)
    zero = jnp.zeros_like(v)
    return jnp.concatenate([jnp.where(lane < HEAD_DIM, v, zero), jnp.where(lane >= HEAD_DIM, v, zero)], 0)


def one_pair(v):
    n = v.shape[0] // 2
    lane = lax.broadcasted_iota(jnp.int32, (n, v.shape[1]), 1)
    return jnp.where(lane < HEAD_DIM, v[:n], v[n:])


def weights_of(k, q2, mask):
    s = dot_nt(k, q2) * SCALE
    if mask is not None:
        s = jnp.where(mask, s, MASKED)
    e = jnp.exp(s - jnp.max(s, 0, keepdims=True))
    return e * (1.0 / jnp.sum(e, 0, keepdims=True))


def pair_forward(q, k, v, mask):
    p = weights_of(k, two_heads(q), mask)
    return one_pair(dot_tn(p.astype(NARROW), v)).astype(NARROW)


def pair_backward(q, k, v, do, mask):
    q2, do2 = two_heads(q), two_heads(do)
    p = weights_of(k, q2, mask)
    dp = dot_nt(v, do2)
    ds = (p * (dp - jnp.sum(p * dp, 0, keepdims=True))).astype(NARROW)
    dq = one_pair(dot_tn(ds, k)) * SCALE
    dk = dot_nn(ds, q2) * SCALE
    dv = dot_nn(p.astype(NARROW), do2)
    return dq.astype(NARROW), dk.astype(NARROW), dv.astype(NARROW)


def layer_kernel(
    tokens, images, caption_image, self_qkv, self_out, cross_q, cross_kv, cross_out, mlp_in, mlp_out, gains, biases, cotangent,
    o_mixed, o_tokens, o_images, o_qkv, o_self, o_query, o_pair, o_cross, o_inner, o_outer, o_small,
    stage, from_core, from_x, from_z, late_z, late_x, small, small_core, small_x, small_z,
    w_qkv, w_self, w_query, w_pair, w_cross, w_inner, w_outer, land_r, land_c,
    f_a, f_b, tok, cot, aft_self, aft_cross,
    rows, normed_two, t_one, t_two, t_a, t_b,
    qkv, o_s, q_c, o_c, d_oc, kv, img,
    send_os, send_oc, land_os, land_oc, hidden, g_pre, g_m,
    send_n, land_n3, send_m, land_m, land_n1, sums,
    in_sem, stage_sem, out_sem, ws, wr, ex_s, ex_r, s1, r1, s2, r2, s3, r3,
):
    b, t = lax.axis_index("batch"), lax.axis_index("tensor")
    core, x, z = b % 2, (b // 2) % 2, b // 4
    zl = z % 2
    core_peer = b + 1 - 2 * core
    x_peer = b + 2 - 4 * x
    zn_peer = b + 4 - 8 * zl
    z_near, z_far, z_across = z + 1 - 2 * zl, (z + 2) % 4, 3 - z
    z_of = (z_near, z_far, z_across)
    z_peers = [at * 4 + b % 4 for at in z_of]
    at_end = (z == 0) | (z == 3)
    inside = (z == 1) | (z == 2)
    other = 1 - t

    def remote(src, dst, send, recv, peer, side=None):
        return pltpu.make_async_remote_copy(
            src, dst, send, recv, device_id=(peer, t if side is None else side), device_id_type=MESH)

    loads = [
        pltpu.make_async_copy(tokens, f_a, in_sem.at[0]),
        pltpu.make_async_copy(images, img, in_sem.at[1]),
        pltpu.make_async_copy(cotangent, f_b, in_sem.at[2]),
    ]
    jobs = []
    for j in range(3):
        for r in range(2):
            jobs.append((self_qkv.at[j, pl.ds(r * SIDE, SIDE)], w_qkv, (j, pl.ds(r * SIDE, SIDE))))
    for c in range(2):
        jobs.append((self_out.at[:, pl.ds(c * SIDE, SIDE)], w_self, (t, slice(None), pl.ds(c * SIDE, SIDE))))
    for j in range(2):
        for r in range(2):
            jobs.append((cross_kv.at[j, pl.ds(r * SIDE, SIDE)], w_pair, (j, t, pl.ds(r * SIDE, SIDE))))
    for r in range(2):
        jobs.append((cross_q.at[pl.ds(r * SIDE, SIDE)], w_query, (t, pl.ds(r * SIDE, SIDE))))
    for c in range(2):
        jobs.append((cross_out.at[:, pl.ds(c * SIDE, SIDE)], w_cross, (t, slice(None), pl.ds(c * SIDE, SIDE))))
    for c in range(4):
        for r in range(2):
            jobs.append((mlp_in.at[pl.ds(r * SIDE, SIDE), pl.ds(c * SIDE, SIDE)], w_inner, (pl.ds(r * SIDE, SIDE), pl.ds(c * SIDE, SIDE))))
    for r in range(4):
        for c in range(2):
            jobs.append((mlp_out.at[pl.ds(r * SIDE, SIDE), pl.ds(c * SIDE, SIDE)], w_outer, (pl.ds(r * SIDE, SIDE), pl.ds(c * SIDE, SIDE))))
    slots = stage.shape[0]
    staged = [0]

    def stage_copy(n):
        return pltpu.make_async_copy(jobs[n][0], stage.at[n % slots], stage_sem.at[n % slots])

    def stage_until(n):
        while staged[0] < n:
            k = staged[0]
            stage_copy(k).wait()
            jobs[k][1][jobs[k][2]] = stage[k % slots].astype(NARROW)
            if k + slots < len(jobs):
                stage_copy(k + slots).start()
            staged[0] += 1

    loads[0].start()
    for n in range(slots):
        stage_copy(n).start()
    loads[1].start()
    loads[2].start()

    barrier = pltpu.get_barrier_semaphore()
    for peer in (core_peer, x_peer, *z_peers):
        pl.semaphore_signal(barrier, 1, device_id=(peer, t), device_id_type=MESH)
    pl.semaphore_signal(barrier, 1, device_id=(b, other), device_id_type=MESH)

    piece = zl * 4 + x * 2 + core
    at_x, at_z, at_xz = piece + 2 - 4 * x, piece + 4 - 8 * zl, piece + 6 - 4 * x - 8 * zl
    exchange_from = [self_out, cross_out, cross_q]

    def part(k, p, half=None):
        size = ROWS_OUT if k < 2 else 2 * ROWS_OUT
        start = p * size
        if half is not None:
            size = size // 2
            start = start + half * size
        at = pl.ds(pl.multiple_of(start, 8), size)
        return land_r.at[k, at] if k < 2 else land_c.at[0, at] if k == 2 else land_c.at[pl.ds(1, 2), at]

    def over_y(k):
        size = ROWS_OUT if k < 2 else 2 * ROWS_OUT
        at = pl.ds(pl.multiple_of(piece * size, 8), size)
        src = exchange_from[k].at[at] if k < 3 else cross_kv.at[:, at]
        return remote(src, part(k, piece), ws.at[k, 0], wr.at[k, 0], b, other)

    def over_x(k, p):
        return remote(part(k, p), part(k, p), ws.at[k, 1], wr.at[k, 1], x_peer)

    def over_z(k, p):
        return remote(part(k, p), part(k, p), ws.at[k, 2], wr.at[k, 2], zn_peer)

    def half_z(k, p):
        return remote(part(k, p, 0), part(k, p, 0), ws.at[k, 3], wr.at[k, 3], zn_peer)

    def half_x(k, p):
        return remote(part(k, p, 1), part(k, p, 1), ws.at[k, 4], wr.at[k, 4], x_peer)

    def to_core(k, p, n):
        return remote(part(k, p), part(k, p), ws.at[k, 5 + n], wr.at[k, 5 + n], core_peer)

    def w_first(k):
        over_y(k).start()

    def w_second(k):
        over_y(k).wait_recv()
        over_x(k, piece).start()
        over_z(k, piece).start()
        to_core(k, piece, 0).start()

    def w_third(k):
        over_x(k, at_x).wait_recv()
        half_z(k, at_x).start()
        to_core(k, at_x, 1).start()
        over_z(k, at_z).wait_recv()
        half_x(k, at_z).start()
        to_core(k, at_z, 2).start()

    def w_fourth(k):
        half_z(k, at_xz).wait_recv()
        half_x(k, at_xz).wait_recv()
        to_core(k, at_xz, 3).start()

    def w_last(k):
        flip = 1 - 2 * core
        for n, p in enumerate((piece, at_x, at_z, at_xz)):
            to_core(k, p + flip, n).wait_recv()
        if k == 0:
            w_self[other] = land_r[0].astype(NARROW)
        elif k == 1:
            w_cross[other] = land_r[1].astype(NARROW)
        elif k == 2:
            w_query[other] = land_c[0].astype(NARROW)
        else:
            for j in range(2):
                w_pair[j, other] = land_c[1 + j].astype(NARROW)

    def w_drain(k):
        over_y(k).wait_send()
        over_x(k, piece).wait_send()
        over_z(k, piece).wait_send()
        half_z(k, at_x).wait_send()
        half_x(k, at_z).wait_send()
        for n, p in enumerate((piece, at_x, at_z, at_xz)):
            to_core(k, p, n).wait_send()

    def swap(n, src, dst):
        return remote(src, dst, ex_s.at[n], ex_r.at[n], b, other)

    out_of = (
        [o_outer.at[:, pl.ds(i * SIDE, SIDE)] for i in range(4)]
        + [o_inner.at[:, pl.ds(i * SIDE, SIDE)] for i in range(4)]
        + [o_cross, o_query, o_pair.at[0], o_pair.at[1], o_self, o_qkv.at[0], o_qkv.at[1], o_qkv.at[2], o_small]
    )
    x_first = [i for i in range(N_BLOCKS) if i not in Z_FIRST]

    def span(start, size):
        return pl.ds(pl.multiple_of(start, ROWS_OUT), size)

    def core_rows(side):
        return span(side * SIDE, SIDE)

    def x_rows(side):
        return span(side * (SIDE // 2), SIDE // 2)

    def z_rows(at):
        return span(at * ROWS_OUT, ROWS_OUT)

    def xz_rows(side, at):
        return span(side * (SIDE // 2) + at * ROWS_OUT, ROWS_OUT)

    def core_of(i):
        return (stage.at[i % slots], from_core.at[i]) if i < N_BLOCKS else (small.at[core_rows(1 - core)], small_core)

    def x_of(i):
        return from_x.at[x_first.index(i)] if i < N_BLOCKS else small_x

    def parts_of(i):
        if i in Z_FIRST:
            n = Z_FIRST.index(i)
            return [
                (lambda at, count=1, side=side: from_core.at[i, span(side * (SIDE // 2) + at * ROWS_OUT, ROWS_OUT * count)],
                 lambda slot, count=1, side=side: late_z.at[n, side, span(slot * ROWS_OUT, ROWS_OUT * count)])
                for side in range(2)
            ]
        land = from_z.at[x_first.index(i)] if i < N_BLOCKS else small_z
        return [
            (lambda at, count=1: x_of(i).at[span(at * ROWS_OUT, ROWS_OUT * count)],
             lambda slot, count=1: land.at[span(slot * ROWS_OUT, ROWS_OUT * count)])
        ]

    def sc_core(i):
        src, dst = core_of(i)
        return remote(src, dst, s1.at[i], r1.at[i], core_peer)

    def sc_x(i):
        if i in Z_FIRST:
            return remote(from_core.at[i, xz_rows(1 - x, z)], late_x.at[Z_FIRST.index(i)], s2.at[i], r2.at[i], x_peer)
        return remote(core_of(i)[1].at[x_rows(1 - x)], x_of(i), s2.at[i], r2.at[i], x_peer)

    def z_long(i, part):
        rows_of, land = parts_of(i)[part]
        return remote(rows_of(1 - z // 2, 3), land(0, 3), s3.at[i, 0, part], r3.at[i, 0, part], z_peers[0])

    def z_short(i, part, n):
        rows_of, land = parts_of(i)[part]
        at, slot = ((z_near, 0), (z_far, 1), (z_across, 3))[n]
        return remote(rows_of(at), land(slot), s3.at[i, n, part], r3.at[i, n, part], z_peers[n])

    def sc_out(i):
        src = from_core.at[i, xz_rows(x, z)] if i in Z_FIRST else x_of(i).at[z_rows(z)]
        return pltpu.make_async_copy(src, out_of[i], out_sem.at[i])

    waiting, flying = [], [0]

    def x_push():
        while waiting and flying[0] < X_DEPTH:
            sc_x(waiting.pop(0)).start()
            flying[0] += 1

    def sc_send(i, left, right):
        if i >= slots:
            sc_core(i - slots).wait_send()
        stage[i % slots] = dot_nn(left(1 - core), right())
        sc_core(i).start()

    def sc_kept(i):
        if i in Z_FIRST:
            z_begin(i)
        else:
            waiting.append(i)
            x_push()

    def sc_keep(i, left, right):
        mine = dot_nn(left(core), right())
        sc_core(i).wait_recv()
        from_core[i] = from_core[i] + mine
        sc_kept(i)

    def x_sum(i):
        sc_x(i).wait_recv()
        mine = x_of(i)
        mine[...] = mine[...] + core_of(i)[1][x_rows(x)]
        flying[0] -= 1
        x_push()

    def z_begin(i):
        for part in range(len(parts_of(i))):

            @pl.when(at_end)
            def _():
                z_long(i, part).start()

            @pl.when(inside)
            def _():
                z_short(i, part, 0).start()

    def z_middle(i):
        for part, (rows_of, land) in enumerate(parts_of(i)):

            @pl.when(inside)
            def _():
                z_long(i, part).wait_recv()
                for at, slot in ((z_across, 1), (z_far, 2 - 2 * (z // 2)), (z, 2 * (z // 2))):
                    ref = rows_of(at)
                    ref[...] = ref[...] + land(slot)[...]
                z_short(i, part, 2).start()
                z_short(i, part, 1).start()

    def z_end(i):
        for part, (rows_of, land) in enumerate(parts_of(i)):
            ref = rows_of(z)

            @pl.when(at_end)
            def _():
                z_short(i, part, 0).wait_recv()
                z_short(i, part, 1).wait_recv()
                ref[...] = ref[...] + (land(0)[...] + land(1)[...])

            @pl.when(inside)
            def _():
                z_short(i, part, 2).wait_recv()
                ref[...] = ref[...] + land(3)[...]

    def z_drain(i):
        for part in range(len(parts_of(i))):

            @pl.when(at_end)
            def _():
                z_long(i, part).wait_send()

            @pl.when(inside)
            def _():
                for n in range(3):
                    z_short(i, part, n).wait_send()

    def step(i, n):
        if i in Z_FIRST:
            if n == 0:
                z_middle(i)
            elif n == 1:
                z_end(i)
                sc_x(i).start()
            else:
                sc_x(i).wait_recv()
                ref = from_core.at[i, xz_rows(x, z)]
                ref[...] = ref[...] + late_x[Z_FIRST.index(i)]
                sc_out(i).start()
        elif n == 0:
            x_sum(i)
            z_begin(i)
        elif n == 1:
            z_middle(i)
        else:
            z_end(i)
            sc_out(i).start()

    ticked = [0]

    def tick(n=1):
        for _ in range(n):
            for n in (2, 1, 0):
                if 0 <= ticked[0] - LAGS[n] <= N_BLOCKS:
                    step(ticked[0] - LAGS[n], n)
            ticked[0] += 1

    def put_transposed(value, ref):
        vt = value.T
        for zz in range(4):
            for xx in range(2):
                for cc in range(2):
                    block = (zz * 2 + xx) * 2 + cc
                    ref[pl.ds(cc * SIDE + xx * (SIDE // 2) + zz * ROWS_OUT, ROWS_OUT)] = vt[block * ROWS_OUT : (block + 1) * ROWS_OUT]

    def left_of(ref):
        return lambda side: ref[core_rows(side)]

    ids = [caption_image[c] - 2 * b for c in range(4)]
    def pick(options, at):
        value = options[3]
        for e in (2, 1, 0):
            value = jnp.where(at == e, options[e], value)
        return value

    slot_of = [ids[c] * 2 + sum([(ids[e] == ids[c]).astype(jnp.int32) for e in range(c)], jnp.int32(0)) for c in range(4)]
    caption_at = [sum([jnp.where(slot_of[c] == s, c, 0) for c in range(4)], jnp.int32(0)) for s in range(4)]

    def text(s):
        return pl.ds(s * CAP_LEN, CAP_LEN)

    loads[0].wait()
    for s in range(4):
        v = pick([f_a[e] for e in range(4)], caption_at[s])
        tok[text(s)] = v
        hat, _ = ln_parts(v)
        rows[text(s)] = (hat * gains[0:1] + biases[0:1]).astype(NARROW)
    pl.semaphore_wait(barrier, 6)
    w_first(0)
    for j in range(3):
        stage_until(2 * j + 2)
        qkv[j] = dot_nn(rows[...], w_qkv[j]).astype(NARROW)

    w_first(1)
    key_at = lax.broadcasted_iota(jnp.int32, (128, 256), 0)
    query_at = lax.broadcasted_iota(jnp.int32, (128, 256), 1) % 128
    causal = (key_at <= query_at) & (key_at // CAP_LEN == query_at // CAP_LEN)

    def pair_cols(p):
        return pl.ds(p * 2 * HEAD_DIM, 2 * HEAD_DIM)

    def caps(i):
        return pl.ds(i * 2 * CAP_LEN, 2 * CAP_LEN)

    def keys(i):
        return pl.ds(i * 576, 576)

    def os_swap(i):
        return swap(i, send_os.at[caps(i)], land_os.at[caps(i)])

    def oc_swap(i):
        return swap(2 + i, send_oc.at[caps(i)], land_oc.at[caps(i)])

    for i in range(2):
        for p in range(3):
            c = pair_cols(p)
            o = pair_forward(qkv[0, caps(i), c], qkv[1, caps(i), c], qkv[2, caps(i), c], causal)
            o_s[t, caps(i), c] = o
            send_os[caps(i), c] = o.astype(WIDE)
        os_swap(i).start()

    def kv_half(side):
        for j in range(2):
            for r in range(3):
                at = pl.ds(r * SIDE, SIDE)
                kv[j, side, at] = dot_nn(img[at], w_pair[j, side]).astype(NARROW)

    for k in W_AFTER_SELF:
        w_first(k)
    w_second(0)
    stage_until(12)
    loads[1].wait()
    kv_half(t)
    w_third(0)
    w_second(1)
    put_transposed(rows[...], t_one)
    stage_until(16)
    loads[2].wait()
    for s in range(4):
        v = pick([f_b[e] for e in range(4)], caption_at[s])
        cot[text(s)] = v
        g_m[text(s)] = v.astype(NARROW)
    w_fourth(0)
    put_transposed(g_m[...], t_b)
    w_last(0)
    for i in range(2):
        os_swap(i).wait_recv()
        at = caps(i)
        o_s[other, at] = land_os[at].astype(NARROW)
        aft_self[at] = tok[at] + (dot_nn(o_s[0, at], w_self[0]) + dot_nn(o_s[1, at], w_self[1]))
        hat, _ = ln_parts(aft_self[at])
        normed_two[at] = (hat * gains[1:2] + biases[1:2]).astype(NARROW)
        q_c[t, at] = dot_nn(normed_two[at], w_query[t]).astype(NARROW)
        for p in range(3):
            c = pair_cols(p)
            o = pair_forward(q_c[t, at, c], kv[0, t, keys(i), c], kv[1, t, keys(i), c], None)
            o_c[t, at, c] = o
            send_oc[at, c] = o.astype(WIDE)
        oc_swap(i).start()
        if i == 0:
            w_third(1)
    for k in W_AFTER_CROSS:
        w_first(k)
    w_fourth(1)
    stage_until(24)
    w_last(1)
    for k in W_AFTER_SELF:
        w_second(k)
    put_transposed(normed_two[...], t_two)
    stage_until(32)
    for k in W_AFTER_SELF:
        w_third(k)

    def cols(i):
        return pl.ds(i * SIDE, SIDE)

    for i in range(2):
        oc_swap(i).wait_recv()
        at = caps(i)
        o_c[other, at] = land_oc[at].astype(NARROW)
        aft_cross[at] = aft_self[at] + (dot_nn(o_c[0, at], w_cross[0]) + dot_nn(o_c[1, at], w_cross[1]))
        hat, _ = ln_parts(aft_cross[at])
        rows[at] = (hat * gains[2:3] + biases[2:3]).astype(NARROW)
        for n in range(4):
            v = dot_nn(rows[at], w_inner[:, cols(n)])
            th = jnp.tanh(GELU_A * (v + GELU_B * (v * v * v)))
            hidden[at, cols(n)] = (0.5 * v * (1.0 + th)).astype(NARROW)
            slope = 0.5 * (1.0 + th) + 0.5 * v * (1.0 - th * th) * (GELU_A * (1.0 + 3.0 * GELU_B * (v * v)))
            if i == 1:
                sc_send(n, left_of(t_b), lambda: hidden[:, cols(n)])
            g_pre[at, cols(n)] = (slope * dot_nt(g_m[at], w_outer[cols(n)])).astype(NARROW)
            if i == 1 and n:
                sc_keep(n - 1, left_of(t_b), lambda: hidden[:, cols(n - 1)])

    send_n[...] = dot_nt(g_pre[...], w_inner[...])
    swap(4, send_n, land_n3).start()
    sc_keep(3, left_of(t_b), lambda: hidden[:, cols(3)])
    put_transposed(rows[...], t_a)
    for i in range(4):
        sc_send(4 + i, left_of(t_a), lambda: g_pre[:, cols(i)])
        if i:
            sc_keep(3 + i, left_of(t_a), lambda: g_pre[:, cols(i - 1)])
    sc_keep(7, left_of(t_a), lambda: g_pre[:, cols(3)])
    send_m[...] = dot_nn(hidden[...], w_outer[...])
    for k in W_AFTER_CROSS:
        w_second(k)
    for k in W_AFTER_CROSS:
        w_third(k)
    tick()
    for k in (2, 3):
        w_fourth(k)
    tick()
    for k in (2, 3):
        w_last(k)
    q_c[other] = dot_nn(normed_two[...], w_query[other]).astype(NARROW)
    kv_half(other)
    for r in range(3):
        vt = img[pl.ds(r * SIDE, SIDE)].T
        for zz in range(4):
            for xx in range(2):
                for cc in range(2):
                    block = (zz * 2 + xx) * 2 + cc
                    w_inner[pl.ds(cc * SIDE + xx * (SIDE // 2) + zz * ROWS_OUT, ROWS_OUT), cols(r)] = vt[block * ROWS_OUT : (block + 1) * ROWS_OUT]
    tick()
    swap(4, send_n, land_n3).wait()
    swap(5, send_m, land_m).start()

    def norm_back(n, value, grad_of, into_rows):
        gain_sum, bias_sum = jnp.zeros((1, 768), WIDE), jnp.zeros((1, 768), WIDE)
        for s in range(4):
            dx, gs, bs = ln_back(value[text(s)], gains[n : n + 1], grad_of(s))
            res = cot[text(s)] + dx
            cot[text(s)] = res
            if into_rows is not None:
                into_rows[text(s)] = res.astype(NARROW)
            gain_sum, bias_sum = gain_sum + gs, bias_sum + bs
        sums[n : n + 1] = gain_sum
        sums[3 + n : 4 + n] = bias_sum

    sums[...] = jnp.zeros_like(sums)
    norm_back(2, aft_cross, lambda s: send_n[text(s)] + land_n3[text(s)], rows)
    put_transposed(rows[...], t_a)
    sc_send(8, left_of(t_a), lambda: o_c[t])
    for h in range(2):
        d_oc[h] = dot_nt(rows[...], w_cross[h]).astype(NARROW)
    sc_keep(8, left_of(t_a), lambda: o_c[t])
    tick()

    for h in range(2):
        for p in range(3):
            for i in range(2):
                c = pair_cols(p)
                dq, dk, dv = pair_backward(q_c[h, caps(i), c], kv[0, h, keys(i), c], kv[1, h, keys(i), c], d_oc[h, caps(i), c], None)
                q_c[h, caps(i), c] = dq
                kv[0, h, keys(i), c] = dk
                kv[1, h, keys(i), c] = dv
        tick()
    f_a[...] = (dot_nt(q_c[0], w_query[0]) + dot_nt(q_c[1], w_query[1])).reshape(f_a.shape)
    sc_send(9, left_of(t_two), lambda: q_c[t])
    norm_back(1, aft_self, lambda s: f_a[s], rows)
    sc_keep(9, left_of(t_two), lambda: q_c[t])
    for j in range(2):
        sc_send(10 + j, lambda side: w_inner[core_rows(side), pl.ds(0, 1152)], lambda: kv[j, t])
    for j in range(2):
        sc_keep(10 + j, lambda side: w_inner[core_rows(side), pl.ds(0, 1152)], lambda: kv[j, t])
    tick()
    put_transposed(rows[...], t_a)
    sc_send(12, left_of(t_a), lambda: o_s[t])
    d_oc[0] = dot_nt(rows[...], w_self[t]).astype(NARROW)
    sc_keep(12, left_of(t_a), lambda: o_s[t])
    for i in range(2):
        for p in range(3):
            c = pair_cols(p)
            at = caps(i)
            dq, dk, dv = pair_backward(qkv[0, at, c], qkv[1, at, c], qkv[2, at, c], d_oc[0, at, c], causal)
            qkv[0, at, c] = dq
            qkv[1, at, c] = dk
            qkv[2, at, c] = dv
    send_n[...] = (dot_nt(qkv[0], w_qkv[0]) + dot_nt(qkv[1], w_qkv[1])) + dot_nt(qkv[2], w_qkv[2])
    swap(6, send_n, land_n1).start()
    tick()
    for j in range(3):
        sc_send(13 + j, left_of(t_one), lambda: qkv[j])
    for j in range(3):
        sc_keep(13 + j, left_of(t_one), lambda: qkv[j])
    tick()

    for k in range(4):
        w_drain(k)

    def image_out(n):
        r, c = n // 2, n % 2
        return pltpu.make_async_copy(
            land_c.at[r, pl.ds(c * SIDE, SIDE)], o_images.at[pl.ds(r * SIDE, SIDE), cols(c)], out_sem.at[N_BLOCKS + 1 + n])

    for r in range(3):
        for c in range(2):
            at = pl.ds(r * SIDE, SIDE)
            total = None
            for j in range(2):
                for h in range(2):
                    term = dot_nt(kv[j, h, at], w_pair[j, h, cols(c)])
                    total = term if total is None else total + term
            land_c[r, pl.ds(c * SIDE, SIDE)] = total
            image_out(2 * r + c).start()
        tick()
    swap(5, send_m, land_m).wait()

    for s in range(4):
        send_m[text(s)] = aft_cross[text(s)] + (send_m[text(s)] + land_m[text(s)])
    for c in range(4):
        f_b[c] = pick([send_m[text(e)] for e in range(4)], slot_of[c])
    mixed_out = pltpu.make_async_copy(f_b, o_mixed, in_sem.at[0])
    mixed_out.start()
    tick()
    swap(6, send_n, land_n1).wait()
    norm_back(0, tok, lambda s: send_n[text(s)] + land_n1[text(s)], None)
    put_transposed(jnp.concatenate([sums[...], jnp.zeros((120, 768), WIDE)], 0), small)
    sc_core(N_BLOCKS).start()
    for c in range(4):
        f_a[c] = pick([cot[text(e)] for e in range(4)], slot_of[c])
    tokens_out = pltpu.make_async_copy(f_a, o_tokens, in_sem.at[1])
    tokens_out.start()
    sc_core(N_BLOCKS).wait_recv()
    small_core[...] = small_core[...] + small[core_rows(core)]
    sc_kept(N_BLOCKS)
    tick(N_BLOCKS + 1 + LAGS[2] - ticked[0])

    for i in range(2):
        os_swap(i).wait_send()
        oc_swap(i).wait_send()
    for i in range(N_BLOCKS + 1):
        if i >= N_BLOCKS - slots:
            sc_core(i).wait_send()
        sc_x(i).wait_send()
        z_drain(i)
        sc_out(i).wait()
    for n in range(6):
        image_out(n).wait()
    mixed_out.wait()
    tokens_out.wait()


def finish_kernel(*refs):
    ins, outs, held, turned, (get, put) = refs[:11], refs[11:23], refs[23:34], refs[34:36], refs[36:38]
    pieces = [(0, slice(0, 2)), (0, slice(2, 4)), (1, slice(0, 2)), (1, slice(2, 4))]
    pieces += [(2, pl.ds(r * 192, 192)) for r in range(6)] + [(k, slice(None)) for k in range(3, 11)]
    loads = [pltpu.make_async_copy(ins[k].at[at], held[k].at[at], get.at[n]) for n, (k, at) in enumerate(pieces)]
    puts = [pltpu.make_async_copy(held[k].at[at], outs[k].at[at], put.at[n]) for n, (k, at) in enumerate(pieces[:-1])]
    for c in loads:
        c.start()
    loads[-1].wait()
    small = held[10][...].T
    for h in range(2):
        turned[h][...] = small[3 * h : 3 * h + 3]
        puts.append(pltpu.make_async_copy(turned[h], outs[10 + h], put.at[len(pieces) - 1 + h]))
        puts[-1].start()
    for n in range(len(pieces) - 1):
        loads[n].wait()
        puts[n].start()
    for c in puts:
        c.wait()


def fast_layer(
    tokens, images, caption_image, self_qkv, self_out, cross_q, cross_kv, cross_out, mlp_in, mlp_out, ln_gains, ln_biases, cotangent
):
    f32, bf16, dma = WIDE, NARROW, pltpu.SemaphoreType.DMA
    out = lambda *shape: jax.ShapeDtypeStruct(shape, f32)
    vmem = lambda kind, *shape: pltpu.VMEM(shape, kind)
    n, late = N_BLOCKS, len(Z_FIRST)
    anywhere, local = pl.BlockSpec(memory_space=pl.ANY), pl.BlockSpec(memory_space=pltpu.VMEM)
    results = pl.pallas_call(
        layer_kernel,
        out_shape=[
            out(4, 64, 768), out(4, 64, 768), out(1152, 768), out(3, 48, 384), out(48, 384), out(48, 384), out(2, 48, 384),
            out(48, 384), out(48, 1536), out(48, 1536), out(48, 128),
        ],
        in_specs=[anywhere, anywhere, pl.BlockSpec(memory_space=pltpu.SMEM)] + [anywhere] * 7 + [local, local, anywhere],
        out_specs=[anywhere] * 11,
        scratch_shapes=[
            vmem(f32, 4, 384, 384), vmem(f32, n, 384, 384), vmem(f32, n - late, 192, 384), vmem(f32, n - late, 192, 384),
            vmem(f32, late, 2, 192, 384), vmem(f32, late, 48, 384),
            vmem(f32, 768, 128), vmem(f32, 384, 128), vmem(f32, 192, 128), vmem(f32, 192, 128),
            vmem(bf16, 3, 768, 384), vmem(bf16, 2, 384, 768), vmem(bf16, 2, 768, 384), vmem(bf16, 2, 2, 768, 384),
            vmem(bf16, 2, 384, 768), vmem(bf16, 768, 1536), vmem(bf16, 1536, 768), vmem(f32, 2, 384, 768), vmem(f32, 3, 768, 384),
            vmem(f32, 4, 64, 768), vmem(f32, 4, 64, 768), vmem(f32, 256, 768), vmem(f32, 256, 768), vmem(f32, 256, 768), vmem(f32, 256, 768),
            vmem(bf16, 256, 768), vmem(bf16, 256, 768), vmem(bf16, 768, 256), vmem(bf16, 768, 256), vmem(bf16, 768, 256), vmem(bf16, 768, 256),
            vmem(bf16, 3, 256, 384), vmem(bf16, 2, 256, 384), vmem(bf16, 2, 256, 384), vmem(bf16, 2, 256, 384), vmem(bf16, 2, 256, 384),
            vmem(bf16, 2, 2, 1152, 384), vmem(bf16, 1152, 768),
            vmem(f32, 256, 384), vmem(f32, 256, 384), vmem(f32, 256, 384), vmem(f32, 256, 384), vmem(bf16, 256, 1536), vmem(bf16, 256, 1536), vmem(bf16, 256, 768),
            vmem(f32, 256, 768), vmem(f32, 256, 768), vmem(f32, 256, 768), vmem(f32, 256, 768), vmem(f32, 256, 768), vmem(f32, 8, 768),
            dma((3,)), dma((4,)), dma((n + 7,)), dma((4, 9)), dma((4, 9)), dma((7,)), dma((7,)),
            dma((n + 1,)), dma((n + 1,)), dma((n + 1,)), dma((n + 1,)), dma((n + 1, 3, 2)), dma((n + 1, 3, 2)),
        ],
        compiler_params=pltpu.CompilerParams(collective_id=0, has_side_effects=True, vmem_limit_bytes=VMEM_BYTES),
        cost_estimate=pl.CostEstimate(flops=15_000_000_000, bytes_accessed=32_000_000, transcendentals=8_000_000),
        name="layer",
    )(
        tokens.reshape(4, 64, 768), images.reshape(1152, 768), caption_image, self_qkv, self_out, cross_q, cross_kv, cross_out,
        mlp_in, mlp_out, ln_gains, ln_biases, cotangent.reshape(4, 64, 768),
    )
    shapes = [tuple(r.shape) for r in results]
    mixed, grad_tokens, grad_images, qkv, own_out, query, pair, cross, inner, outer, by_gain, by_bias = pl.pallas_call(
        finish_kernel,
        out_shape=[out(*s) for s in shapes[:-1]] + [out(3, 48), out(3, 48)],
        in_specs=[anywhere] * 11,
        out_specs=[anywhere] * 12,
        scratch_shapes=[vmem(f32, *s) for s in shapes] + [vmem(f32, 3, 48), vmem(f32, 3, 48), dma((18,)), dma((19,))],
        compiler_params=pltpu.CompilerParams(vmem_limit_bytes=VMEM_BYTES),
        name="finish",
    )(*results)
    return (
        mixed.reshape(256, 768), grad_tokens.reshape(256, 768), grad_images.reshape(2, 576, 768),
        qkv, own_out.T, query, pair, cross.T, inner, outer.T, by_gain, by_bias,
    )


def layer_norm(value, gain, bias):
    center = value - jnp.mean(value, -1, keepdims=True)
    spread = jnp.mean(center * center, -1, keepdims=True)
    return center * lax.rsqrt(spread + EPS) * gain + bias


def matmul(left, right):
    return jnp.dot(left, right, preferred_element_type=WIDE)


def left_product(left, right):
    return lax.dot_general(left, right, (((0,), (0,)), ((), ())), preferred_element_type=WIDE)


def right_product(left, right):
    return lax.dot_general(left, right, (((1,), (1,)), ((), ())), preferred_element_type=WIDE)


def split_heads(value, count, heads):
    return value.reshape(count, -1, heads, HEAD_DIM)


def masked_scores(queries, keys, mask, scale):
    scores = jnp.einsum("cqhe,ckhe->chqk", queries, keys, preferred_element_type=WIDE) * scale
    if mask is not None:
        scores = jnp.where(mask, scores, MASKED)
    return scores


def attend(queries, keys, values, mask, scale):
    scores = masked_scores(queries, keys, mask, scale)
    top = jnp.max(scores, -1, keepdims=True)
    expo = jnp.exp(scores - top)
    total = jnp.sum(expo, -1, keepdims=True)
    weights = (expo / total).astype(NARROW)
    outcome = jnp.einsum("chqk,ckhe->cqhe", weights, values, preferred_element_type=WIDE)
    return (outcome, top + jnp.log(total))


def attend_back(queries, keys, values, mask, scale, logsum, grad_out):
    scores = masked_scores(queries, keys, mask, scale)
    weights = jnp.exp(scores - logsum)
    grad_weights = jnp.einsum("cqhe,ckhe->chqk", grad_out, values, preferred_element_type=WIDE)
    inner = jnp.sum(weights * grad_weights, -1, keepdims=True)
    grad_scores = (weights * (grad_weights - inner)).astype(NARROW)
    grad_queries = (
        jnp.einsum("chqk,ckhe->cqhe", grad_scores, keys, preferred_element_type=WIDE) * scale
    )
    grad_keys = (
        jnp.einsum("chqk,cqhe->ckhe", grad_scores, queries, preferred_element_type=WIDE) * scale
    )
    grad_values = jnp.einsum(
        "chqk,cqhe->ckhe", weights.astype(NARROW), grad_out, preferred_element_type=WIDE
    )
    return (grad_queries, grad_keys, grad_values)


def on_device(
    tokens,
    images,
    caption_image,
    self_qkv,
    self_out,
    cross_q,
    cross_kv,
    cross_out,
    mlp_in,
    mlp_out,
    ln_gains,
    ln_biases,
    cotangent,
):
    rows = tokens.shape[0]
    captions = rows // CAP_LEN
    pairs = images.shape[0]
    local_width = self_out.shape[0]
    heads = local_width // HEAD_DIM
    scale = HEAD_DIM ** (-0.5)
    causal = lax.broadcasted_iota(jnp.int32, (CAP_LEN, CAP_LEN), 0) >= lax.broadcasted_iota(
        jnp.int32, (CAP_LEN, CAP_LEN), 1
    )
    w_qkv = self_qkv.astype(NARROW)
    w_self = self_out.astype(NARROW)
    w_query = cross_q.astype(NARROW)
    w_pair = cross_kv.astype(NARROW)
    w_cross = cross_out.astype(NARROW)
    w_inner = mlp_in.astype(NARROW)
    w_outer = mlp_out.astype(NARROW)
    normed_one = layer_norm(tokens, ln_gains[0], ln_biases[0]).astype(NARROW)
    projected = jnp.einsum("td,sde->ste", normed_one, w_qkv, preferred_element_type=WIDE).astype(
        NARROW
    )
    self_queries = split_heads(projected[0], captions, heads)
    self_keys = split_heads(projected[1], captions, heads)
    self_values = split_heads(projected[2], captions, heads)
    mixed_self, self_logsum = attend(self_queries, self_keys, self_values, causal, scale)
    joined_self = mixed_self.reshape(rows, local_width).astype(NARROW)
    after_self = tokens + lax.psum(matmul(joined_self, w_self), "tensor")
    normed_two = layer_norm(after_self, ln_gains[1], ln_biases[1]).astype(NARROW)
    cross_queries = split_heads(matmul(normed_two, w_query).astype(NARROW), captions, heads)
    image_kv = jnp.einsum("pnd,sde->spne", images, w_pair, preferred_element_type=WIDE).astype(
        NARROW
    )
    local_ids = caption_image - lax.axis_index("batch") * pairs
    picked = jnp.take(image_kv, local_ids, axis=1)
    cross_keys = split_heads(picked[0], captions, heads)
    cross_values = split_heads(picked[1], captions, heads)
    mixed_cross, cross_logsum = attend(cross_queries, cross_keys, cross_values, None, scale)
    joined_cross = mixed_cross.reshape(rows, local_width).astype(NARROW)
    after_cross = after_self + lax.psum(matmul(joined_cross, w_cross), "tensor")
    normed_three = layer_norm(after_cross, ln_gains[2], ln_biases[2]).astype(NARROW)
    hidden_pre = matmul(normed_three, w_inner)
    hidden = jax.nn.gelu(hidden_pre).astype(NARROW)
    mixed = after_cross + lax.psum(matmul(hidden, w_outer), "tensor")
    grad_branch = cotangent.astype(NARROW)
    grad_mlp_out = left_product(hidden, grad_branch)
    grad_hidden = right_product(grad_branch, w_outer)
    gelu_back = jax.vjp(jax.nn.gelu, hidden_pre)[1]
    grad_pre = gelu_back(grad_hidden)[0].astype(NARROW)
    grad_mlp_in = left_product(normed_three, grad_pre)
    grad_normed_three = lax.psum(right_product(grad_pre, w_inner), "tensor")
    norm_three_back = jax.vjp(layer_norm, after_cross, ln_gains[2], ln_biases[2])[1]
    input_three, gain_three, bias_three = norm_three_back(grad_normed_three)
    grad_after_cross = cotangent + input_three
    grad_cross_branch = grad_after_cross.astype(NARROW)
    grad_cross_out = left_product(joined_cross, grad_cross_branch)
    grad_mixed_cross = split_heads(
        right_product(grad_cross_branch, w_cross).astype(NARROW), captions, heads
    )
    grad_cq, grad_ck, grad_cv = attend_back(
        cross_queries, cross_keys, cross_values, None, scale, cross_logsum, grad_mixed_cross
    )
    grad_query_rows = grad_cq.reshape(rows, local_width).astype(NARROW)
    grad_cross_q = left_product(normed_two, grad_query_rows)
    chosen = (local_ids[:, None] == jnp.arange(pairs, dtype=jnp.int32)[None, :]).astype(WIDE)
    caption_grads = jnp.stack([grad_ck, grad_cv]).reshape(2, captions, -1, local_width)
    grad_pair = jnp.einsum(
        "cp,scne->spne", chosen, caption_grads, precision=lax.Precision.HIGHEST
    ).astype(NARROW)
    grad_cross_kv = jnp.einsum("pnd,spne->sde", images, grad_pair, preferred_element_type=WIDE)
    images_part = jnp.einsum("spne,sde->pnd", grad_pair, w_pair, preferred_element_type=WIDE)
    normed_two_part = right_product(grad_query_rows, w_query)
    grad_normed_two, grad_images = lax.psum((normed_two_part, images_part), "tensor")
    norm_two_back = jax.vjp(layer_norm, after_self, ln_gains[1], ln_biases[1])[1]
    input_two, gain_two, bias_two = norm_two_back(grad_normed_two)
    grad_after_self = grad_after_cross + input_two
    grad_self_branch = grad_after_self.astype(NARROW)
    grad_self_out = left_product(joined_self, grad_self_branch)
    grad_mixed_self = split_heads(
        right_product(grad_self_branch, w_self).astype(NARROW), captions, heads
    )
    grad_sq, grad_sk, grad_sv = attend_back(
        self_queries, self_keys, self_values, causal, scale, self_logsum, grad_mixed_self
    )
    grad_projected = (
        jnp.stack([grad_sq, grad_sk, grad_sv]).reshape(3, rows, local_width).astype(NARROW)
    )
    grad_self_qkv = jnp.einsum(
        "td,ste->sde", normed_one, grad_projected, preferred_element_type=WIDE
    )
    normed_one_part = jnp.einsum("ste,sde->td", grad_projected, w_qkv, preferred_element_type=WIDE)
    grad_normed_one = lax.psum(normed_one_part, "tensor")
    norm_one_back = jax.vjp(layer_norm, tokens, ln_gains[0], ln_biases[0])[1]
    input_one, gain_one, bias_one = norm_one_back(grad_normed_one)
    grad_tokens = grad_after_self + input_one
    grad_gains = jnp.stack([gain_one, gain_two, gain_three])
    grad_biases = jnp.stack([bias_one, bias_two, bias_three])
    every_sum = (
        lax.psum_scatter(grad_self_qkv, "batch", scatter_dimension=1, tiled=True),
        lax.psum_scatter(grad_self_out, "batch", scatter_dimension=1, tiled=True),
        lax.psum_scatter(grad_cross_q, "batch", scatter_dimension=0, tiled=True),
        lax.psum_scatter(grad_cross_kv, "batch", scatter_dimension=1, tiled=True),
        lax.psum_scatter(grad_cross_out, "batch", scatter_dimension=1, tiled=True),
        lax.psum_scatter(grad_mlp_in, "batch", scatter_dimension=0, tiled=True),
        lax.psum_scatter(grad_mlp_out, "batch", scatter_dimension=1, tiled=True),
        lax.psum_scatter(grad_gains, "batch", scatter_dimension=1, tiled=True),
        lax.psum_scatter(grad_biases, "batch", scatter_dimension=1, tiled=True),
    )
    (
        summed_qkv,
        summed_self,
        summed_query,
        summed_pair,
        summed_cross,
        summed_inner,
        summed_outer,
        summed_gains,
        summed_biases,
    ) = every_sum
    return (
        mixed,
        grad_tokens,
        grad_images,
        summed_qkv,
        summed_self,
        summed_query,
        summed_pair,
        summed_cross,
        summed_inner,
        summed_outer,
        summed_gains,
        summed_biases,
    )


def solution(mesh):
    in_specs = (
        P("batch", None),
        P("batch", None, None),
        P("batch"),
        P(None, None, "tensor"),
        P("tensor", None),
        P(None, "tensor"),
        P(None, None, "tensor"),
        P("tensor", None),
        P(None, "tensor"),
        P("tensor", None),
        P(),
        P(),
        P("batch", None),
    )
    out_specs = (
        P("batch", None),
        P("batch", None),
        P("batch", None, None),
        P(None, "batch", "tensor"),
        P("tensor", "batch"),
        P("batch", "tensor"),
        P(None, "batch", "tensor"),
        P("tensor", "batch"),
        P("batch", "tensor"),
        P("tensor", "batch"),
        P(None, "batch"),
        P(None, "batch"),
    )
    fast = mesh.shape["batch"] == 16 and mesh.shape["tensor"] == 2
    return jax.shard_map(
        fast_layer if fast else on_device, mesh=mesh, in_specs=in_specs, out_specs=out_specs, check_vma=False
    )
```
